32 devices in a mesh: dp: 4 (over y, x), hid: 4 (over z), wid: 2 (over core).
Axes of the slice: x: 2, y: 2, z: 4, core: 2. Of those that a mesh axis runs over, the one named last changes fastest.
Arguments:
- layer_in: bfloat16 [8, 1024, 1536], P('dp', ('hid', 'wid')), may hold values from -6 to 6
- segment_ids: int32 [8, 1024], P('dp', ('hid', 'wid')), may hold values from 0 to 2, never falling along the last dimension, each value on 1 to 768 neighbouring positions
- out_grad: bfloat16 [8, 1024, 1536], P('dp', ('hid', 'wid')), may hold values from -6 to 6
- gain_attn: bfloat16 [1536], P(('dp', 'hid', 'wid')), may hold values from 0.5 to 1.5
- w_query: bfloat16 [1536, 1536], P(('dp', 'hid', 'wid')), may hold values from -0.15625 to 0.15625
- w_key: bfloat16 [1536, 1536], P(('dp', 'hid', 'wid')), may hold values from -0.15625 to 0.15625
- w_value: bfloat16 [1536, 1536], P(('dp', 'hid', 'wid')), may hold values from -0.15625 to 0.15625
- w_dir: bfloat16 [1536, 1536], P(('dp', 'hid', 'wid')), may hold values from -0.15625 to 0.15625
- w_beta: bfloat16 [1536, 12], P(('dp', 'hid', 'wid')), may hold values from -0.3125 to 0.3125
- b_beta: bfloat16 [12], replicated, may hold values from -2 to 2
- w_out: bfloat16 [1536, 1536], P(('dp', 'hid', 'wid')), may hold values from -0.875 to 0.875
- gain_mlp: bfloat16 [1536], P(('dp', 'hid', 'wid')), may hold values from 0.5 to 1.5
- w_gate: bfloat16 [1536, 4096], P(('dp', 'wid'), 'hid'), may hold values from -0.15625 to 0.15625
- w_up: bfloat16 [1536, 4096], P(('dp', 'wid'), 'hid'), may hold values from -0.15625 to 0.15625
- w_down: bfloat16 [4096, 1536], P('hid', ('dp', 'wid')), may hold values from -0.09375 to 0.09375
Outputs:
- layer_out: bfloat16 [8, 1024, 1536], P('dp', ('hid', 'wid'))
- grad_in: bfloat16 [8, 1024, 1536], P('dp', ('hid', 'wid'))
- grad_gain_attn: float32 [1536], P(('dp', 'hid', 'wid'))
- grad_query: float32 [1536, 1536], P(('dp', 'hid', 'wid'))
- grad_key: float32 [1536, 1536], P(('dp', 'hid', 'wid'))
- grad_value: float32 [1536, 1536], P(('dp', 'hid', 'wid'))
- grad_dir: float32 [1536, 1536], P(('dp', 'hid', 'wid'))
- grad_beta: float32 [1536, 12], P(('dp', 'hid', 'wid'))
- grad_bias: float32 [12], replicated
- grad_out_proj: float32 [1536, 1536], P(('dp', 'hid', 'wid'))
- grad_gain_mlp: float32 [1536], P(('dp', 'hid', 'wid'))
- grad_gate: float32 [1536, 4096], P(('dp', 'wid'), 'hid')
- grad_up: float32 [1536, 4096], P(('dp', 'wid'), 'hid')
- grad_down: float32 [4096, 1536], P('hid', ('dp', 'wid'))
The draws below stay inside these ranges and needn't reach their ends.
Inputs may be any that keep to these rules, and one draw needn't show every extreme that they name: `segment_ids`: within a row the document numbers never fall; each document has 1 to 768 tokens and one has exactly 768.
All inputs are finite; a program needn't handle non-finite values.
Results may differ from the reference program's by a relative error of at most 0.017.
Values may be sent and summed in bfloat16 or wider, within the bound.
No kernel may reach another device: no remote copies, remote signals or barrier semaphores. Data moves between devices by JAX's collectives and lax.ppermute only.
A program may use at most 512 MiB of HBM per device.

```python
import math
import jax
import jax.numpy as jnp
import numpy as np
from jax import lax

D = 1536
HEADS = 12
HSIZE = 128
FF = 4096
CH = 128
DOCS = 3
LEN = 1024
ROWS = 8
DOC_MOST = 768


def draw_layer_in(key, part):
    key = jax.random.fold_in(key, 11)
    noise_key, common_key, slope_key = jax.random.split(key, 3)
    position = jnp.arange(LEN, dtype=jnp.float32)[None, :, None] * (2.0 / LEN) - 1.0
    common = jax.random.normal(common_key, (ROWS, 1, D), jnp.float32)
    slope_dir = jax.random.normal(slope_key, (ROWS, 1, D), jnp.float32)
    noise_part = jax.random.normal(noise_key, (ROWS, LEN, D), jnp.float32)
    strength = 0.6
    values = noise_part + strength * common + strength * position * slope_dir
    return jnp.clip(values, -6.0, 6.0).astype(jnp.bfloat16)


def levels(own_key, shape, cuts, low, top_value):
    factor_of = 1.0
    for dim, shards_of in cuts:
        draws = jax.random.uniform(jax.random.fold_in(jax.random.fold_in(own_key, 6), dim), (shards_of,), jnp.float32, low / len(cuts), top_value / len(cuts))
        factor_of = factor_of * jnp.repeat(jnp.exp(draws), shape[dim] // shards_of).reshape((-1,) + (1,) * (len(shape) - 1 - dim))
    return factor_of


def length_profile(number_of, total, most, lean):
    loads = [(1 << 20) // math.isqrt(standing ** lean) + 1 for standing in range(2, number_of + 1)]
    rest, given = total - most - (number_of - 1), [1] * (number_of - 1)
    while rest > 0:
        movable = [i for i in range(number_of - 1) if given[i] < most]
        whole, left = sum([loads[i] for i in movable]), rest
        for i in movable:
            addition = min(most - given[i], max(1, left * loads[i] // whole), rest)
            given[i] = given[i] + addition
            rest = rest - addition
    return np.array([most] + given)


def ragged(key, amount, total, bound, slope):
    if amount == 2:
        one = jax.random.randint(key, (), max(1, total - bound), min(bound, total - 1) + 1)
        return jnp.stack([one, total - one])
    tallies = jnp.asarray(length_profile(amount, total, bound, slope), jnp.int32)
    couples = (amount - 1) // 2
    source_of, taker = tallies[1:1 + 2 * couples:2], tallies[2:2 + 2 * couples:2]
    room = jnp.minimum(source_of - 1, bound - taker)
    shifted = jax.random.randint(jax.random.fold_in(key, 1), (couples,), 0, 1 << 20) % (room + 1)
    tallies = tallies.at[1:1 + 2 * couples:2].set(source_of - shifted).at[2:2 + 2 * couples:2].set(taker + shifted)
    return tallies[jax.random.permutation(jax.random.fold_in(key, 2), amount)]


def bell_draw(key, shape, deviation, reach, pieces=(), held_as=jnp.bfloat16):
    drawn = jax.random.normal(key, shape, jnp.float32) * deviation
    if len(pieces) > 0:
        drawn = levels(key, shape, pieces, -0.22, 0.18) * drawn
    return jnp.clip(drawn, min=-reach, max=reach).astype(held_as)


def setup_inputs(seed: int = 0) -> dict:
    splits = jax.random.split(jax.random.key(seed), 16)
    layer_in = draw_layer_in(jax.random.fold_in(splits[15], 71), 0)
    segment_ids = jax.vmap(lambda own: jnp.searchsorted(jnp.cumsum(ragged(own, DOCS, LEN, DOC_MOST, 1)), jnp.arange(LEN), side="right"))(jax.random.split(splits[1], ROWS)).reshape((ROWS, LEN)).astype(jnp.int32)
    out_grad = bell_draw(splits[2], (ROWS, LEN, D), 1.0, 6.0, ((0, 4), (1, 8)))
    gain_attn = jnp.clip(1.0 + 0.1 * jax.random.normal(splits[3], (D,), jnp.float32), 0.5, 1.5).astype(jnp.bfloat16)
    w_query = bell_draw(splits[4], (D, D), D ** -0.5, 0.15625, ((0, 32),))
    w_key = bell_draw(splits[5], (D, D), D ** -0.5, 0.15625, ((0, 32),))
    w_value = bell_draw(splits[6], (D, D), D ** -0.5, 0.15625, ((0, 32),))
    w_dir = bell_draw(splits[7], (D, D), D ** -0.5, 0.15625, ((0, 32),))
    w_beta = bell_draw(splits[8], (D, HEADS), (D // 4) ** -0.5, 0.3125, ((0, 32),))
    b_beta = jnp.clip(jax.random.uniform(splits[9], (HEADS,), jnp.float32, -2.0, 2.0), -2.0, 2.0).astype(jnp.bfloat16)
    w_out = bell_draw(splits[10], (D, D), (D // 32) ** -0.5, 0.875, ((0, 32),))
    gain_mlp = jnp.clip(1.0 + 0.1 * jax.random.normal(splits[11], (D,), jnp.float32), 0.5, 1.5).astype(jnp.bfloat16)
    w_gate = bell_draw(splits[12], (D, FF), D ** -0.5, 0.15625, ((0, 8), (1, 4)))
    w_up = bell_draw(splits[13], (D, FF), D ** -0.5, 0.15625, ((0, 8), (1, 4)))
    w_down = bell_draw(splits[14], (FF, D), FF ** -0.5, 0.09375, ((0, 4), (1, 8)))
    return {"layer_in": layer_in, "segment_ids": segment_ids, "out_grad": out_grad, "gain_attn": gain_attn, "w_query": w_query, "w_key": w_key, "w_value": w_value, "w_dir": w_dir, "w_beta": w_beta, "b_beta": b_beta, "w_out": w_out, "gain_mlp": gain_mlp, "w_gate": w_gate, "w_up": w_up, "w_down": w_down}


EPS = 1e-06
NEG = -1e+30
HIGH = lax.Precision.HIGHEST

@jax.custom_vjp
def low(v):
    return lax.optimization_barrier(v.astype(jnp.bfloat16)).astype(jnp.float32)

@jax.custom_vjp
def low_back(v):
    return v

def low_keep(v):
    return (low(v), None)

def low_pass(kept, grad):
    return (grad,)

def back_keep(v):
    return (v, None)

def back_low(kept, grad):
    return (low(grad),)
low.defvjp(low_keep, low_pass)
low_back.defvjp(back_keep, back_low)

def norm_in(tensor, gain_vec):
    return tensor * lax.rsqrt(lax.optimization_barrier(jnp.mean(tensor * tensor, axis=-1, keepdims=True)) + EPS) * gain_vec

def span_local(queries, keys_in, directions, logits):
    unit_dirs = directions * lax.rsqrt(lax.optimization_barrier(jnp.sum(directions * directions, axis=-1, keepdims=True)) + EPS)
    beta_rate = 2.0 * jax.nn.sigmoid(logits)
    block_size = queries.shape[-2]
    row_index = lax.broadcasted_iota(jnp.int32, (block_size, block_size), 0)
    col_index = lax.broadcasted_iota(jnp.int32, (block_size, block_size), 1)
    strict_mask = row_index > col_index
    lower_mask = row_index >= col_index
    dir_gram = jnp.einsum('...me,...ne->...mn', unit_dirs, unit_dirs, precision=HIGH)
    system = jnp.where(strict_mask, dir_gram, 0.0) + jnp.where(row_index == col_index, 1.0 / beta_rate[..., :, None], 0.0)
    query_dirs = jnp.where(lower_mask, jnp.einsum('...ie,...me->...im', queries, unit_dirs, precision=HIGH), 0.0)
    dirs_keys = jnp.where(strict_mask, jnp.einsum('...me,...je->...mj', unit_dirs, keys_in, precision=HIGH), 0.0)
    solved_keys = lax.linalg.triangular_solve(system, dirs_keys, left_side=True, lower=True)
    solved_query = lax.linalg.triangular_solve(system, query_dirs, left_side=False, lower=True)
    solved_dirs = lax.linalg.triangular_solve(system, unit_dirs, left_side=True, lower=True)
    intra_score = jnp.einsum('...ie,...je->...ij', queries, keys_in, precision=HIGH) - jnp.einsum('...im,...mj->...ij', query_dirs, solved_keys, precision=HIGH)
    q_in = queries - jnp.einsum('...im,...me->...ie', solved_query, unit_dirs, precision=HIGH)
    k_out = keys_in - jnp.einsum('...mj,...me->...je', solved_keys, unit_dirs, precision=HIGH)
    identity = jnp.eye(queries.shape[-1], dtype=queries.dtype)
    transform = identity - jnp.einsum('...me,...mf->...ef', unit_dirs, solved_dirs, precision=HIGH)
    return (q_in, k_out, transform, intra_score)

def split_heads(tensor, head_count):
    row_count, tok_count, width = tensor.shape
    return tensor.reshape(row_count, tok_count, head_count, width // head_count).transpose(0, 2, 1, 3)

def row_attention(packed):
    queries, keys_all, values_all, directions, logits, segments = packed
    block_count = queries.shape[0] // CH

    def blocks(tensor):
        return split_heads(tensor.reshape(block_count, CH, tensor.shape[-1]), HEADS)
    query_h = blocks(queries)
    key_h = blocks(keys_all)
    value_h = blocks(values_all)
    dir_h = blocks(directions)
    logit_h = logits.reshape(block_count, CH, HEADS).transpose(0, 2, 1)
    q_in, k_out, transform, intra_score = span_local(query_h, key_h, dir_h, logit_h)
    seg_blocks = segments.reshape(block_count, CH)
    block_ids = jnp.arange(block_count)
    row_index = lax.broadcasted_iota(jnp.int32, (CH, CH), 0)
    col_index = lax.broadcasted_iota(jnp.int32, (CH, CH), 1)
    score_scale = 1.0 / math.sqrt(HSIZE)
    flat_values = value_h.transpose(1, 0, 2, 3).reshape(HEADS, block_count * CH, HSIZE)

    def block_step(key_frame, block_index):
        own_seg = seg_blocks[block_index]
        query_r = low(q_in[block_index])
        cross_scores = score_scale * jnp.einsum('hie,ahje->hiaj', query_r, key_frame, precision=HIGH)
        cross_scores = cross_scores.reshape(HEADS, CH, block_count * CH)
        permit_cross = (block_ids[None, :, None] < block_index) & (own_seg[:, None, None] == seg_blocks[None, :, :])
        permit_cross = permit_cross.reshape(CH, block_count * CH)
        permit_intra = (row_index >= col_index) & (own_seg[:, None] == own_seg[None, :])
        scores = low_back(jnp.concatenate([cross_scores, score_scale * intra_score[block_index]], axis=-1))
        permit = jnp.concatenate([permit_cross, permit_intra], axis=-1)[None]
        scores = jnp.where(permit, scores, NEG)
        row_max = lax.optimization_barrier(jnp.max(scores, axis=-1, keepdims=True))
        weights = jnp.exp(scores - row_max)
        probs = low(weights / lax.optimization_barrier(jnp.sum(weights, axis=-1, keepdims=True)))
        both_values = jnp.concatenate([flat_values, value_h[block_index]], axis=1)
        attended = jnp.einsum('hij,hje->hie', probs, both_values, precision=HIGH)
        frame_next = low(jnp.einsum('ahjf,hef->ahje', key_frame, transform[block_index], precision=HIGH))
        earlier = (block_ids < block_index)[:, None, None, None]
        current = (block_ids == block_index)[:, None, None, None]
        key_frame = jnp.where(earlier, frame_next, jnp.where(current, low(k_out[block_index])[None], 0.0))
        return (key_frame, attended)
    frame_start = jnp.zeros((block_count, HEADS, CH, HSIZE), jnp.float32)
    unused, outputs = lax.scan(jax.checkpoint(block_step), frame_start, block_ids)
    return outputs.transpose(0, 2, 1, 3).reshape(block_count * CH, HEADS * HSIZE)

def reference(layer_in, segment_ids, out_grad, gain_attn, w_query, w_key, w_value, w_dir, w_beta, b_beta, w_out, gain_mlp, w_gate, w_up, w_down):
    params = tuple((item.astype(jnp.float32) for item in (gain_attn, w_query, w_key, w_value, w_dir, w_beta, b_beta, w_out, gain_mlp, w_gate, w_up, w_down)))
    layer_f = layer_in.astype(jnp.float32)

    def forward(layer_val, weights):
        gain_one, wq_full, wk_full, wv_full, wdir_full, wbeta_full, bias_full, wout_full, gain_two, gate_full, up_full, down_full = weights
        act_one = low(norm_in(layer_val, gain_one))

        def project(matrix):
            return jnp.dot(act_one, matrix, precision=HIGH)
        queries = low(low_back(project(wq_full)))
        keys_all = low(low_back(project(wk_full)))
        values_all = low(low_back(project(wv_full)))
        directions = low_back(project(wdir_full))
        logits = low_back(project(wbeta_full) + bias_full)
        attended = lax.map(jax.checkpoint(row_attention), (queries, keys_all, values_all, directions, logits, segment_ids))
        attended = low(low_back(attended))
        middle = layer_val + low_back(jnp.dot(attended, wout_full, precision=HIGH))
        act_two = low(norm_in(middle, gain_two))
        gate_val = low_back(jnp.dot(act_two, gate_full, precision=HIGH))
        up_val = low_back(jnp.dot(act_two, up_full, precision=HIGH))
        hidden = low(jax.nn.silu(gate_val) * up_val)
        return middle + low_back(jnp.dot(hidden, down_full, precision=HIGH))
    out_val, pullback = jax.vjp(forward, layer_f, params)
    grad_layer, grads = pullback(out_grad.astype(jnp.float32))
    return (out_val.astype(jnp.bfloat16), grad_layer.astype(jnp.bfloat16), grads[0], grads[1], grads[2], grads[3], grads[4], grads[5], grads[6], grads[7], grads[8], grads[9], grads[10], grads[11])
```

```python
import functools
import math

import jax
import jax.numpy as jnp
from jax import lax
from jax.experimental import pallas as pl
from jax.experimental.pallas import tpu as pltpu
from jax.sharding import PartitionSpec as P

EPS = 1e-06
NEG = -1e30
F32 = jnp.float32
BF16 = jnp.bfloat16
NN = ((1,), (0,))
NT = ((1,), (1,))
TN = ((0,), (0,))
VMEM_BYTES = 56 * 1024 * 1024


def halves(x):
    if x.dtype == BF16:
        return (x,)
    top = x.astype(BF16)
    return (top, (x - top.astype(F32)).astype(BF16))


def dot(left, right, dims):
    total = None
    for a, x in enumerate(left):
        for b, y in enumerate(right):
            if a + b > 1:
                continue
            term = lax.dot_general(x, y, (dims, ((), ())), preferred_element_type=F32)
            total = term if total is None else total + term
    return total


def iotas(size):
    rows = lax.broadcasted_iota(jnp.int32, (size, size), 0)
    cols = lax.broadcasted_iota(jnp.int32, (size, size), 1)
    return rows, cols


def unit_dirs(raw):
    inv = lax.rsqrt(jnp.sum(raw * raw, axis=-1, keepdims=True) + EPS)
    return raw * inv, inv


def local_forward(heads, q_ref, k_ref, raw_ref, logit_ref, qin_ref, kout_ref, ptop_ref, plow_ref,
                  intra_ref, t_ref, e_ref, cm_ref, s_ref):
    size = q_ref.shape[0]
    width = q_ref.shape[1] // heads
    rows, cols = iotas(size)
    strict, lower, diag = rows > cols, rows >= cols, rows == cols
    for h in range(heads):
        at = slice(h * width, (h + 1) * width)
        q, k = q_ref[:, at], k_ref[:, at]
        w, _ = unit_dirs(raw_ref[:, at])
        beta_row = 2.0 * jax.nn.sigmoid(logit_ref[0, h : h + 1, :])
        beta = jnp.where(diag, beta_row, 0.0)
        beta_col = jnp.sum(beta, axis=1, keepdims=True)
        ws = halves(w)
        gram = dot(ws, ws, NT)
        apart = rows ^ cols
        t = beta - jnp.where(strict & (apart == 1), beta_col * gram * beta_row, 0.0)
        shift = 1
        while (1 << shift) < size:
            part = jnp.where(strict & ((apart >> shift) == 1), gram, 0.0)
            ts = halves(t)
            t = t - dot(halves(dot(ts, halves(part), NN)), ts, NN)
            shift += 1
        ts = halves(t)
        b = jnp.where(lower, dot((q,), ws, NT), 0.0)
        m = jnp.where(strict, dot(ws, (k,), NT), 0.0)
        bs = halves(b)
        e = dot(ts, halves(m), NN)
        s = dot(ts, ws, NN)
        cm = dot(bs, ts, NN)
        es = halves(e)
        intra_ref[:, at] = dot((q,), (k,), NT) - dot(bs, es, NN)
        qin_ref[:, at] = (q.astype(F32) - dot(halves(cm), ws, NN)).astype(BF16)
        kout_ref[:, at] = (k.astype(F32) - dot(es, ws, TN)).astype(BF16)
        step = jnp.where(diag, 1.0, 0.0) - dot(ws, halves(s), TN)
        top, low = halves(step)
        ptop_ref[:, at] = top
        plow_ref[:, at] = low
        t_ref[:, at] = t
        e_ref[:, at] = e
        cm_ref[:, at] = cm
        s_ref[:, at] = s


def cross_forward(heads, group, scale, qin_ref, kout_ref, ptop_ref, plow_ref, intra_ref, v_ref,
                  segc_ref, segr_ref, out_ref, prob_ref, keep_ref, frame, score):
    size = qin_ref.shape[0]
    width = qin_ref.shape[1] // heads
    total = v_ref.shape[0]
    wide = group * size
    c = pl.program_id(0)

    @pl.when(c == 0)
    def _():
        frame[...] = jnp.zeros_like(frame)
        score[...] = jnp.full_like(score, NEG)

    rows, cols = iotas(size)
    own = pl.multiple_of(c * size, size)
    seg = segc_ref[...]
    for h in range(heads):
        at = slice(h * width, (h + 1) * width)
        q = qin_ref[:, at]
        for g in range(total // wide):
            part = slice(g * wide, (g + 1) * wide)

            @pl.when(g * group < c)
            def _():
                raw = scale * lax.dot_general(
                    q, frame[h, part, :], (NT, ((), ())), preferred_element_type=F32)
                place = lax.broadcasted_iota(jnp.int32, (size, wide), 1) + g * wide
                permit = (place < own) & (seg == segr_ref[:, part])
                score[h, :, part] = jnp.where(permit, raw, NEG)

        permit = (rows >= cols) & (seg == segr_ref[:, pl.ds(own, size)])
        score[h, :, pl.ds(own, size)] = jnp.where(permit, scale * intra_ref[:, at], NEG)
        s = score[h]
        e = jnp.exp(s - jnp.max(s, axis=-1, keepdims=True))
        p = (e / jnp.sum(e, axis=-1, keepdims=True)).astype(BF16)
        prob_ref[0, h] = p
        out_ref[:, at] = lax.dot_general(
            p, v_ref[:, at], (NN, ((), ())), preferred_element_type=F32).astype(BF16)
        keep_ref[0, h] = frame[h]
        step = (ptop_ref[:, at], plow_ref[:, at])
        for g in range(total // wide):
            part = slice(g * wide, (g + 1) * wide)

            @pl.when(g * group < c)
            def _():
                frame[h, part, :] = dot((frame[h, part, :],), step, NT).astype(BF16)

        frame[h, pl.ds(own, size), :] = kout_ref[:, at]


def cross_backward(heads, group, scale, grad_ref, v_ref, prob_ref, keep_ref, qin_ref, ptop_ref,
                   plow_ref, dqin_ref, dintra_ref, dkout_ref, dstep_ref, dv_ref, carry, dvals, ds_ref):
    size = grad_ref.shape[0]
    width = grad_ref.shape[1] // heads
    total = v_ref.shape[0]
    wide = group * size
    c = pl.num_programs(0) - 1 - pl.program_id(0)

    @pl.when(pl.program_id(0) == 0)
    def _():
        carry[...] = jnp.zeros_like(carry)
        dvals[...] = jnp.zeros_like(dvals)

    own = pl.multiple_of(c * size, size)
    for h in range(heads):
        at = slice(h * width, (h + 1) * width)
        grad, q = grad_ref[:, at], qin_ref[:, at]
        p = prob_ref[0, h]
        dp = lax.dot_general(grad, v_ref[:, at], (NT, ((), ())), preferred_element_type=F32)
        pf = p.astype(F32)
        delta = jnp.sum(pf * dp, axis=-1, keepdims=True)
        ds = (pf * (dp - delta)).astype(BF16)
        ds_ref[h] = ds
        dintra_ref[:, at] = ds_ref[h, :, pl.ds(own, size)]
        dqin_ref[:, at] = scale * lax.dot_general(
            ds, keep_ref[0, h], (NN, ((), ())), preferred_element_type=F32)
        dkout_ref[:, at] = carry[h, pl.ds(own, size), :]
        dstep_ref[:, at] = lax.dot_general(
            carry[h].astype(BF16), keep_ref[0, h], (TN, ((), ())), preferred_element_type=F32)
        step = (ptop_ref[:, at], plow_ref[:, at])
        for g in range(total // wide):
            part = slice(g * wide, (g + 1) * wide)

            @pl.when(g * group <= c)
            def _():
                dvals[h, part, :] += lax.dot_general(
                    prob_ref[0, h, :, part], grad, (TN, ((), ())), preferred_element_type=F32)

            @pl.when(g * group < c)
            def _():
                fresh = scale * lax.dot_general(
                    ds_ref[h, :, part], q, (TN, ((), ())), preferred_element_type=F32)
                carry[h, part, :] = fresh + dot((carry[h, part, :].astype(BF16),), step, NN)

        @pl.when(c == 0)
        def _():
            dv_ref[:, at] = dvals[h].astype(BF16)


def local_backward(heads, scale, q_ref, k_ref, raw_ref, logit_ref, t_ref, e_ref, cm_ref, s_ref,
                   dqin_ref, dintra_ref, dkout_ref, dstep_ref, dq_ref, dk_ref, draw_ref, dlogit_ref):
    size = q_ref.shape[0]
    width = q_ref.shape[1] // heads
    rows, cols = iotas(size)
    strict, lower, diag = rows > cols, rows >= cols, rows == cols
    for h in range(heads):
        at = slice(h * width, (h + 1) * width)
        q, k = (q_ref[:, at],), (k_ref[:, at],)
        raw = raw_ref[:, at]
        w, inv = unit_dirs(raw)
        beta_row = 2.0 * jax.nn.sigmoid(logit_ref[0, h : h + 1, :])
        ws = halves(w)
        ts, es, cms, ss = (halves(ref[:, at]) for ref in (t_ref, e_ref, cm_ref, s_ref))
        dqin, dkout = dqin_ref[:, at], dkout_ref[:, at]
        dintra = (dintra_ref[:, at],)
        dqs, dks, dps = halves(dqin), halves(dkout), halves(dstep_ref[:, at])
        b = jnp.where(lower, dot(q, ws, NT), 0.0)
        d_s = -dot(ws, dps, NN)
        d_e = -(dot(ws, dks, NT) + scale * dot(halves(b), dintra, TN))
        d_cm = -dot(dqs, ws, NT)
        y_s = dot(ts, halves(d_s), TN)
        y_e = dot(ts, halves(d_e), TN)
        y_c = dot(halves(d_cm), ts, NT)
        d_x = -(dot(halves(y_s), ss, NT) + dot(halves(y_e), es, NT) + dot(cms, halves(y_c), TN))
        d_b = halves(jnp.where(lower, y_c - scale * dot(dintra, es, NT), 0.0))
        d_m = halves(jnp.where(strict, y_e, 0.0))
        d_a = halves(jnp.where(strict, d_x, 0.0))
        dq_ref[:, at] = (dqin + scale * dot(dintra, k, NN) + dot(d_b, ws, NN)).astype(BF16)
        dk_ref[:, at] = (dkout + scale * dot(dintra, q, TN) + dot(d_m, ws, TN)).astype(BF16)
        d_w = (y_s - dot(ss, dps, NT) - dot(es, dks, NN) - dot(cms, dqs, TN)
               + dot(d_b, q, TN) + dot(d_m, k, NN) + dot(d_a, ws, NN) + dot(d_a, ws, TN))
        draw = inv * d_w - raw * (inv * inv * inv) * jnp.sum(raw * d_w, axis=-1, keepdims=True)
        draw_ref[:, at] = draw.astype(BF16)
        at_diag = jnp.sum(jnp.where(diag, d_x, 0.0), axis=0, keepdims=True)
        dlogit_ref[0, h : h + 1, :] = -at_diag * (1.0 - 0.5 * beta_row) / beta_row


def run(body, grid, inputs, in_specs, outputs, out_specs, scratch, flops):
    return pl.pallas_call(
        body, grid=(grid,), in_specs=in_specs, out_specs=out_specs, out_shape=outputs,
        scratch_shapes=scratch,
        compiler_params=pltpu.CompilerParams(
            dimension_semantics=("arbitrary",), vmem_limit_bytes=VMEM_BYTES),
        cost_estimate=pl.CostEstimate(
            flops=flops, transcendentals=0,
            bytes_accessed=sum(x.size * x.dtype.itemsize for x in (*inputs, *outputs))),
    )(*inputs)


def shape(dims, dtype):
    return jax.ShapeDtypeStruct(dims, dtype)


def group_of(blocks):
    return 4 if blocks % 4 == 0 else 1


def attention_forward(q, k, v, raw, logits, segments, size):
    tokens, width = q.shape
    blocks, heads, _ = logits.shape
    head = width // heads
    block = pl.BlockSpec((size, width), lambda c: (c, 0))
    square = pl.BlockSpec((head, width), lambda c: (c, 0))
    logit_block = pl.BlockSpec((1, heads, size), lambda c: (c, 0, 0))
    f, b = shape((tokens, width), F32), shape((tokens, width), BF16)
    stepped = shape((blocks * head, width), BF16)
    saved_s = shape((tokens, width), F32)
    qin, kout, ptop, plow, intra, t, e, cm, s = run(
        functools.partial(local_forward, heads), blocks, (q, k, raw, logits),
        [block, block, block, logit_block], (b, b, stepped, stepped, f, f, f, f, saved_s),
        [block, block, square, square, block, block, block, block, block], [],
        blocks * heads * 62 * 2 * size * size * head)
    group = group_of(blocks)
    whole = pl.BlockSpec((tokens, width), lambda c: (0, 0))
    wide_prob = pl.BlockSpec((1, heads, size, tokens), lambda c: (c, 0, 0, 0))
    wide_keep = pl.BlockSpec((1, heads, tokens, head), lambda c: (c, 0, 0, 0))
    out, prob, keep = run(
        functools.partial(cross_forward, heads, group, 1.0 / math.sqrt(head)), blocks,
        (qin, kout, ptop, plow, intra, v, segments.reshape(tokens, 1), segments.reshape(1, tokens)),
        [block, block, square, square, block, whole,
         pl.BlockSpec((size, 1), lambda c: (c, 0)), pl.BlockSpec((1, tokens), lambda c: (0, 0))],
        (b, shape((blocks, heads, size, tokens), BF16), shape((blocks, heads, tokens, head), BF16)),
        [block, wide_prob, wide_keep],
        [pltpu.VMEM((heads, tokens, head), BF16), pltpu.VMEM((heads, size, tokens), F32)],
        blocks * heads * 4 * 2 * size * tokens * head)
    return out, (q, k, v, raw, logits, qin, ptop, plow, t, e, cm, s, prob, keep)


def attention_backward(saved, grad, size):
    q, k, v, raw, logits, qin, ptop, plow, t, e, cm, s, prob, keep = saved
    tokens, width = q.shape
    blocks, heads, _ = logits.shape
    head = width // heads
    scale = 1.0 / math.sqrt(head)
    back = lambda c: (blocks - 1 - c, 0)
    block = pl.BlockSpec((size, width), back)
    square = pl.BlockSpec((head, width), back)
    whole = pl.BlockSpec((tokens, width), lambda c: (0, 0))
    wide_prob = pl.BlockSpec((1, heads, size, tokens), lambda c: (blocks - 1 - c, 0, 0, 0))
    wide_keep = pl.BlockSpec((1, heads, tokens, head), lambda c: (blocks - 1 - c, 0, 0, 0))
    f, b = shape((tokens, width), F32), shape((tokens, width), BF16)
    dqin, dintra, dkout, dstep, dv = run(
        functools.partial(cross_backward, heads, group_of(blocks), scale), blocks,
        (grad, v, prob, keep, qin, ptop, plow),
        [block, whole, wide_prob, wide_keep, block, square, square],
        (f, b, f, shape((blocks * head, width), F32), b),
        [block, block, block, square, whole],
        [pltpu.VMEM((heads, tokens, head), F32), pltpu.VMEM((heads, tokens, head), F32),
         pltpu.VMEM((heads, size, tokens), BF16)],
        blocks * heads * 7 * 2 * size * tokens * head)
    block = pl.BlockSpec((size, width), lambda c: (c, 0))
    square = pl.BlockSpec((head, width), lambda c: (c, 0))
    logit_block = pl.BlockSpec((1, heads, size), lambda c: (c, 0, 0))
    dq, dk, draw, dlogit = run(
        functools.partial(local_backward, heads, scale), blocks,
        (q, k, raw, logits, t, e, cm, s, dqin, dintra, dkout, dstep),
        [block, block, block, logit_block, block, block, block, block, block, block, block, square],
        (b, b, b, shape((blocks, heads, size), F32)), [block, block, block, logit_block], [],
        blocks * heads * 60 * 2 * size * size * head)
    return dq, dk, dv, draw, dlogit


def norm_in(tensor, gain_vec):
    return tensor * lax.rsqrt(jnp.mean(tensor * tensor, axis=-1, keepdims=True) + EPS) * gain_vec


def mm(left, right, dims=NN):
    return lax.dot_general(left, right, (dims, ((), ())), preferred_element_type=F32)


def to_row(x):
    cores, rows = lax.axis_size("wid"), x.shape[0]
    me = lax.axis_index("wid")
    if cores == rows == 2:
        got = lax.ppermute(lax.dynamic_index_in_dim(x, 1 - me, 0, False), "wid", [(0, 1), (1, 0)])
        mine = lax.dynamic_index_in_dim(x, me, 0, False)
        return jnp.concatenate([jnp.where(me == 0, mine, got), jnp.where(me == 0, got, mine)], axis=0)
    every = lax.all_gather(x, "wid", axis=0, tiled=False)
    every = lax.dynamic_index_in_dim(every, me // (cores // rows), 1, False)
    return every.reshape((-1,) + x.shape[2:])


def from_row(x, rows):
    cores = lax.axis_size("wid")
    me = lax.axis_index("wid")
    parts = x.reshape((cores, x.shape[0] // cores) + x.shape[1:])
    if cores == rows == 2:
        got = lax.ppermute(lax.dynamic_index_in_dim(parts, 1 - me, 0, False), "wid", [(0, 1), (1, 0)])
        mine = lax.dynamic_index_in_dim(parts, me, 0, False)
        return jnp.stack([jnp.where(me == 0, mine, got), jnp.where(me == 0, got, mine)], axis=0)
    return lax.all_to_all(parts, "wid", 0, 0, tiled=True)[:: cores // rows]


def per_device(layer_in, segment_ids, out_grad, gain_attn, w_query, w_key, w_value, w_dir, w_beta,
               b_beta, w_out, gain_mlp, w_gate, w_up, w_down):
    every = ("dp", "hid", "wid")
    n_dp, n_hid, n_wid = (lax.axis_size(axis) for axis in every)
    row_count, tok, width = layer_in.shape
    heads = b_beta.shape[0]
    own_heads = heads // n_hid
    span = width // n_hid
    shard = w_query.shape[0]
    held = n_wid * tok
    copies = n_wid // row_count
    my_hid = lax.axis_index("hid")

    row_in = lax.all_gather(to_row(layer_in), "hid", axis=0, tiled=True)
    segs = lax.all_gather(segment_ids, ("hid", "wid"), axis=0, tiled=False)
    segs = lax.dynamic_index_in_dim(segs, lax.axis_index("wid") // copies, 1, False).reshape(-1)

    small = jnp.concatenate([w_beta, gain_attn[:, None], gain_mlp[:, None]], axis=1)
    small = lax.all_gather(small.reshape(-1), every, axis=0, tiled=True).reshape(width, heads + 2)
    beta_own = lax.dynamic_slice_in_dim(small[:, :heads], my_hid * own_heads, own_heads, 1)
    bias_own = lax.dynamic_slice_in_dim(b_beta, my_hid * own_heads, own_heads, 0).astype(F32)
    gain_one, gain_two = small[:, heads].astype(F32), small[:, heads + 1].astype(F32)

    cat = jnp.stack([w_query, w_key, w_value, w_dir], axis=1).reshape(shard, 4, n_hid, span)
    cat = cat.transpose(2, 0, 1, 3).reshape(n_hid, shard, 4 * span)
    cat = lax.all_to_all(cat, "hid", 0, 0, tiled=True)
    cat = lax.all_gather(cat, ("dp", "wid"), axis=0, tiled=False)
    cat = cat.reshape(n_dp, n_wid, n_hid, shard, 4 * span).transpose(0, 2, 1, 3, 4)
    cat = cat.reshape(width, 4 * span)
    wout_full = lax.all_gather(w_out, every, axis=0, tiled=True)

    ff = jnp.stack([w_gate, w_up, w_down.T], axis=0)
    ff_rows, ff_cols = ff.shape[1], ff.shape[2]
    part = ff_cols // n_dp
    ff = ff.reshape(3, ff_rows, n_dp, part).transpose(2, 0, 1, 3)
    ff = lax.all_to_all(ff, "dp", 0, 0, tiled=True)
    ff = lax.all_gather(ff, ("hid", "wid"), axis=0, tiled=False)
    ff = ff.reshape(n_hid, n_wid, n_dp, 3, ff_rows, part).transpose(3, 2, 1, 4, 0, 5)
    ff = ff.reshape(3, width, ff_cols)
    gate_w, up_w, down_wt = ff[0], ff[1], ff[2]

    act_one = norm_in(row_in.astype(F32), gain_one).astype(BF16)
    query = mm(act_one, cat[:, :span]).astype(BF16)
    key = mm(act_one, cat[:, span : 2 * span]).astype(BF16)
    value = mm(act_one, cat[:, 2 * span : 3 * span]).astype(BF16)
    raw = mm(act_one, cat[:, 3 * span :])
    logits = mm(act_one, beta_own) + bias_own
    logits = logits.reshape(-1, tok, own_heads).transpose(0, 2, 1)
    att, saved = attention_forward(query, key, value, raw, logits, segs, tok)

    att = lax.all_to_all(att.reshape(n_hid, held, span), "hid", 0, 0, tiled=True)
    att = from_row(att.transpose(1, 0, 2).reshape(held, width), row_count)
    att = att.reshape(row_count * tok, width)

    layer_f = layer_in.astype(F32).reshape(row_count * tok, width)
    grad_b = out_grad.reshape(row_count * tok, width)
    middle = layer_f + mm(att, wout_full)
    act_two = norm_in(middle, gain_two).astype(BF16)
    act_all = lax.all_gather(act_two, "dp", axis=0, tiled=True)
    grad_all = lax.all_gather(grad_b, "dp", axis=0, tiled=True)
    gate, up = mm(act_all, gate_w), mm(act_all, up_w)
    sig = jax.nn.sigmoid(gate)
    silu = gate * sig
    hidden = (silu * up).astype(BF16)
    mlp = lax.psum_scatter(mm(hidden, down_wt, NT).astype(BF16), "dp", scatter_dimension=0, tiled=True)
    layer_out = (middle + mlp.astype(F32)).astype(BF16)
    d_hidden = mm(grad_all, down_wt)
    d_gate = (d_hidden * up * sig * (1.0 + gate * (1.0 - sig))).astype(BF16)
    d_up = (d_hidden * silu).astype(BF16)
    d_act = mm(d_gate, gate_w, NT) + mm(d_up, up_w, NT)
    d_act = lax.psum_scatter(d_act.astype(BF16), "dp", scatter_dimension=0, tiled=True).astype(F32)
    ff_grads = jnp.stack([mm(act_all, d_gate, TN).astype(BF16), mm(act_all, d_up, TN).astype(BF16),
                          mm(grad_all, hidden, TN).astype(BF16)], axis=0)
    ff_grads = ff_grads.reshape(3, n_dp, n_wid, ff_rows, n_hid, part).transpose(4, 2, 1, 0, 3, 5)
    ff_grads = ff_grads.reshape(n_hid * n_wid, n_dp, 3, ff_rows, part)
    ff_grads = lax.psum_scatter(ff_grads, ("hid", "wid"), scatter_dimension=0, tiled=True)[0]
    ff_grads = lax.all_to_all(ff_grads, "dp", 0, 0, tiled=True)
    ff_grads = ff_grads.transpose(1, 2, 0, 3).reshape(3, ff_rows, ff_cols).astype(F32)

    _, pull_two = jax.vjp(norm_in, middle, gain_two)
    d_mid_norm, d_gain_two = pull_two(d_act)
    d_middle = grad_b.astype(F32) + d_mid_norm
    d_branch = d_middle.astype(BF16)
    d_att = mm(d_branch, wout_full, NT).astype(BF16).reshape(row_count, tok, width)
    d_att = to_row(d_att).reshape(held, n_hid, span).transpose(1, 0, 2)
    d_att = lax.all_to_all(d_att, "hid", 0, 0, tiled=True).reshape(n_hid * held, span)
    grad_wout = mm(att, d_branch, TN).astype(BF16)
    grad_wout = lax.psum_scatter(grad_wout, every, scatter_dimension=0, tiled=True).astype(F32)

    dq, dk, dv, draw, dlogit = attention_backward(saved, d_att, tok)
    d_cat = jnp.concatenate([dq, dk, dv, draw], axis=1)
    d_logit = dlogit.transpose(0, 2, 1).reshape(-1, own_heads).astype(BF16)
    d_act_one = mm(d_cat, cat, NT) + mm(d_logit, beta_own, NT)
    d_act_one = lax.psum_scatter(d_act_one.astype(BF16), "hid", scatter_dimension=0, tiled=True)
    d_act_one = from_row(d_act_one, row_count).reshape(row_count * tok, width).astype(F32)
    if copies > 1:
        first = lax.axis_index("wid") % copies == 0
        d_cat, d_logit = jnp.where(first, d_cat, 0), jnp.where(first, d_logit, 0)
    cat_grad = mm(act_one, d_cat, TN).astype(BF16)
    cat_grad = cat_grad.reshape(n_dp, n_hid, n_wid, shard, 4 * span).transpose(0, 2, 1, 3, 4)
    cat_grad = cat_grad.reshape(n_dp * n_wid, n_hid, shard, 4 * span)
    cat_grad = lax.psum_scatter(cat_grad, ("dp", "wid"), scatter_dimension=0, tiled=True)[0]
    cat_grad = lax.all_to_all(cat_grad, "hid", 0, 0, tiled=True)
    cat_grad = cat_grad.reshape(n_hid, shard, 4, span).transpose(2, 1, 0, 3)
    cat_grad = cat_grad.reshape(4, shard, width).astype(F32)

    _, pull_one = jax.vjp(norm_in, layer_f, gain_one)
    d_in_norm, d_gain_one = pull_one(d_act_one)
    grad_in = (d_middle + d_in_norm).astype(BF16)

    beta_grad = lax.dynamic_update_slice_in_dim(
        jnp.zeros((width, heads), F32), mm(act_one, d_logit, TN), my_hid * own_heads, 1)
    bias_grad = lax.dynamic_update_slice_in_dim(
        jnp.zeros((heads,), F32), jnp.sum(d_logit.astype(F32), axis=0), my_hid * own_heads, 0)
    small_grad = jnp.concatenate([beta_grad, d_gain_one[:, None], d_gain_two[:, None]], axis=1)
    small_grad = lax.psum_scatter(
        small_grad.reshape(n_dp * n_hid * n_wid, -1), every, scatter_dimension=0, tiled=True)
    small_grad = small_grad.reshape(shard, heads + 2)
    bias_grad = lax.psum(bias_grad, every)

    return (
        layer_out.reshape(layer_in.shape), grad_in.reshape(layer_in.shape), small_grad[:, heads],
        cat_grad[0], cat_grad[1], cat_grad[2], cat_grad[3], small_grad[:, :heads], bias_grad,
        grad_wout, small_grad[:, heads + 1], ff_grads[0], ff_grads[1], ff_grads[2].T,
    )


def solution(mesh):
    in_specs = (
        P("dp", ("hid", "wid"), None),
        P("dp", ("hid", "wid")),
        P("dp", ("hid", "wid"), None),
        P(("dp", "hid", "wid")),
        P(("dp", "hid", "wid"), None),
        P(("dp", "hid", "wid"), None),
        P(("dp", "hid", "wid"), None),
        P(("dp", "hid", "wid"), None),
        P(("dp", "hid", "wid"), None),
        P(),
        P(("dp", "hid", "wid"), None),
        P(("dp", "hid", "wid")),
        P(("dp", "wid"), "hid"),
        P(("dp", "wid"), "hid"),
        P("hid", ("dp", "wid")),
    )
    out_specs = (
        P("dp", ("hid", "wid"), None),
        P("dp", ("hid", "wid"), None),
        P(("dp", "hid", "wid")),
        P(("dp", "hid", "wid"), None),
        P(("dp", "hid", "wid"), None),
        P(("dp", "hid", "wid"), None),
        P(("dp", "hid", "wid"), None),
        P(("dp", "hid", "wid"), None),
        P(),
        P(("dp", "hid", "wid"), None),
        P(("dp", "hid", "wid")),
        P(("dp", "wid"), "hid"),
        P(("dp", "wid"), "hid"),
        P("hid", ("dp", "wid")),
    )
    return jax.shard_map(
        per_device, mesh=mesh, in_specs=in_specs, out_specs=out_specs, check_vma=False
    )
```

```python
import functools
import math

import jax
import jax.numpy as jnp
from jax import lax
from jax.experimental import pallas as pl
from jax.experimental.pallas import tpu as pltpu
from jax.sharding import PartitionSpec as P

EPS = 1e-06
NEG = -1e30
F32 = jnp.float32
BF16 = jnp.bfloat16
NN = ((1,), (0,))
NT = ((1,), (1,))
TN = ((0,), (0,))
VMEM_BYTES = 56 * 1024 * 1024
SOME = 2


def mm(left, right, dims=NN):
    return lax.dot_general(left, right, (dims, ((), ())), preferred_element_type=F32)


def halves(x):
    if x.dtype == BF16:
        return (x,)
    top = x.astype(BF16)
    return (top, (x - top.astype(F32)).astype(BF16))


def dot(left, right, dims):
    picked = [(a, b) for a in range(len(left)) for b in range(len(right)) if a + b < 2]
    if len(picked) == 1:
        return mm(left[0], right[0], dims)
    x = jnp.concatenate([left[a] for a, _ in picked], axis=dims[0][0])
    y = jnp.concatenate([right[b] for _, b in picked], axis=dims[1][0])
    return mm(x, y, dims)


def iotas(size):
    rows = lax.broadcasted_iota(jnp.int32, (size, size), 0)
    cols = lax.broadcasted_iota(jnp.int32, (size, size), 1)
    return rows, cols


def unit_dirs(raw):
    inv = lax.rsqrt(jnp.sum(raw * raw, axis=-1, keepdims=True) + EPS)
    return raw * inv, inv


def local_forward(heads, size, q_ref, k_ref, raw_ref, logit_ref, qin_ref, kout_ref, ptop_ref, plow_ref,
                  intra_ref, t_ref, e_ref, cm_ref, s_ref):
    width = q_ref.shape[1] // heads
    rows, cols = iotas(size)
    strict, lower, diag = rows > cols, rows >= cols, rows == cols
    apart = rows ^ cols
    some = range(q_ref.shape[0] // size)
    at = [(slice(n * size, (n + 1) * size), slice(h * width, (h + 1) * width)) for n in some for h in range(heads)]
    wide = [(slice(n * width, (n + 1) * width), slice(h * width, (h + 1) * width)) for n in some for h in range(heads)]
    every = range(len(at))
    betas = [2.0 * jax.nn.sigmoid(logit_ref[n, h : h + 1, :]) for n in some for h in range(heads)]
    q, k = [q_ref[a] for a in at], [k_ref[a] for a in at]
    ws = [halves(unit_dirs(raw_ref[a])[0]) for a in at]
    gram = [jnp.where(strict, dot(w, w, NT), 0.0) for w in ws]
    beta = [jnp.where(diag, b, 0.0) for b in betas]
    beta_col = [jnp.sum(b, axis=1, keepdims=True) for b in beta]
    t = [beta[u] - jnp.where(apart == 1, beta_col[u] * gram[u] * betas[u], 0.0) for u in every]
    shift = 1
    while (1 << shift) < size:
        near = (apart >> shift) == 1
        part = [halves(jnp.where(near, g, 0.0)) for g in gram]
        ts = [halves(x) for x in t]
        once = [dot(ts[u], part[u], NN) for u in every]
        t = [t[u] - dot(halves(once[u]), ts[u], NN) for u in every]
        shift += 1
    ts = [halves(x) for x in t]
    bs = [halves(jnp.where(lower, dot((q[u],), ws[u], NT), 0.0)) for u in every]
    ms = [halves(jnp.where(strict, dot(ws[u], (k[u],), NT), 0.0)) for u in every]
    e = [dot(ts[u], ms[u], NN) for u in every]
    s = [dot(ts[u], ws[u], NN) for u in every]
    cm = [dot(bs[u], ts[u], NN) for u in every]
    es = [halves(x) for x in e]
    for u in every:
        t_ref[at[u]], e_ref[at[u]], cm_ref[at[u]], s_ref[at[u]] = t[u], e[u], cm[u], s[u]
        intra_ref[at[u]] = dot((q[u],), (k[u],), NT) - dot(bs[u], es[u], NN)
        qin_ref[at[u]] = (q[u].astype(F32) - dot(halves(cm[u]), ws[u], NN)).astype(BF16)
        kout_ref[at[u]] = (k[u].astype(F32) - dot(es[u], ws[u], TN)).astype(BF16)
        step = jnp.where(diag, 1.0, 0.0) - dot(ws[u], halves(s[u]), TN)
        ptop_ref[wide[u]], plow_ref[wide[u]] = halves(step)


def cross_forward(heads, group, scale, qin_ref, kout_ref, ptop_ref, plow_ref, intra_ref, v_ref,
                  segc_ref, segr_ref, out_ref, prob_ref, keep_ref, frame, score):
    size = qin_ref.shape[0]
    width = qin_ref.shape[1] // heads
    total = v_ref.shape[0]
    wide = group * size
    c = pl.program_id(0)
    parts = [slice(g * wide, (g + 1) * wide) for g in range(total // wide)]
    at = [slice(h * width, (h + 1) * width) for h in range(heads)]
    every = range(heads)

    @pl.when(c == 0)
    def _():
        frame[...] = jnp.zeros_like(frame)
        score[...] = jnp.full_like(score, NEG)

    rows, cols = iotas(size)
    own = pl.multiple_of(c * size, size)
    seg = segc_ref[...]
    for g, part in enumerate(parts):

        @pl.when(g * group < c)
        def _():
            raw = [mm(qin_ref[:, at[h]], frame[h, part, :], NT) for h in every]
            place = lax.broadcasted_iota(jnp.int32, (size, wide), 1) + g * wide
            permit = (place < own) & (seg == segr_ref[:, part])
            for h in every:
                score[h, :, part] = jnp.where(permit, scale * raw[h], NEG)

    permit = (rows >= cols) & (seg == segr_ref[:, pl.ds(own, size)])
    for h in every:
        score[h, :, pl.ds(own, size)] = jnp.where(permit, scale * intra_ref[:, at[h]], NEG)
    top = [jnp.max(score[h], axis=-1, keepdims=True) for h in every]
    e = [jnp.exp(score[h] - top[h]) for h in every]
    inv = [1.0 / jnp.sum(x, axis=-1, keepdims=True) for x in e]
    for h in every:
        prob_ref[0, h] = (e[h] * inv[h]).astype(BF16)
    for h in every:
        out_ref[:, at[h]] = mm(prob_ref[0, h], v_ref[:, at[h]]).astype(BF16)
        keep_ref[0, h] = frame[h]
    for g, part in enumerate(parts):

        @pl.when(g * group < c)
        def _():
            moved = [dot((frame[h, part, :],), (ptop_ref[:, at[h]], plow_ref[:, at[h]]), NT) for h in every]
            for h in every:
                frame[h, part, :] = moved[h].astype(BF16)

    for h in every:
        frame[h, pl.ds(own, size), :] = kout_ref[:, at[h]]


def cross_backward(heads, group, scale, grad_ref, v_ref, prob_ref, keep_ref, qin_ref, ptop_ref,
                   plow_ref, dqin_ref, dintra_ref, dkout_ref, dstep_ref, dv_ref, carry, dvals, ds_ref):
    size = grad_ref.shape[0]
    width = grad_ref.shape[1] // heads
    total = v_ref.shape[0]
    wide = group * size
    c = pl.num_programs(0) - 1 - pl.program_id(0)
    parts = [slice(g * wide, (g + 1) * wide) for g in range(total // wide)]
    at = [slice(h * width, (h + 1) * width) for h in range(heads)]
    every = range(heads)

    @pl.when(pl.program_id(0) == 0)
    def _():
        carry[...] = jnp.zeros_like(carry)
        dvals[...] = jnp.zeros_like(dvals)

    own = pl.multiple_of(c * size, size)
    dp = [mm(grad_ref[:, at[h]], v_ref[:, at[h]], NT) for h in every]
    pf = [prob_ref[0, h].astype(F32) for h in every]
    delta = [jnp.sum(pf[h] * dp[h], axis=-1, keepdims=True) for h in every]
    for h in every:
        ds_ref[h] = (pf[h] * (dp[h] - delta[h])).astype(BF16)
    low = [carry[h].astype(BF16) for h in every]
    dqin = [mm(ds_ref[h], keep_ref[0, h]) for h in every]
    dstep = [mm(low[h], keep_ref[0, h], TN) for h in every]
    for h in every:
        dqin_ref[:, at[h]] = scale * dqin[h]
        dstep_ref[:, at[h]] = dstep[h]
        dintra_ref[:, at[h]] = ds_ref[h, :, pl.ds(own, size)]
        dkout_ref[:, at[h]] = carry[h, pl.ds(own, size), :]
    for g, part in enumerate(parts):

        @pl.when(g * group <= c)
        def _():
            more = [mm(prob_ref[0, h, :, part], grad_ref[:, at[h]], TN) for h in every]
            for h in every:
                dvals[h, part, :] += more[h]

        @pl.when(g * group < c)
        def _():
            fresh = [mm(ds_ref[h, :, part], qin_ref[:, at[h]], TN) for h in every]
            moved = [dot((carry[h, part, :].astype(BF16),), (ptop_ref[:, at[h]], plow_ref[:, at[h]]), NN)
                     for h in every]
            for h in every:
                carry[h, part, :] = scale * fresh[h] + moved[h]

    @pl.when(c == 0)
    def _():
        for h in every:
            dv_ref[:, at[h]] = dvals[h].astype(BF16)


def local_backward(heads, size, scale, q_ref, k_ref, raw_ref, logit_ref, t_ref, e_ref, cm_ref, s_ref,
                   dqin_ref, dintra_ref, dkout_ref, dstep_ref, dq_ref, dk_ref, draw_ref, dlogit_ref):
    width = q_ref.shape[1] // heads
    rows, cols = iotas(size)
    strict, lower, diag = rows > cols, rows >= cols, rows == cols
    some = range(q_ref.shape[0] // size)
    units = [(n, h) for n in some for h in range(heads)]
    at = [(slice(n * size, (n + 1) * size), slice(h * width, (h + 1) * width)) for n, h in units]
    wide = [(slice(n * width, (n + 1) * width), slice(h * width, (h + 1) * width)) for n, h in units]
    every = range(len(units))
    q, k = [(q_ref[a],) for a in at], [(k_ref[a],) for a in at]
    both = [unit_dirs(raw_ref[a]) for a in at]
    betas = [2.0 * jax.nn.sigmoid(logit_ref[n, h : h + 1, :]) for n, h in units]
    ws = [halves(w) for w, _ in both]
    ts, es, cms, ss = ([halves(ref[a]) for a in at] for ref in (t_ref, e_ref, cm_ref, s_ref))
    dintra = [(dintra_ref[a],) for a in at]
    dqs, dks = [halves(dqin_ref[a]) for a in at], [halves(dkout_ref[a]) for a in at]
    dps = [halves(dstep_ref[a]) for a in wide]
    b = [halves(jnp.where(lower, dot(q[u], ws[u], NT), 0.0)) for u in every]
    d_s = [halves(-dot(ws[u], dps[u], NN)) for u in every]
    d_e = [halves(-(dot(ws[u], dks[u], NT) + scale * dot(b[u], dintra[u], TN))) for u in every]
    d_cm = [halves(-dot(dqs[u], ws[u], NT)) for u in every]
    y_s = [dot(ts[u], d_s[u], TN) for u in every]
    y_e = [dot(ts[u], d_e[u], TN) for u in every]
    y_c = [dot(d_cm[u], ts[u], NT) for u in every]
    d_x = [-(dot(halves(y_s[u]), ss[u], NT) + dot(halves(y_e[u]), es[u], NT) + dot(cms[u], halves(y_c[u]), TN))
           for u in every]
    d_b = [halves(jnp.where(lower, y_c[u] - scale * dot(dintra[u], es[u], NT), 0.0)) for u in every]
    d_m = [halves(jnp.where(strict, y_e[u], 0.0)) for u in every]
    d_a = [halves(jnp.where(strict, d_x[u], 0.0)) for u in every]
    for u in every:
        a = at[u]
        dq_ref[a] = (dqin_ref[a] + scale * dot(dintra[u], k[u], NN) + dot(d_b[u], ws[u], NN)).astype(BF16)
        dk_ref[a] = (dkout_ref[a] + scale * dot(dintra[u], q[u], TN) + dot(d_m[u], ws[u], TN)).astype(BF16)
    d_w = [y_s[u] - dot(ss[u], dps[u], NT) - dot(es[u], dks[u], NN) - dot(cms[u], dqs[u], TN)
           + dot(d_b[u], q[u], TN) + dot(d_m[u], k[u], NN) + dot(d_a[u], ws[u], NN) + dot(d_a[u], ws[u], TN)
           for u in every]
    for u, (n, h) in enumerate(units):
        raw, inv = raw_ref[at[u]], both[u][1]
        draw = inv * d_w[u] - raw * (inv * inv * inv) * jnp.sum(raw * d_w[u], axis=-1, keepdims=True)
        draw_ref[at[u]] = draw.astype(BF16)
        at_diag = jnp.sum(jnp.where(diag, d_x[u], 0.0), axis=0, keepdims=True)
        dlogit_ref[n, h : h + 1, :] = -at_diag * (1.0 - 0.5 * betas[u]) / betas[u]


def run(body, grid, inputs, in_specs, outputs, out_specs, scratch, flops):
    return pl.pallas_call(
        body, grid=(grid,), in_specs=in_specs, out_specs=out_specs, out_shape=outputs,
        scratch_shapes=scratch,
        compiler_params=pltpu.CompilerParams(
            dimension_semantics=("arbitrary",), vmem_limit_bytes=VMEM_BYTES),
        cost_estimate=pl.CostEstimate(
            flops=flops, transcendentals=0,
            bytes_accessed=sum(x.size * x.dtype.itemsize for x in (*inputs, *outputs))),
    )(*inputs)


def shape(dims, dtype):
    return jax.ShapeDtypeStruct(dims, dtype)


def group_of(blocks):
    return 4 if blocks % 4 == 0 else 1


def attention_local(q, k, raw, logits, size):
    tokens, width = q.shape
    blocks, heads, _ = logits.shape
    head = width // heads
    some = SOME if blocks % SOME == 0 else 1
    block = pl.BlockSpec((some * size, width), lambda c: (c, 0))
    square = pl.BlockSpec((some * head, width), lambda c: (c, 0))
    logit_block = pl.BlockSpec((some, heads, size), lambda c: (c, 0, 0))
    f, b = shape((tokens, width), F32), shape((tokens, width), BF16)
    stepped = shape((blocks * head, width), BF16)
    return run(
        functools.partial(local_forward, heads, size), blocks // some, (q, k, raw, logits),
        [block, block, block, logit_block], (b, b, stepped, stepped, f, f, f, f, f),
        [block, block, square, square, block, block, block, block, block], [],
        blocks * heads * 62 * 2 * size * size * head)


def attention_cross(q, k, v, raw, logits, segments, local, size):
    qin, kout, ptop, plow, intra, t, e, cm, s = local
    tokens, width = q.shape
    blocks, heads, _ = logits.shape
    head = width // heads
    block = pl.BlockSpec((size, width), lambda c: (c, 0))
    square = pl.BlockSpec((head, width), lambda c: (c, 0))
    b = shape((tokens, width), BF16)
    group = group_of(blocks)
    whole = pl.BlockSpec((tokens, width), lambda c: (0, 0))
    wide_prob = pl.BlockSpec((1, heads, size, tokens), lambda c: (c, 0, 0, 0))
    wide_keep = pl.BlockSpec((1, heads, tokens, head), lambda c: (c, 0, 0, 0))
    out, prob, keep = run(
        functools.partial(cross_forward, heads, group, 1.0 / math.sqrt(head)), blocks,
        (qin, kout, ptop, plow, intra, v, segments.reshape(tokens, 1), segments.reshape(1, tokens)),
        [block, block, square, square, block, whole,
         pl.BlockSpec((size, 1), lambda c: (c, 0)), pl.BlockSpec((1, tokens), lambda c: (0, 0))],
        (b, shape((blocks, heads, size, tokens), BF16), shape((blocks, heads, tokens, head), BF16)),
        [block, wide_prob, wide_keep],
        [pltpu.VMEM((heads, tokens, head), BF16), pltpu.VMEM((heads, size, tokens), F32)],
        blocks * heads * 4 * 2 * size * tokens * head)
    return out, (q, k, v, raw, logits, qin, ptop, plow, t, e, cm, s, prob, keep)


def attention_backward_cross(saved, grad, size):
    q, k, v, raw, logits, qin, ptop, plow, t, e, cm, s, prob, keep = saved
    tokens, width = q.shape
    blocks, heads, _ = logits.shape
    head = width // heads
    scale = 1.0 / math.sqrt(head)
    back = lambda c: (blocks - 1 - c, 0)
    block = pl.BlockSpec((size, width), back)
    square = pl.BlockSpec((head, width), back)
    whole = pl.BlockSpec((tokens, width), lambda c: (0, 0))
    wide_prob = pl.BlockSpec((1, heads, size, tokens), lambda c: (blocks - 1 - c, 0, 0, 0))
    wide_keep = pl.BlockSpec((1, heads, tokens, head), lambda c: (blocks - 1 - c, 0, 0, 0))
    f, b = shape((tokens, width), F32), shape((tokens, width), BF16)
    dqin, dintra, dkout, dstep, dv = run(
        functools.partial(cross_backward, heads, group_of(blocks), scale), blocks,
        (grad, v, prob, keep, qin, ptop, plow),
        [block, whole, wide_prob, wide_keep, block, square, square],
        (f, b, f, shape((blocks * head, width), F32), b),
        [block, block, block, square, whole],
        [pltpu.VMEM((heads, tokens, head), F32), pltpu.VMEM((heads, tokens, head), F32),
         pltpu.VMEM((heads, size, tokens), BF16)],
        blocks * heads * 7 * 2 * size * tokens * head)
    return dv, dqin, dintra, dkout, dstep


def attention_backward_local(saved, crossed, size):
    q, k, v, raw, logits, qin, ptop, plow, t, e, cm, s, prob, keep = saved
    tokens, width = q.shape
    blocks, heads, _ = logits.shape
    head = width // heads
    scale = 1.0 / math.sqrt(head)
    some = SOME if blocks % SOME == 0 else 1
    b = shape((tokens, width), BF16)
    block = pl.BlockSpec((some * size, width), lambda c: (c, 0))
    square = pl.BlockSpec((some * head, width), lambda c: (c, 0))
    logit_block = pl.BlockSpec((some, heads, size), lambda c: (c, 0, 0))
    return run(
        functools.partial(local_backward, heads, size, scale), blocks // some,
        (q, k, raw, logits, t, e, cm, s, *crossed),
        [block, block, block, logit_block, block, block, block, block, block, block, block, square],
        (b, b, b, shape((blocks, heads, size), F32)), [block, block, block, logit_block], [],
        blocks * heads * 60 * 2 * size * size * head)


def ff_forward(me_ref, act_ref, grad_ref, own_ref, other_ref, mlp_ref, dact_ref, hid_ref, dgate_ref, dup_ref,
               gate_w, up_w, down_w, mlp, dact):
    tokens = act_ref.shape[0]
    cores, chips, rows = own_ref.shape[1] + other_ref.shape[1], own_ref.shape[2], own_ref.shape[4]
    tile = min(tokens, 256)

    for r in range(chips):
        for n in range(cores):
            held = own_ref.at[0, 0, r] if n == 0 else other_ref.at[0, n - 1, r]
            chip, core = me_ref[0] ^ r, me_ref[1] ^ n
            to = pl.ds(pl.multiple_of((chip * cores + core) * rows, rows), rows)
            gate_w[to, :] = held[0]
            up_w[to, :] = held[1]
            down_w[to, :] = held[2]

    @pl.when(pl.program_id(0) == 0)
    def _():
        mlp[...] = jnp.zeros_like(mlp)
        dact[...] = jnp.zeros_like(dact)

    @pl.loop(0, tokens // tile)
    def _(i):
        at = pl.ds(pl.multiple_of(i * tile, tile), tile)
        act, grad = act_ref[at, :], grad_ref[at, :]
        gate, up = mm(act, gate_w[...]), mm(act, up_w[...])
        sig = jax.nn.sigmoid(gate)
        silu = gate * sig
        hidden = (silu * up).astype(BF16)
        d_hidden = mm(grad, down_w[...])
        d_gate = (d_hidden * up * sig * (1.0 + gate * (1.0 - sig))).astype(BF16)
        d_up = (d_hidden * silu).astype(BF16)
        hid_ref[at, :] = hidden
        dgate_ref[at, :] = d_gate
        dup_ref[at, :] = d_up
        mlp[at, :] += mm(hidden, down_w[...], NT)
        dact[at, :] += mm(d_gate, gate_w[...], NT) + mm(d_up, up_w[...], NT)

    @pl.when(pl.program_id(0) == pl.num_programs(0) - 1)
    def _():
        mlp_ref[...] = mlp[...].astype(BF16)
        dact_ref[...] = dact[...].astype(BF16)


def ff_weights(me_ref, act_ref, grad_ref, hid_ref, dgate_ref, dup_ref, own_ref, other_ref):
    cores, chips, rows = own_ref.shape[1] + other_ref.shape[1], own_ref.shape[2], own_ref.shape[4]
    for d in range(chips):
        at = slice(d * cores * rows, (d + 1) * cores * rows)
        act, grad = act_ref[:, at], grad_ref[:, at]
        r = me_ref[0] ^ d
        for i, part in enumerate((mm(act, dgate_ref[...], TN), mm(act, dup_ref[...], TN),
                                  mm(grad, hid_ref[...], TN))):
            pieces = [part[w * rows : (w + 1) * rows, :].astype(BF16) for w in range(cores)]
            for n in range(cores):
                piece = pieces[0]
                for w in range(1, cores):
                    piece = jnp.where((me_ref[1] ^ n) == w, pieces[w], piece)
                if n == 0:
                    own_ref[0, 0, r, i] = piece
                else:
                    other_ref[0, n - 1, r, i] = piece


def place_self():
    return jnp.stack([lax.axis_index("dp"), lax.axis_index("wid")]).astype(jnp.int32)


SCALARS = pl.BlockSpec(memory_space=pltpu.SMEM)


def feed_forward(act, grad, own, other):
    tokens, width = act.shape
    groups, part = own.shape[0], own.shape[5]
    whole = pl.BlockSpec((tokens, width), lambda h: (0, 0))
    units = pl.BlockSpec((tokens, part), lambda h: (0, h))
    held = [pl.BlockSpec((1,) + x.shape[1:], lambda h: (h, 0, 0, 0, 0, 0)) for x in (own, other)]
    full, some = shape((tokens, width), BF16), shape((tokens, groups * part), BF16)
    flops = 6 * 2 * tokens * width * groups * part
    return run(ff_forward, groups, (place_self(), act, grad, own, other), [SCALARS, whole, whole, *held],
               (full, full, some, some, some), [whole, whole, units, units, units],
               [pltpu.VMEM((width, part), BF16)] * 3 + [pltpu.VMEM((tokens, width), F32)] * 2, flops)


def feed_forward_weights(act, grad, hidden, d_gate, d_up, own, other):
    tokens, width = act.shape
    groups, part = own.shape[0], own.shape[5]
    whole = pl.BlockSpec((tokens, width), lambda h: (0, 0))
    units = pl.BlockSpec((tokens, part), lambda h: (0, h))
    held = [pl.BlockSpec((1,) + x.shape[1:], lambda h: (h, 0, 0, 0, 0, 0)) for x in (own, other)]
    return run(ff_weights, groups, (place_self(), act, grad, hidden, d_gate, d_up),
               [SCALARS, whole, whole, units, units, units],
               (shape(own.shape, BF16), shape(other.shape, BF16)), held, [],
               3 * 2 * tokens * width * groups * part)


def row_grads(me_ref, left_ref, right_ref, side_ref, own_ref, other_ref):
    cores, shards, rows = own_ref.shape[0] + other_ref.shape[0], own_ref.shape[2], own_ref.shape[3]
    columns, side = right_ref.shape[1], side_ref.shape[1]
    for start in range(0, columns, 512):
        stop = min(start + 512, columns)
        part = mm(left_ref[...], right_ref[:, start:stop], TN)
        if stop == columns:
            beside = side_ref[...]
            if side < stop - start:
                beside = jnp.concatenate([jnp.zeros((part.shape[0], stop - start - side), F32), beside], axis=1)
            part = part + beside
        part = part.astype(BF16)
        for h in range(shards):
            pieces = [part[(h * cores + w) * rows : (h * cores + w + 1) * rows, :] for w in range(cores)]
            for n in range(cores):
                piece = pieces[0]
                for w in range(1, cores):
                    piece = jnp.where((me_ref[1] ^ n) == w, pieces[w], piece)
                if n == 0:
                    own_ref[0, 0, h, :, start:stop] = piece
                else:
                    other_ref[n - 1, 0, h, :, start:stop] = piece


def row_gradients(left, right, side, chips, shards, cores):
    tokens, width = left.shape
    columns = right.shape[1]
    rows = width // (chips * shards * cores)
    if rows % 16:
        full = mm(left, right, TN) + jnp.pad(side, ((0, 0), (columns - side.shape[1], 0)))
        full = full.astype(BF16).reshape(chips, shards, cores, rows, columns)
        full = jnp.take(full, lax.axis_index("wid") ^ jnp.arange(cores), axis=2).transpose(2, 0, 1, 3, 4)
        return full[:1], full[1:]
    outs = [shape((n, chips, shards, rows, columns), BF16) for n in (1, cores - 1)]
    specs = [pl.BlockSpec((x.shape[0], 1, shards, rows, columns), lambda d: (0, d, 0, 0, 0)) for x in outs]
    return run(row_grads, chips, (place_self(), left, right, side),
               [SCALARS, pl.BlockSpec((tokens, width // chips), lambda d: (0, d)),
                pl.BlockSpec((tokens, columns), lambda d: (0, 0)),
                pl.BlockSpec((width // chips, side.shape[1]), lambda d: (d, 0))],
               tuple(outs), specs, [], 2 * tokens * width * columns)


def lay_rows(turned, me_ref, own_ref, other_ref, out_ref):
    cores, shards, rows = own_ref.shape[0] + other_ref.shape[0], own_ref.shape[2], own_ref.shape[3]
    for k in range(shards):
        h = lax.rem(me_ref[2] - k + shards, shards) if turned else k
        for n in range(cores):
            to = pl.ds(pl.multiple_of((h * cores + (me_ref[1] ^ n)) * rows, rows), rows)
            out_ref[to, :] = own_ref[0, 0, k] if n == 0 else other_ref[n - 1, 0, k]


def gathered_rows(own, other, turned=True):
    _, chips, shards, rows, columns = own.shape
    cores = 1 + other.shape[0]
    if rows % 16:
        full = jnp.concatenate([own, other], axis=0)
        full = jnp.take(full, lax.axis_index("wid") ^ jnp.arange(cores), axis=0)
        if turned:
            full = jnp.take(full, (lax.axis_index("hid") - jnp.arange(shards)) % shards, axis=2)
        return full.transpose(1, 2, 0, 3, 4).reshape(-1, columns)
    me = jnp.concatenate([place_self(), lax.axis_index("hid")[None].astype(jnp.int32)])
    specs = [pl.BlockSpec((x.shape[0], 1, shards, rows, columns), lambda d: (0, d, 0, 0, 0)) for x in (own, other)]
    size = cores * shards * rows
    return run(functools.partial(lay_rows, turned), chips, (me, own, other), [SCALARS, *specs],
               (shape((chips * size, columns), BF16),), [pl.BlockSpec((size, columns), lambda d: (d, 0))], [], 0)[0]


def norm_in(tensor, gain_vec):
    return tensor * lax.rsqrt(jnp.mean(tensor * tensor, axis=-1, keepdims=True) + EPS) * gain_vec


def pick(x, index, axis=0):
    return lax.dynamic_index_in_dim(x, index, axis, keepdims=False)


def place(buffer, piece, index, axis=0):
    return lax.dynamic_update_index_in_dim(buffer, piece, index, axis)


def add(left, *others):
    total = left.astype(F32)
    for other in others:
        total = total + other.astype(F32)
    return total.astype(left.dtype)


def to_row(x):
    cores, rows = lax.axis_size("wid"), x.shape[0]
    me = lax.axis_index("wid")
    if cores == rows == 2:
        got = lax.ppermute(pick(x, 1 - me), "wid", [(0, 1), (1, 0)])
        mine = pick(x, me)
        return jnp.concatenate([jnp.where(me == 0, mine, got), jnp.where(me == 0, got, mine)], axis=0)
    every = pick(lax.all_gather(x, "wid", axis=0, tiled=False), me // (cores // rows), 1)
    return every.reshape((-1,) + x.shape[2:])


def from_row(x, rows):
    cores = lax.axis_size("wid")
    me = lax.axis_index("wid")
    parts = x.reshape((cores, x.shape[0] // cores) + x.shape[1:])
    if cores == rows == 2:
        got = lax.ppermute(pick(parts, 1 - me), "wid", [(0, 1), (1, 0)])
        mine = pick(parts, me)
        return jnp.stack([jnp.where(me == 0, mine, got), jnp.where(me == 0, got, mine)], axis=0)
    return lax.all_to_all(parts, "wid", 0, 0, tiled=True)[:: cores // rows]


def line_step(right, left, axis):
    count = lax.axis_size(axis)
    return (lax.ppermute(right, axis, [(i, i + 1) for i in range(count - 1)]),
            lax.ppermute(left, axis, [(i + 1, i) for i in range(count - 1)]))


def line_pieces(steps, axis):
    count, me = lax.axis_size(axis), lax.axis_index(axis)
    pieces = [(me, steps[0][0])]
    for k in range(1, count):
        pieces.append((lax.rem(me - k + count, count), jnp.where(me >= k, steps[k][0], steps[count - k][1])))
    return pieces


def sum_send(pieces, received, t, axis):
    count, me = lax.axis_size(axis), lax.axis_index(axis)
    mine, yours = (pick(pieces, jnp.minimum(me + count - t, count - 1)), pick(pieces, jnp.maximum(me - count + t, 0)))
    if received:
        mine, yours = add(mine, received[0]), add(yours, received[1])
    mine, yours = together(mine, yours)
    return (lax.ppermute(mine, axis, [(i, i + 1) for i in range(t)]),
            lax.ppermute(yours, axis, [(count - 1 - i, count - 2 - i) for i in range(t)]))


def choose(parts, index):
    return lax.select_n(index.astype(jnp.int32), *parts)


def exchange(blocks, axis):
    count, me = lax.axis_size(axis), lax.axis_index(axis)
    got = [choose(blocks, me)]
    for k in range(1, count):
        sent = choose(blocks, lax.rem(me + k, count))
        got.append(lax.ppermute(sent, axis, [(i, (i + k) % count) for i in range(count)]))
    return got


def by_source(got, axis):
    count, me = lax.axis_size(axis), lax.axis_index(axis)
    return [choose(got, lax.rem(me - j + count, count)) for j in range(count)]


def pairs(count, flip):
    return [(i, i ^ flip) for i in range(count)]


def gather_near(x, axis):
    if lax.axis_size(axis) != 4:
        return (x,)
    return x, lax.ppermute(x, axis, pairs(4, 1)), lax.ppermute(x, axis, pairs(4, 2))


def gather_far(near, axis):
    if len(near) == 1:
        return near
    x, one, two = near
    half = x.shape[0] // 2
    return x, one, two, lax.ppermute(one[:half], axis, pairs(4, 2)), lax.ppermute(two[half:], axis, pairs(4, 1))


def gather_end(far, axis):
    if len(far) == 1:
        return lax.all_gather(far[0], axis, axis=0, tiled=False)
    x, one, two, top, low = far
    me = lax.axis_index(axis)
    out = jnp.zeros((4,) + x.shape, x.dtype)
    out = place(place(place(out, x, me), one, me ^ 1), two, me ^ 2)
    return place(out, jnp.concatenate([top, low], axis=0), me ^ 3)


def square_gather(x, axis):
    return gather_end(gather_far(gather_near(x, axis), axis), axis)


def sum_far(x, axis):
    if lax.axis_size(axis) != 4:
        return (x,)
    half = x.shape[1] // 2
    far = pick(x, lax.axis_index(axis) ^ 3)
    return x, lax.ppermute(far[:half], axis, pairs(4, 2)), lax.ppermute(far[half:], axis, pairs(4, 1))


def sum_near(far, axis):
    if len(far) == 1:
        return (lax.psum_scatter(far[0], axis, scatter_dimension=0, tiled=False),)
    x, top, low = far
    me = lax.axis_index(axis)
    half = x.shape[1] // 2
    one, two = pick(x, me ^ 1), pick(x, me ^ 2)
    one = jnp.concatenate([add(one[:half], top), one[half:]], axis=0)
    two = jnp.concatenate([two[:half], add(two[half:], low)], axis=0)
    one, two = together(one, two)
    return pick(x, me), lax.ppermute(one, axis, pairs(4, 1)), lax.ppermute(two, axis, pairs(4, 2))


def from_cores(x):
    cores = lax.axis_size("wid")
    return jnp.stack([lax.ppermute(x, "wid", pairs(cores, n)) for n in range(1, cores)], axis=0)


def core_sum(own, other):
    cores = lax.axis_size("wid")
    return add(own, *[lax.ppermute(other[n - 1 : n], "wid", pairs(cores, n)) for n in range(1, cores)])


def together(*values):
    return lax.optimization_barrier(values)


def per_device(layer_in, segment_ids, out_grad, gain_attn, w_query, w_key, w_value, w_dir, w_beta,
               b_beta, w_out, gain_mlp, w_gate, w_up, w_down):
    n_dp, n_hid, n_wid = (lax.axis_size(axis) for axis in ("dp", "hid", "wid"))
    row_count, tok, width = layer_in.shape
    heads = b_beta.shape[0]
    own_heads = heads // n_hid
    span = width // n_hid
    shard = w_query.shape[0]
    held = n_wid * tok
    copies = n_wid // row_count
    my_hid, my_dp = lax.axis_index("hid"), lax.axis_index("dp")
    side = 128
    columns = 4 * span + side

    row_own = to_row(layer_in)
    row_own, w_query, w_key, w_value, w_dir, w_beta = together(row_own, w_query, w_key, w_value, w_dir, w_beta)
    line = [(row_own, row_own)]
    line.append(line_step(*line[-1], "hid"))

    down_t = w_down.T
    ff_rows, ff_cols = down_t.shape
    part = ff_cols // n_dp

    blank = jnp.zeros((shard, side - own_heads - 2), BF16)
    blocks = []
    for j in range(n_hid):
        at = slice(j * span, (j + 1) * span)
        blocks.append(jnp.concatenate(
            [w_query[:, at], w_key[:, at], w_value[:, at], w_dir[:, at],
             w_beta[:, j * own_heads : (j + 1) * own_heads], gain_attn[:, None], gain_mlp[:, None], blank], axis=1))
    cat = exchange(blocks, "hid")
    cut = [jnp.stack([x[:, j * part : (j + 1) * part] for x in (w_gate, w_up, down_t)]) for j in range(n_dp)]
    cat, line[1], cut, w_out = together(cat, line[1], cut, w_out)
    line.append(line_step(*line[-1], "hid"))
    cat = gather_near(jnp.stack(cat, axis=0), "dp")
    wout = exchange([w_out] * n_hid, "hid")
    ff = [choose(cut, my_dp)]
    for r in range(1, n_dp):
        ff.append(lax.ppermute(choose(cut, my_dp ^ r), "dp", pairs(n_dp, r)))
    cat, line[2] = together(cat, line[2])
    line.append(line_step(*line[-1], "hid"))
    cat = gather_end(gather_far(cat, "dp"), "dp")
    cat = gathered_rows(cat[None], from_cores(cat))
    gain_one = cat[:, 4 * span + own_heads].astype(F32)
    gain_two = cat[:, 4 * span + own_heads + 1].astype(F32)
    beta_own = cat[:, 4 * span : 4 * span + own_heads]
    bias_own = lax.dynamic_slice_in_dim(b_beta, my_hid * own_heads, own_heads, 0).astype(F32)

    pieces = line_pieces(line, "hid")
    pieces, ff, wout, out_grad = together(pieces, ff, wout, out_grad)
    ff = lax.all_gather(jnp.stack(ff, axis=0), "hid", axis=0, tiled=False)
    wout = gather_near(jnp.stack(wout, axis=0), "dp")
    grad_b = out_grad.reshape(row_count * tok, width)
    grad_near = gather_near(grad_b, "dp")

    scaled = jnp.zeros((n_hid, held, width), BF16)
    act_one = jnp.zeros((n_hid, held, width), BF16)
    for index, piece in pieces:
        unit = norm_in(piece.astype(F32), 1.0)
        scaled = place(scaled, unit.astype(BF16), index)
        act_one = place(act_one, (unit * gain_one).astype(BF16), index)
    act_one = act_one.reshape(n_hid * held, width)
    scaled = scaled.reshape(n_hid * held, width)
    if n_wid == 2:
        segs = jnp.concatenate(by_source(exchange([to_row(segment_ids)] * n_hid, "hid"), "hid"), axis=0)
    else:
        segs = lax.all_gather(segment_ids, ("hid", "wid"), axis=0, tiled=False)
        segs = pick(segs, lax.axis_index("wid") // copies, 1).reshape(-1)

    query = mm(act_one, cat[:, :span]).astype(BF16)
    key = mm(act_one, cat[:, span : 2 * span]).astype(BF16)
    value = mm(act_one, cat[:, 2 * span : 3 * span]).astype(BF16)
    raw = mm(act_one, cat[:, 3 * span : 4 * span])
    logits = mm(act_one, beta_own) + bias_own
    logits = logits.reshape(-1, tok, own_heads).transpose(0, 2, 1)
    local = attention_local(query, key, raw, logits, tok)
    local, wout, grad_near = together(local, wout, grad_near)
    wout = gather_far(wout, "dp")
    grad_far = gather_far(grad_near, "dp")
    att, saved = attention_cross(query, key, value, raw, logits, segs, local, tok)
    att, wout, grad_far = together(att, wout, grad_far)

    att = exchange([att[j * held : (j + 1) * held] for j in range(n_hid)], "hid")
    ff_own, ff_other = ff[:, None], jnp.moveaxis(from_cores(ff), 0, 1)
    wout = gather_end(wout, "dp")
    wout_full = gathered_rows(wout[None], from_cores(wout))
    grad_all = gather_end(grad_far, "dp").reshape(-1, width)
    att = from_row(jnp.concatenate(by_source(att, "hid"), axis=1), row_count)
    att = att.reshape(row_count * tok, width)

    layer_f = layer_in.astype(F32).reshape(row_count * tok, width)
    middle = layer_f + mm(att, wout_full)
    act_two = norm_in(middle, gain_two).astype(BF16)
    act_all = square_gather(act_two, "dp").reshape(-1, width)
    mlp, d_act, hidden, d_gate, d_up = feed_forward(act_all, grad_all, ff_own, ff_other)
    d_act = sum_near(sum_far(d_act.reshape(n_dp, -1, width), "dp"), "dp")
    hidden, d_gate, d_up, mine = together(hidden, d_gate, d_up, d_act[0])
    g_own, g_other = feed_forward_weights(act_all, grad_all, hidden, d_gate, d_up, ff_own, ff_other)
    near, g_own, g_other = together(d_act[1:], g_own, g_other)
    d_act = add(mine, *near)

    _, pull_two = jax.vjp(norm_in, middle, gain_two)
    d_mid_norm, _ = pull_two(d_act.astype(F32))
    d_middle = grad_b.astype(F32) + d_mid_norm
    d_branch = d_middle.astype(BF16)
    d_att = mm(d_branch, wout_full, NT).astype(BF16).reshape(row_count, tok, width)
    d_att = to_row(d_att)
    ff_grads = core_sum(jnp.moveaxis(g_own, 1, 0), jnp.moveaxis(g_other, 1, 0))[0]
    d_att, ff_grads, att, mlp = together(d_att, ff_grads, att, mlp)
    d_att = exchange([d_att[:, j * span : (j + 1) * span] for j in range(n_hid)], "hid")
    ff_grads = lax.psum_scatter(ff_grads, "hid", scatter_dimension=0, tiled=False)
    mlp = sum_far(mlp.reshape(n_dp, -1, width), "dp")
    no_side = jnp.zeros((width, side), F32)
    wout_rows = row_gradients(att, d_branch, no_side, n_dp, n_hid, n_wid)
    d_att, wout_rows = together(d_att, wout_rows)
    d_att = jnp.concatenate(by_source(d_att, "hid"), axis=0)
    wout_grad = sum_far(core_sum(*wout_rows)[0], "dp")

    crossed = attention_backward_cross(saved, d_att, tok)
    crossed, wout_grad, mlp = together(crossed, wout_grad, mlp)
    wout_grad = sum_near(wout_grad, "dp")
    mlp = sum_near(mlp, "dp")
    dv, *crossed = crossed
    dq, dk, draw, dlogit = attention_backward_local(saved, crossed, tok)
    dq, dk, draw, dlogit, mlp, wout_grad = together(dq, dk, draw, dlogit, mlp, wout_grad)
    layer_out = (middle + add(*mlp).astype(F32)).astype(BF16)
    d_logit = dlogit.transpose(0, 2, 1).reshape(-1, own_heads).astype(BF16)
    d_cat = jnp.concatenate(
        [dq, dk, dv, draw, jnp.pad(d_logit, ((0, 0), (0, side - own_heads)))], axis=1)
    lanes = lax.broadcasted_iota(jnp.int32, (1, side), 1)
    d_act_one = mm(d_cat, cat, NT)
    d_act_one, ff_grads = together(d_act_one.astype(BF16), ff_grads)
    wout_grad = add(*wout_grad)
    wout_got = exchange([wout_grad[j] for j in range(n_hid)], "hid")
    ff_got = [ff_grads[0]]
    for r in range(1, n_dp):
        ff_got.append(lax.ppermute(ff_grads[r], "dp", pairs(n_dp, r)))
    d_sum = d_act_one.reshape(n_hid, held, width)
    received = sum_send(d_sum, (), 1, "hid")

    ones = lambda rows, lane: jnp.broadcast_to(jnp.where(lanes == lane, 1.0, 0.0).astype(BF16), (rows, side))
    in_row = (d_act_one.astype(F32) * scaled.astype(F32)).astype(BF16)
    in_own = (d_act.astype(F32) * norm_in(middle, 1.0)).astype(BF16)
    bias_grad = jnp.sum(d_logit.astype(F32), axis=0)
    row_of = lax.broadcasted_iota(jnp.int32, (width, side), 0) % shard
    beside = mm(in_row, ones(in_row.shape[0], own_heads), TN)
    for n in range(own_heads):
        beside = beside + jnp.where((row_of == n) & (lanes == own_heads + 2), bias_grad[n], 0.0)
    if copies > 1:
        first = lax.axis_index("wid") % copies == 0
        d_cat, beside = jnp.where(first, d_cat, 0), jnp.where(first, beside, 0.0)
    beside = beside + mm(in_own, ones(in_own.shape[0], own_heads + 1), TN)
    cat_grad = row_gradients(act_one, d_cat, beside, n_dp, n_hid, n_wid)
    received, cat_grad = together(received, cat_grad)
    for t in range(2, n_hid):
        received = sum_send(d_sum, received, t, "hid")
        if t == 2:
            cat_grad = sum_far(core_sum(*cat_grad)[0], "dp")
            received, cat_grad = together(received, cat_grad)
    cat_grad = sum_near(cat_grad, "dp")
    d_sum = add(pick(d_sum, my_hid), *received)
    d_sum, wout_got, ff_got, cat_grad = together(d_sum, wout_got, ff_got, cat_grad)
    cat_grad = add(*cat_grad)
    cat_grad = by_source(exchange([cat_grad[j] for j in range(n_hid)], "hid"), "hid")
    d_sum = from_row(d_sum, row_count).reshape(row_count * tok, width).astype(F32)
    grad_wout = sum(x.astype(F32) for x in wout_got)
    ff_grads = jnp.concatenate([choose(ff_got, my_dp ^ j) for j in range(n_dp)], axis=2).astype(F32)
    weight_grads = [
        jnp.concatenate([x[:, i * span : (i + 1) * span] for x in cat_grad], axis=1).astype(F32)
        for i in range(4)]
    tails = [x[:, 4 * span :].astype(F32) for x in cat_grad]
    grad_beta = jnp.concatenate([x[:, :own_heads] for x in tails], axis=1)
    gain_grads = sum(x[:, own_heads : own_heads + 2] for x in tails)
    grad_bias = jnp.concatenate([x[:own_heads, own_heads + 2] for x in tails], axis=0)

    _, pull_one = jax.vjp(lambda t: norm_in(t, gain_one), layer_f)
    grad_in = (d_middle + pull_one(d_sum)[0]).astype(BF16)

    return (
        layer_out.reshape(layer_in.shape), grad_in.reshape(layer_in.shape), gain_grads[:, 0],
        *weight_grads, grad_beta, grad_bias,
        grad_wout, gain_grads[:, 1], ff_grads[0], ff_grads[1], ff_grads[2].T,
    )


def solution(mesh):
    in_specs = (
        P("dp", ("hid", "wid"), None),
        P("dp", ("hid", "wid")),
        P("dp", ("hid", "wid"), None),
        P(("dp", "hid", "wid")),
        P(("dp", "hid", "wid"), None),
        P(("dp", "hid", "wid"), None),
        P(("dp", "hid", "wid"), None),
        P(("dp", "hid", "wid"), None),
        P(("dp", "hid", "wid"), None),
        P(),
        P(("dp", "hid", "wid"), None),
        P(("dp", "hid", "wid")),
        P(("dp", "wid"), "hid"),
        P(("dp", "wid"), "hid"),
        P("hid", ("dp", "wid")),
    )
    out_specs = (
        P("dp", ("hid", "wid"), None),
        P("dp", ("hid", "wid"), None),
        P(("dp", "hid", "wid")),
        P(("dp", "hid", "wid"), None),
        P(("dp", "hid", "wid"), None),
        P(("dp", "hid", "wid"), None),
        P(("dp", "hid", "wid"), None),
        P(("dp", "hid", "wid"), None),
        P(),
        P(("dp", "hid", "wid"), None),
        P(("dp", "hid", "wid")),
        P(("dp", "wid"), "hid"),
        P(("dp", "wid"), "hid"),
        P("hid", ("dp", "wid")),
    )
    return jax.shard_map(
        per_device, mesh=mesh, in_specs=in_specs, out_specs=out_specs, check_vma=False
    )
```

```python
import functools
import math

import jax
import jax.numpy as jnp
from jax import lax
from jax.experimental import pallas as pl
from jax.experimental.pallas import tpu as pltpu
from jax.sharding import PartitionSpec as P

EPS = 1e-06
NEG = -1e30
F32 = jnp.float32
BF16 = jnp.bfloat16
NN = ((1,), (0,))
NT = ((1,), (1,))
TN = ((0,), (0,))
VMEM_BYTES = 56 * 1024 * 1024
SOME = 2


def mm(left, right, dims=NN):
    return lax.dot_general(left, right, (dims, ((), ())), preferred_element_type=F32)


def halves(x):
    if x.dtype == BF16:
        return (x,)
    top = x.astype(BF16)
    return (top, (x - top.astype(F32)).astype(BF16))


def dot(left, right, dims):
    picked = [(a, b) for a in range(len(left)) for b in range(len(right)) if a + b < 2]
    if len(picked) == 1:
        return mm(left[0], right[0], dims)
    x = jnp.concatenate([left[a] for a, _ in picked], axis=dims[0][0])
    y = jnp.concatenate([right[b] for _, b in picked], axis=dims[1][0])
    return mm(x, y, dims)


def iotas(size):
    rows = lax.broadcasted_iota(jnp.int32, (size, size), 0)
    cols = lax.broadcasted_iota(jnp.int32, (size, size), 1)
    return rows, cols


def unit_dirs(raw):
    inv = lax.rsqrt(jnp.sum(raw * raw, axis=-1, keepdims=True) + EPS)
    return raw * inv, inv


def local_forward(heads, size, q_ref, k_ref, raw_ref, logit_ref, qin_ref, kout_ref, ptop_ref, plow_ref,
                  intra_ref, t_ref, e_ref, cm_ref, s_ref):
    width = q_ref.shape[1] // heads
    rows, cols = iotas(size)
    strict, lower, diag = rows > cols, rows >= cols, rows == cols
    apart = rows ^ cols
    some = range(q_ref.shape[0] // size)
    at = [(slice(n * size, (n + 1) * size), slice(h * width, (h + 1) * width)) for n in some for h in range(heads)]
    wide = [(slice(n * width, (n + 1) * width), slice(h * width, (h + 1) * width)) for n in some for h in range(heads)]
    every = range(len(at))
    betas = [2.0 * jax.nn.sigmoid(logit_ref[n, h : h + 1, :]) for n in some for h in range(heads)]
    q, k = [q_ref[a] for a in at], [k_ref[a] for a in at]
    ws = [halves(unit_dirs(raw_ref[a])[0]) for a in at]
    gram = [jnp.where(strict, dot(w, w, NT), 0.0) for w in ws]
    beta = [jnp.where(diag, b, 0.0) for b in betas]
    beta_col = [jnp.sum(b, axis=1, keepdims=True) for b in beta]
    t = [beta[u] - jnp.where(apart == 1, beta_col[u] * gram[u] * betas[u], 0.0) for u in every]
    shift = 1
    while (1 << shift) < size:
        near = (apart >> shift) == 1
        part = [halves(jnp.where(near, g, 0.0)) for g in gram]
        ts = [halves(x) for x in t]
        once = [dot(ts[u], part[u], NN) for u in every]
        t = [t[u] - dot(halves(once[u]), ts[u], NN) for u in every]
        shift += 1
    ts = [halves(x) for x in t]
    bs = [halves(jnp.where(lower, dot((q[u],), ws[u], NT), 0.0)) for u in every]
    ms = [halves(jnp.where(strict, dot(ws[u], (k[u],), NT), 0.0)) for u in every]
    e = [dot(ts[u], ms[u], NN) for u in every]
    s = [dot(ts[u], ws[u], NN) for u in every]
    cm = [dot(bs[u], ts[u], NN) for u in every]
    es = [halves(x) for x in e]
    for u in every:
        t_ref[at[u]], e_ref[at[u]], cm_ref[at[u]], s_ref[at[u]] = t[u], e[u], cm[u], s[u]
        intra_ref[at[u]] = dot((q[u],), (k[u],), NT) - dot(bs[u], es[u], NN)
        qin_ref[at[u]] = (q[u].astype(F32) - dot(halves(cm[u]), ws[u], NN)).astype(BF16)
        kout_ref[at[u]] = (k[u].astype(F32) - dot(es[u], ws[u], TN)).astype(BF16)
        step = jnp.where(diag, 1.0, 0.0) - dot(ws[u], halves(s[u]), TN)
        ptop_ref[wide[u]], plow_ref[wide[u]] = halves(step)


def cross_forward(heads, group, scale, qin_ref, kout_ref, ptop_ref, plow_ref, intra_ref, v_ref,
                  segc_ref, segr_ref, out_ref, prob_ref, keep_ref, frame, score):
    size = qin_ref.shape[0]
    width = qin_ref.shape[1] // heads
    total = v_ref.shape[0]
    wide = group * size
    c = pl.program_id(0)
    parts = [slice(g * wide, (g + 1) * wide) for g in range(total // wide)]
    at = [slice(h * width, (h + 1) * width) for h in range(heads)]
    every = range(heads)

    @pl.when(c == 0)
    def _():
        frame[...] = jnp.zeros_like(frame)
        score[...] = jnp.full_like(score, NEG)

    rows, cols = iotas(size)
    own = pl.multiple_of(c * size, size)
    seg = segc_ref[...]
    for g, part in enumerate(parts):

        @pl.when(g * group < c)
        def _():
            raw = [mm(qin_ref[:, at[h]], frame[h, part, :], NT) for h in every]
            place = lax.broadcasted_iota(jnp.int32, (size, wide), 1) + g * wide
            permit = (place < own) & (seg == segr_ref[:, part])
            for h in every:
                score[h, :, part] = jnp.where(permit, scale * raw[h], NEG)

    permit = (rows >= cols) & (seg == segr_ref[:, pl.ds(own, size)])
    for h in every:
        score[h, :, pl.ds(own, size)] = jnp.where(permit, scale * intra_ref[:, at[h]], NEG)
    top = [jnp.max(score[h], axis=-1, keepdims=True) for h in every]
    e = [jnp.exp(score[h] - top[h]) for h in every]
    inv = [1.0 / jnp.sum(x, axis=-1, keepdims=True) for x in e]
    for h in every:
        prob_ref[0, h] = (e[h] * inv[h]).astype(BF16)
    for h in every:
        out_ref[:, at[h]] = mm(prob_ref[0, h], v_ref[:, at[h]]).astype(BF16)
        keep_ref[0, h] = frame[h]
    for g, part in enumerate(parts):

        @pl.when(g * group < c)
        def _():
            moved = [dot((frame[h, part, :],), (ptop_ref[:, at[h]], plow_ref[:, at[h]]), NT) for h in every]
            for h in every:
                frame[h, part, :] = moved[h].astype(BF16)

    for h in every:
        frame[h, pl.ds(own, size), :] = kout_ref[:, at[h]]


def cross_backward(heads, group, scale, grad_ref, v_ref, prob_ref, keep_ref, qin_ref, ptop_ref,
                   plow_ref, dqin_ref, dintra_ref, dkout_ref, dstep_ref, dv_ref, carry, dvals, ds_ref):
    size = grad_ref.shape[0]
    width = grad_ref.shape[1] // heads
    total = v_ref.shape[0]
    wide = group * size
    c = pl.num_programs(0) - 1 - pl.program_id(0)
    parts = [slice(g * wide, (g + 1) * wide) for g in range(total // wide)]
    at = [slice(h * width, (h + 1) * width) for h in range(heads)]
    every = range(heads)

    @pl.when(pl.program_id(0) == 0)
    def _():
        carry[...] = jnp.zeros_like(carry)
        dvals[...] = jnp.zeros_like(dvals)

    own = pl.multiple_of(c * size, size)
    dp = [mm(grad_ref[:, at[h]], v_ref[:, at[h]], NT) for h in every]
    pf = [prob_ref[0, h].astype(F32) for h in every]
    delta = [jnp.sum(pf[h] * dp[h], axis=-1, keepdims=True) for h in every]
    for h in every:
        ds_ref[h] = (pf[h] * (dp[h] - delta[h])).astype(BF16)
    low = [carry[h].astype(BF16) for h in every]
    dqin = [mm(ds_ref[h], keep_ref[0, h]) for h in every]
    dstep = [mm(low[h], keep_ref[0, h], TN) for h in every]
    for h in every:
        dqin_ref[:, at[h]] = scale * dqin[h]
        dstep_ref[:, at[h]] = dstep[h]
        dintra_ref[:, at[h]] = ds_ref[h, :, pl.ds(own, size)]
        dkout_ref[:, at[h]] = carry[h, pl.ds(own, size), :]
    for g, part in enumerate(parts):

        @pl.when(g * group <= c)
        def _():
            more = [mm(prob_ref[0, h, :, part], grad_ref[:, at[h]], TN) for h in every]
            for h in every:
                dvals[h, part, :] += more[h]

        @pl.when(g * group < c)
        def _():
            fresh = [mm(ds_ref[h, :, part], qin_ref[:, at[h]], TN) for h in every]
            moved = [dot((carry[h, part, :].astype(BF16),), (ptop_ref[:, at[h]], plow_ref[:, at[h]]), NN)
                     for h in every]
            for h in every:
                carry[h, part, :] = scale * fresh[h] + moved[h]

    @pl.when(c == 0)
    def _():
        for h in every:
            dv_ref[:, at[h]] = dvals[h].astype(BF16)


def local_backward(heads, size, scale, q_ref, k_ref, raw_ref, logit_ref, t_ref, e_ref, cm_ref, s_ref,
                   dqin_ref, dintra_ref, dkout_ref, dstep_ref, dq_ref, dk_ref, draw_ref, dlogit_ref):
    width = q_ref.shape[1] // heads
    rows, cols = iotas(size)
    strict, lower, diag = rows > cols, rows >= cols, rows == cols
    some = range(q_ref.shape[0] // size)
    units = [(n, h) for n in some for h in range(heads)]
    at = [(slice(n * size, (n + 1) * size), slice(h * width, (h + 1) * width)) for n, h in units]
    wide = [(slice(n * width, (n + 1) * width), slice(h * width, (h + 1) * width)) for n, h in units]
    every = range(len(units))
    q, k = [(q_ref[a],) for a in at], [(k_ref[a],) for a in at]
    both = [unit_dirs(raw_ref[a]) for a in at]
    betas = [2.0 * jax.nn.sigmoid(logit_ref[n, h : h + 1, :]) for n, h in units]
    ws = [halves(w) for w, _ in both]
    ts, es, cms, ss = ([halves(ref[a]) for a in at] for ref in (t_ref, e_ref, cm_ref, s_ref))
    dintra = [(dintra_ref[a],) for a in at]
    dqs, dks = [halves(dqin_ref[a]) for a in at], [halves(dkout_ref[a]) for a in at]
    dps = [halves(dstep_ref[a]) for a in wide]
    b = [halves(jnp.where(lower, dot(q[u], ws[u], NT), 0.0)) for u in every]
    d_s = [halves(-dot(ws[u], dps[u], NN)) for u in every]
    d_e = [halves(-(dot(ws[u], dks[u], NT) + scale * dot(b[u], dintra[u], TN))) for u in every]
    d_cm = [halves(-dot(dqs[u], ws[u], NT)) for u in every]
    y_s = [dot(ts[u], d_s[u], TN) for u in every]
    y_e = [dot(ts[u], d_e[u], TN) for u in every]
    y_c = [dot(d_cm[u], ts[u], NT) for u in every]
    d_x = [-(dot(halves(y_s[u]), ss[u], NT) + dot(halves(y_e[u]), es[u], NT) + dot(cms[u], halves(y_c[u]), TN))
           for u in every]
    d_b = [halves(jnp.where(lower, y_c[u] - scale * dot(dintra[u], es[u], NT), 0.0)) for u in every]
    d_m = [halves(jnp.where(strict, y_e[u], 0.0)) for u in every]
    d_a = [halves(jnp.where(strict, d_x[u], 0.0)) for u in every]
    for u in every:
        a = at[u]
        dq_ref[a] = (dqin_ref[a] + scale * dot(dintra[u], k[u], NN) + dot(d_b[u], ws[u], NN)).astype(BF16)
        dk_ref[a] = (dkout_ref[a] + scale * dot(dintra[u], q[u], TN) + dot(d_m[u], ws[u], TN)).astype(BF16)
    d_w = [y_s[u] - dot(ss[u], dps[u], NT) - dot(es[u], dks[u], NN) - dot(cms[u], dqs[u], TN)
           + dot(d_b[u], q[u], TN) + dot(d_m[u], k[u], NN) + dot(d_a[u], ws[u], NN) + dot(d_a[u], ws[u], TN)
           for u in every]
    for u, (n, h) in enumerate(units):
        raw, inv = raw_ref[at[u]], both[u][1]
        draw = inv * d_w[u] - raw * (inv * inv * inv) * jnp.sum(raw * d_w[u], axis=-1, keepdims=True)
        draw_ref[at[u]] = draw.astype(BF16)
        at_diag = jnp.sum(jnp.where(diag, d_x[u], 0.0), axis=0, keepdims=True)
        dlogit_ref[n, h : h + 1, :] = -at_diag * (1.0 - 0.5 * betas[u]) / betas[u]


def run(body, grid, inputs, in_specs, outputs, out_specs, scratch, flops):
    return pl.pallas_call(
        body, grid=(grid,), in_specs=in_specs, out_specs=out_specs, out_shape=outputs,
        scratch_shapes=scratch,
        compiler_params=pltpu.CompilerParams(
            dimension_semantics=("arbitrary",), vmem_limit_bytes=VMEM_BYTES),
        cost_estimate=pl.CostEstimate(
            flops=flops, transcendentals=0,
            bytes_accessed=sum(x.size * x.dtype.itemsize for x in (*inputs, *outputs))),
    )(*inputs)


def shape(dims, dtype):
    return jax.ShapeDtypeStruct(dims, dtype)


def group_of(blocks):
    return 4 if blocks % 4 == 0 else 1


def attention_local(q, k, raw, logits, size):
    tokens, width = q.shape
    blocks, heads, _ = logits.shape
    head = width // heads
    some = SOME if blocks % SOME == 0 else 1
    block = pl.BlockSpec((some * size, width), lambda c: (c, 0))
    square = pl.BlockSpec((some * head, width), lambda c: (c, 0))
    logit_block = pl.BlockSpec((some, heads, size), lambda c: (c, 0, 0))
    f, b = shape((tokens, width), F32), shape((tokens, width), BF16)
    stepped = shape((blocks * head, width), BF16)
    return run(
        functools.partial(local_forward, heads, size), blocks // some, (q, k, raw, logits),
        [block, block, block, logit_block], (b, b, stepped, stepped, f, f, f, f, f),
        [block, block, square, square, block, block, block, block, block], [],
        blocks * heads * 62 * 2 * size * size * head)


def attention_cross(q, k, v, raw, logits, segments, local, size):
    qin, kout, ptop, plow, intra, t, e, cm, s = local
    tokens, width = q.shape
    blocks, heads, _ = logits.shape
    head = width // heads
    block = pl.BlockSpec((size, width), lambda c: (c, 0))
    square = pl.BlockSpec((head, width), lambda c: (c, 0))
    b = shape((tokens, width), BF16)
    group = group_of(blocks)
    whole = pl.BlockSpec((tokens, width), lambda c: (0, 0))
    wide_prob = pl.BlockSpec((1, heads, size, tokens), lambda c: (c, 0, 0, 0))
    wide_keep = pl.BlockSpec((1, heads, tokens, head), lambda c: (c, 0, 0, 0))
    out, prob, keep = run(
        functools.partial(cross_forward, heads, group, 1.0 / math.sqrt(head)), blocks,
        (qin, kout, ptop, plow, intra, v, segments.reshape(tokens, 1), segments.reshape(1, tokens)),
        [block, block, square, square, block, whole,
         pl.BlockSpec((size, 1), lambda c: (c, 0)), pl.BlockSpec((1, tokens), lambda c: (0, 0))],
        (b, shape((blocks, heads, size, tokens), BF16), shape((blocks, heads, tokens, head), BF16)),
        [block, wide_prob, wide_keep],
        [pltpu.VMEM((heads, tokens, head), BF16), pltpu.VMEM((heads, size, tokens), F32)],
        blocks * heads * 4 * 2 * size * tokens * head)
    return out, (q, k, v, raw, logits, qin, ptop, plow, t, e, cm, s, prob, keep)


def attention_backward_cross(saved, grad, size):
    q, k, v, raw, logits, qin, ptop, plow, t, e, cm, s, prob, keep = saved
    tokens, width = q.shape
    blocks, heads, _ = logits.shape
    head = width // heads
    scale = 1.0 / math.sqrt(head)
    back = lambda c: (blocks - 1 - c, 0)
    block = pl.BlockSpec((size, width), back)
    square = pl.BlockSpec((head, width), back)
    whole = pl.BlockSpec((tokens, width), lambda c: (0, 0))
    wide_prob = pl.BlockSpec((1, heads, size, tokens), lambda c: (blocks - 1 - c, 0, 0, 0))
    wide_keep = pl.BlockSpec((1, heads, tokens, head), lambda c: (blocks - 1 - c, 0, 0, 0))
    f, b = shape((tokens, width), F32), shape((tokens, width), BF16)
    dqin, dintra, dkout, dstep, dv = run(
        functools.partial(cross_backward, heads, group_of(blocks), scale), blocks,
        (grad, v, prob, keep, qin, ptop, plow),
        [block, whole, wide_prob, wide_keep, block, square, square],
        (f, b, f, shape((blocks * head, width), F32), b),
        [block, block, block, square, whole],
        [pltpu.VMEM((heads, tokens, head), F32), pltpu.VMEM((heads, tokens, head), F32),
         pltpu.VMEM((heads, size, tokens), BF16)],
        blocks * heads * 7 * 2 * size * tokens * head)
    return dv, dqin, dintra, dkout, dstep


def attention_backward_local(saved, crossed, size):
    q, k, v, raw, logits, qin, ptop, plow, t, e, cm, s, prob, keep = saved
    tokens, width = q.shape
    blocks, heads, _ = logits.shape
    head = width // heads
    scale = 1.0 / math.sqrt(head)
    some = SOME if blocks % SOME == 0 else 1
    b = shape((tokens, width), BF16)
    block = pl.BlockSpec((some * size, width), lambda c: (c, 0))
    square = pl.BlockSpec((some * head, width), lambda c: (c, 0))
    logit_block = pl.BlockSpec((some, heads, size), lambda c: (c, 0, 0))
    return run(
        functools.partial(local_backward, heads, size, scale), blocks // some,
        (q, k, raw, logits, t, e, cm, s, *crossed),
        [block, block, block, logit_block, block, block, block, block, block, block, block, square],
        (b, b, b, shape((blocks, heads, size), F32)), [block, block, block, logit_block], [],
        blocks * heads * 60 * 2 * size * size * head)


def ff_forward(me_ref, act_ref, grad_ref, own_ref, other_ref, mlp_ref, dact_ref, hid_ref, dgate_ref, dup_ref,
               gate_w, up_w, down_w, mlp, dact):
    tokens = act_ref.shape[0]
    cores, chips, rows = own_ref.shape[1] + other_ref.shape[1], own_ref.shape[2], own_ref.shape[4]
    tile = min(tokens, 256)

    for r in range(chips):
        for n in range(cores):
            held = own_ref.at[0, 0, r] if n == 0 else other_ref.at[0, n - 1, r]
            chip, core = me_ref[0] ^ r, me_ref[1] ^ n
            to = pl.ds(pl.multiple_of((chip * cores + core) * rows, rows), rows)
            gate_w[to, :] = held[0]
            up_w[to, :] = held[1]
            down_w[to, :] = held[2]

    @pl.when(pl.program_id(0) == 0)
    def _():
        mlp[...] = jnp.zeros_like(mlp)
        dact[...] = jnp.zeros_like(dact)

    @pl.loop(0, tokens // tile)
    def _(i):
        at = pl.ds(pl.multiple_of(i * tile, tile), tile)
        act, grad = act_ref[at, :], grad_ref[at, :]
        gate, up = mm(act, gate_w[...]), mm(act, up_w[...])
        sig = jax.nn.sigmoid(gate)
        silu = gate * sig
        hidden = (silu * up).astype(BF16)
        d_hidden = mm(grad, down_w[...])
        d_gate = (d_hidden * up * sig * (1.0 + gate * (1.0 - sig))).astype(BF16)
        d_up = (d_hidden * silu).astype(BF16)
        hid_ref[at, :] = hidden
        dgate_ref[at, :] = d_gate
        dup_ref[at, :] = d_up
        mlp[at, :] += mm(hidden, down_w[...], NT)
        dact[at, :] += mm(d_gate, gate_w[...], NT) + mm(d_up, up_w[...], NT)

    @pl.when(pl.program_id(0) == pl.num_programs(0) - 1)
    def _():
        mlp_ref[...] = mlp[...].astype(BF16)
        dact_ref[...] = dact[...].astype(BF16)


def ff_weights(me_ref, act_ref, grad_ref, hid_ref, dgate_ref, dup_ref, own_ref, other_ref):
    cores, chips, rows = own_ref.shape[1] + other_ref.shape[1], own_ref.shape[2], own_ref.shape[4]
    for d in range(chips):
        at = slice(d * cores * rows, (d + 1) * cores * rows)
        act, grad = act_ref[:, at], grad_ref[:, at]
        r = me_ref[0] ^ d
        for i, part in enumerate((mm(act, dgate_ref[...], TN), mm(act, dup_ref[...], TN),
                                  mm(grad, hid_ref[...], TN))):
            pieces = [part[w * rows : (w + 1) * rows, :].astype(BF16) for w in range(cores)]
            for n in range(cores):
                piece = pieces[0]
                for w in range(1, cores):
                    piece = jnp.where((me_ref[1] ^ n) == w, pieces[w], piece)
                if n == 0:
                    own_ref[0, 0, r, i] = piece
                else:
                    other_ref[0, n - 1, r, i] = piece


def place_self():
    return jnp.stack([lax.axis_index("dp"), lax.axis_index("wid")]).astype(jnp.int32)


SCALARS = pl.BlockSpec(memory_space=pltpu.SMEM)


def feed_forward(act, grad, own, other):
    tokens, width = act.shape
    groups, part = own.shape[0], own.shape[5]
    whole = pl.BlockSpec((tokens, width), lambda h: (0, 0))
    units = pl.BlockSpec((tokens, part), lambda h: (0, h))
    held = [pl.BlockSpec((1,) + x.shape[1:], lambda h: (h, 0, 0, 0, 0, 0)) for x in (own, other)]
    full, some = shape((tokens, width), BF16), shape((tokens, groups * part), BF16)
    flops = 6 * 2 * tokens * width * groups * part
    return run(ff_forward, groups, (place_self(), act, grad, own, other), [SCALARS, whole, whole, *held],
               (full, full, some, some, some), [whole, whole, units, units, units],
               [pltpu.VMEM((width, part), BF16)] * 3 + [pltpu.VMEM((tokens, width), F32)] * 2, flops)


def feed_forward_weights(act, grad, hidden, d_gate, d_up, own, other):
    tokens, width = act.shape
    groups, part = own.shape[0], own.shape[5]
    whole = pl.BlockSpec((tokens, width), lambda h: (0, 0))
    units = pl.BlockSpec((tokens, part), lambda h: (0, h))
    held = [pl.BlockSpec((1,) + x.shape[1:], lambda h: (h, 0, 0, 0, 0, 0)) for x in (own, other)]
    return run(ff_weights, groups, (place_self(), act, grad, hidden, d_gate, d_up),
               [SCALARS, whole, whole, units, units, units],
               (shape(own.shape, BF16), shape(other.shape, BF16)), held, [],
               3 * 2 * tokens * width * groups * part)


def split_rows(me_ref, part, at, own_ref, other_ref):
    cores, shards, rows = own_ref.shape[0] + other_ref.shape[0], own_ref.shape[2], own_ref.shape[3]
    for h in range(shards):
        pieces = [part[(h * cores + w) * rows : (h * cores + w + 1) * rows, :] for w in range(cores)]
        for n in range(cores):
            piece = pieces[0]
            for w in range(1, cores):
                piece = jnp.where((me_ref[1] ^ n) == w, pieces[w], piece)
            if n == 0:
                own_ref[0, 0, h, :, at] = piece
            else:
                other_ref[n - 1, 0, h, :, at] = piece


def row_grads(me_ref, left_ref, right_ref, own_ref, other_ref):
    columns = right_ref.shape[1]
    for start in range(0, columns, 512):
        at = slice(start, min(start + 512, columns))
        split_rows(me_ref, mm(left_ref[...], right_ref[:, at], TN).astype(BF16), at, own_ref, other_ref)


def split_whole(full, chips, shards, cores, rows):
    full = full.astype(BF16).reshape(chips, shards, cores, rows, full.shape[1])
    full = jnp.take(full, lax.axis_index("wid") ^ jnp.arange(cores), axis=2).transpose(2, 0, 1, 3, 4)
    return full[:1], full[1:]


def row_gradients(left, right, chips, shards, cores):
    tokens, width = left.shape
    columns = right.shape[1]
    rows = width // (chips * shards * cores)
    if rows % 16:
        return split_whole(mm(left, right, TN), chips, shards, cores, rows)
    outs = [shape((n, chips, shards, rows, columns), BF16) for n in (1, cores - 1)]
    specs = [pl.BlockSpec((x.shape[0], 1, shards, rows, columns), lambda d: (0, d, 0, 0, 0)) for x in outs]
    return run(row_grads, chips, (place_self(), left, right),
               [SCALARS, pl.BlockSpec((tokens, width // chips), lambda d: (0, d)),
                pl.BlockSpec((tokens, columns), lambda d: (0, 0))],
               tuple(outs), specs, [], 2 * tokens * width * columns)


def input_grads(me_ref, bias_ref, left_ref, right_ref, w_ref, two_ref, din_ref, own_ref, other_ref):
    columns, side = right_ref.shape[1], 128
    heads, rows = bias_ref.shape[0], own_ref.shape[3]
    din_ref[...] = mm(right_ref[...], w_ref[...], NT).astype(BF16)
    spans = [(start, min(start + 512, columns - side)) for start in range(0, columns - side, 512)]
    gain_sum = jnp.zeros((left_ref.shape[1], 1), F32)
    for start, stop in spans + [(columns - side, columns)]:
        part = mm(left_ref[...], right_ref[:, start:stop], TN)
        weight = w_ref[:, start:stop].astype(F32)
        lane = lax.broadcasted_iota(jnp.int32, part.shape, 1)
        if stop == columns:
            gain_sum = gain_sum + jnp.sum(jnp.where(lane < heads, part * weight, 0.0), axis=1, keepdims=True)
            gain = jnp.sum(jnp.where(lane == heads, weight, 0.0), axis=1, keepdims=True)
            row = lax.rem(lax.broadcasted_iota(jnp.int32, part.shape, 0), rows)
            two = jnp.transpose(jnp.broadcast_to(two_ref[...], (side, part.shape[0])))
            part = jnp.where(lane < heads, part, 0.0) + jnp.where(lane == heads, gain_sum / gain, 0.0)
            for n in range(heads):
                part = part + jnp.where((lane == heads + 2) & (row == n), bias_ref[n], 0.0)
            part = jnp.where(me_ref[2] == 1, part, 0.0) + jnp.where(lane == heads + 1, two, 0.0)
        else:
            gain_sum = gain_sum + jnp.sum(part * weight, axis=1, keepdims=True)
            part = jnp.where(me_ref[2] == 1, part, 0.0)
        split_rows(me_ref, part.astype(BF16), slice(start, stop), own_ref, other_ref)


def input_gradients(left, right, weights, two, bias, once, chips, shards, cores):
    tokens, width = left.shape
    columns, heads = right.shape[1], bias.shape[0]
    rows = width // (chips * shards * cores)
    if rows % 16:
        full = mm(left, right, TN)
        lane = lax.broadcasted_iota(jnp.int32, (width, columns), 1) - (columns - 128)
        row = lax.broadcasted_iota(jnp.int32, (width, columns), 0) % rows
        wide = weights.astype(F32)
        gain = jnp.sum(jnp.where(lane < heads, full * wide, 0.0), axis=1, keepdims=True)
        gain = gain / wide[:, columns - 128 + heads][:, None]
        full = full + jnp.where(lane == heads, gain, 0.0)
        for n in range(heads):
            full = full + jnp.where((lane == heads + 2) & (row == n), bias[n], 0.0)
        full = jnp.where(once, full, 0.0) + jnp.where(lane == heads + 1, two.T, 0.0)
        return (mm(right, weights, NT).astype(BF16), *split_whole(full, chips, shards, cores, rows))
    outs = [shape((n, chips, shards, rows, columns), BF16) for n in (1, cores - 1)]
    specs = [pl.BlockSpec((x.shape[0], 1, shards, rows, columns), lambda d: (0, d, 0, 0, 0)) for x in outs]
    features = pl.BlockSpec((tokens, width // chips), lambda d: (0, d))
    me = jnp.concatenate([place_self(), once[None].astype(jnp.int32)])
    return run(input_grads, chips, (me, bias, left, right, weights, two),
               [SCALARS, SCALARS, features, pl.BlockSpec((tokens, columns), lambda d: (0, 0)),
                pl.BlockSpec((width // chips, columns), lambda d: (d, 0)), pl.BlockSpec((1, width // chips), lambda d: (0, d))],
               (shape((tokens, width), BF16), *outs), [features, *specs], [], 4 * tokens * width * columns)


def lay_columns(me_ref, *refs):
    *got, a_ref, b_ref, c_ref, d_ref, tail_ref = refs
    count, span = len(got), a_ref.shape[1] // len(got)
    for k, ref in enumerate(got):
        source = lax.rem(me_ref[0] - k + count, count)
        to = pl.ds(pl.multiple_of(source * span, 128), span)
        for i, out in enumerate((a_ref, b_ref, c_ref, d_ref)):
            out[:, to] = ref[:, i * span : (i + 1) * span].astype(F32)
        tail_ref[source] = ref[:, 4 * span :].astype(F32)


def laid_columns(got, side):
    count, (rows, columns) = len(got), got[0].shape
    span = (columns - side) // 4
    if rows % 16 or span % 128:
        got = by_source(got, "hid")
        whole = [jnp.concatenate([x[:, i * span : (i + 1) * span] for x in got], axis=1).astype(F32) for i in range(4)]
        return (*whole, jnp.stack([x[:, 4 * span :] for x in got]).astype(F32))
    one = pl.BlockSpec((rows, columns), lambda i: (0, 0))
    out = pl.BlockSpec((rows, count * span), lambda i: (0, 0))
    return run(lay_columns, 1, (lax.axis_index("hid")[None].astype(jnp.int32), *got), [SCALARS] + [one] * count,
               (shape((rows, count * span), F32),) * 4 + (shape((count, rows, side), F32),),
               [out] * 4 + [pl.BlockSpec((count, rows, side), lambda i: (0, 0, 0))], [], 0)


def lay_ff(me_ref, *refs):
    *got, gate_ref, up_ref, down_ref = refs
    part = got[0].shape[2]
    for r, ref in enumerate(got):
        to = pl.ds(pl.multiple_of((me_ref[0] ^ r) * part, 128), part)
        gate_ref[:, to] = ref[0].astype(F32)
        up_ref[:, to] = ref[1].astype(F32)
        down_ref[to, :] = jnp.transpose(ref[2].astype(F32))


def laid_ff(got):
    count, (_, rows, part) = len(got), got[0].shape
    outs = ((rows, count * part), (rows, count * part), (count * part, rows))
    return run(lay_ff, 1, (lax.axis_index("dp")[None].astype(jnp.int32), *got),
               [SCALARS] + [pl.BlockSpec((3, rows, part), lambda i: (0, 0, 0))] * count,
               tuple(shape(x, F32) for x in outs), [pl.BlockSpec(x, lambda i: (0, 0)) for x in outs], [], 0)


def lay_rows(me_ref, own_ref, other_ref, out_ref, *turned):
    cores, shards, rows = own_ref.shape[0] + other_ref.shape[0], own_ref.shape[2], own_ref.shape[3]
    for k in range(shards):
        h = lax.rem(me_ref[2] - k + shards, shards)
        for n in range(cores):
            to = pl.ds(pl.multiple_of((h * cores + (me_ref[1] ^ n)) * rows, rows), rows)
            out_ref[to, :] = own_ref[0, 0, k] if n == 0 else other_ref[n - 1, 0, k]
    for ref in turned:
        ref[...] = jnp.transpose(out_ref[:, -ref.shape[0] :].astype(F32))


def gathered_rows(own, other, side):
    _, chips, shards, rows, columns = own.shape
    cores = 1 + other.shape[0]
    if rows % 16:
        full = jnp.concatenate([own, other], axis=0)
        full = jnp.take(full, lax.axis_index("wid") ^ jnp.arange(cores), axis=0)
        full = jnp.take(full, (lax.axis_index("hid") - jnp.arange(shards)) % shards, axis=2)
        full = full.transpose(1, 2, 0, 3, 4).reshape(-1, columns)
        return full, (full[:, columns - side :].astype(F32).T if side else None)
    me = jnp.concatenate([place_self(), lax.axis_index("hid")[None].astype(jnp.int32)])
    specs = [pl.BlockSpec((x.shape[0], 1, shards, rows, columns), lambda d: (0, d, 0, 0, 0)) for x in (own, other)]
    size = cores * shards * rows
    outs, out_specs = [shape((chips * size, columns), BF16)], [pl.BlockSpec((size, columns), lambda d: (d, 0))]
    if side:
        outs.append(shape((side, chips * size), F32))
        out_specs.append(pl.BlockSpec((side, size), lambda d: (0, d)))
    out = run(lay_rows, chips, (me, own, other), [SCALARS, *specs], tuple(outs), out_specs, [], 0)
    return out[0], (out[1] if side else None)


def project(heads, tok, bias_ref, x_ref, w_ref, gain_ref, act_ref, q_ref, k_ref, v_ref, raw_ref, logit_ref):
    x = x_ref[...].astype(F32)
    unit = x * lax.rsqrt(jnp.mean(x * x, axis=-1, keepdims=True) + EPS)
    act_ref[...] = (unit * gain_ref[...]).astype(BF16)
    act, span = act_ref[...], q_ref.shape[1]
    for i, out in enumerate((q_ref, k_ref, v_ref, raw_ref)):
        out[...] = mm(act, w_ref[:, i * span : (i + 1) * span]).astype(out.dtype)
    beside = mm(act, w_ref[:, 4 * span :])
    for n in range(beside.shape[0] // tok):
        rows = jnp.transpose(beside[n * tok : (n + 1) * tok, :])
        for h in range(heads):
            logit_ref[n, h : h + 1, :] = rows[h : h + 1, :] + bias_ref[h]


def projected(x, weights, gain, bias, heads, tok):
    tokens, width = x.shape
    span = (weights.shape[1] - 128) // 4
    blocks = tokens // tok
    some = 2 if blocks % 2 == 0 else 1
    wide, narrow = (pl.BlockSpec((some * tok, n), lambda c: (c, 0)) for n in (width, span))
    whole = lambda c: (0, 0)
    return run(
        functools.partial(project, heads, tok), blocks // some, (bias, x, weights, gain),
        [SCALARS, wide, pl.BlockSpec(weights.shape, whole), pl.BlockSpec((1, width), whole)],
        (shape((tokens, width), BF16), shape((tokens, span), BF16),
         shape((tokens, span), BF16), shape((tokens, span), BF16), shape((tokens, span), F32),
         shape((blocks, heads, tok), F32)),
        [wide, narrow, narrow, narrow, narrow, pl.BlockSpec((some, heads, tok), lambda c: (c, 0, 0))], [],
        2 * tokens * width * weights.shape[1])


def norm_in(tensor, gain_vec):
    return tensor * lax.rsqrt(jnp.mean(tensor * tensor, axis=-1, keepdims=True) + EPS) * gain_vec


def pick(x, index, axis=0):
    return lax.dynamic_index_in_dim(x, index, axis, keepdims=False)


def place(buffer, piece, index, axis=0):
    return lax.dynamic_update_index_in_dim(buffer, piece, index, axis)


def add(left, *others):
    total = left.astype(F32)
    for other in others:
        total = total + other.astype(F32)
    return total.astype(left.dtype)


def to_row(x):
    cores, rows = lax.axis_size("wid"), x.shape[0]
    me = lax.axis_index("wid")
    if cores == rows == 2:
        got = lax.ppermute(pick(x, 1 - me), "wid", [(0, 1), (1, 0)])
        mine = pick(x, me)
        return jnp.concatenate([jnp.where(me == 0, mine, got), jnp.where(me == 0, got, mine)], axis=0)
    every = pick(lax.all_gather(x, "wid", axis=0, tiled=False), me // (cores // rows), 1)
    return every.reshape((-1,) + x.shape[2:])


def from_row(x, rows):
    cores = lax.axis_size("wid")
    me = lax.axis_index("wid")
    parts = x.reshape((cores, x.shape[0] // cores) + x.shape[1:])
    if cores == rows == 2:
        got = lax.ppermute(pick(parts, 1 - me), "wid", [(0, 1), (1, 0)])
        mine = pick(parts, me)
        return jnp.stack([jnp.where(me == 0, mine, got), jnp.where(me == 0, got, mine)], axis=0)
    return lax.all_to_all(parts, "wid", 0, 0, tiled=True)[:: cores // rows]


def choose(parts, index):
    return lax.select_n(index.astype(jnp.int32), *parts)


def exchange(blocks, axis):
    count, me = lax.axis_size(axis), lax.axis_index(axis)
    got = [choose(blocks, me)]
    for k in range(1, count):
        sent = choose(blocks, lax.rem(me + k, count))
        got.append(lax.ppermute(sent, axis, [(i, (i + k) % count) for i in range(count)]))
    return got


def exchange_rows(x, axis):
    count, me = lax.axis_size(axis), lax.axis_index(axis)
    sent = together(*[pick(x, lax.rem(me + k, count)) for k in range(1, count)])
    return [pick(x, me)] + [lax.ppermute(sent[k - 1], axis, [(i, (i + k) % count) for i in range(count)])
                            for k in range(1, count)]


def by_source(got, axis):
    count, me = lax.axis_size(axis), lax.axis_index(axis)
    return [choose(got, lax.rem(me - j + count, count)) for j in range(count)]


def pairs(count, flip):
    return [(i, i ^ flip) for i in range(count)]


def gather_near(x, axis):
    if lax.axis_size(axis) != 4:
        return (x,)
    return x, lax.ppermute(x, axis, pairs(4, 1)), lax.ppermute(x, axis, pairs(4, 2))


def gather_far(near, axis):
    if len(near) == 1:
        return near
    x, one, two = near
    half = x.shape[0] // 2
    return x, one, two, lax.ppermute(one[:half], axis, pairs(4, 2)), lax.ppermute(two[half:], axis, pairs(4, 1))


def gather_end(far, axis):
    if len(far) == 1:
        return lax.all_gather(far[0], axis, axis=0, tiled=False)
    x, one, two, top, low = far
    me = lax.axis_index(axis)
    out = jnp.zeros((4,) + x.shape, x.dtype)
    out = place(place(place(out, x, me), one, me ^ 1), two, me ^ 2)
    return place(out, jnp.concatenate([top, low], axis=0), me ^ 3)


def square_gather(x, axis):
    return gather_end(gather_far(gather_near(x, axis), axis), axis)


def sum_far(x, axis):
    if lax.axis_size(axis) != 4:
        return (x,)
    half = x.shape[1] // 2
    far = pick(x, lax.axis_index(axis) ^ 3)
    return x, lax.ppermute(far[:half], axis, pairs(4, 2)), lax.ppermute(far[half:], axis, pairs(4, 1))


def sum_near(far, axis):
    if len(far) == 1:
        return (lax.psum_scatter(far[0], axis, scatter_dimension=0, tiled=False),)
    x, top, low = far
    me = lax.axis_index(axis)
    half = x.shape[1] // 2
    one, two = pick(x, me ^ 1), pick(x, me ^ 2)
    one = jnp.concatenate([add(one[:half], top), one[half:]], axis=0)
    two = jnp.concatenate([two[:half], add(two[half:], low)], axis=0)
    one, two = together(one, two)
    return pick(x, me), lax.ppermute(one, axis, pairs(4, 1)), lax.ppermute(two, axis, pairs(4, 2))


def from_cores(x):
    cores = lax.axis_size("wid")
    return jnp.stack([lax.ppermute(x, "wid", pairs(cores, n)) for n in range(1, cores)], axis=0)


def core_sum(own, other):
    cores = lax.axis_size("wid")
    return add(own, *[lax.ppermute(other[n - 1 : n], "wid", pairs(cores, n)) for n in range(1, cores)])


def together(*values):
    return lax.optimization_barrier(values)


def per_device(layer_in, segment_ids, out_grad, gain_attn, w_query, w_key, w_value, w_dir, w_beta,
               b_beta, w_out, gain_mlp, w_gate, w_up, w_down):
    n_dp, n_hid, n_wid = (lax.axis_size(axis) for axis in ("dp", "hid", "wid"))
    row_count, tok, width = layer_in.shape
    heads = b_beta.shape[0]
    own_heads = heads // n_hid
    span = width // n_hid
    shard = w_query.shape[0]
    held = n_wid * tok
    copies = n_wid // row_count
    my_hid, my_dp = lax.axis_index("hid"), lax.axis_index("dp")
    side = 128
    columns = 4 * span + side

    row_own = to_row(layer_in)
    row_own, w_query, w_key, w_value, w_dir, w_beta, w_out, w_gate, w_up, w_down, out_grad = together(
        row_own, w_query, w_key, w_value, w_dir, w_beta, w_out, w_gate, w_up, w_down, out_grad)
    row_in = lax.all_gather(row_own, "hid", axis=0, tiled=True)

    down_t = w_down.T
    ff_rows, ff_cols = down_t.shape
    part = ff_cols // n_dp

    spare = side // 2
    ride = n_wid == row_count == 2 and own_heads + 2 <= spare and shard * spare >= held
    seg_rows = to_row(segment_ids).astype(BF16) if ride else jnp.zeros((held,), BF16)
    seg_rows = jnp.pad(seg_rows[: shard * spare], (0, max(0, shard * spare - held))).reshape(shard, spare)
    blank = jnp.zeros((shard, spare - own_heads - 2), BF16)
    blocks = []
    for j in range(n_hid):
        at = slice(j * span, (j + 1) * span)
        blocks.append(jnp.concatenate(
            [w_query[:, at], w_key[:, at], w_value[:, at], w_dir[:, at], w_beta[:, j * own_heads : (j + 1) * own_heads],
             gain_attn[:, None], gain_mlp[:, None], blank, seg_rows], axis=1))
    cat = exchange(blocks, "hid")
    segs = [x[:, columns - spare :].reshape(-1)[:held].astype(jnp.int32) for x in cat]
    cat = gather_near(jnp.stack(cat, axis=0), "dp")
    grad_b = out_grad.reshape(row_count * tok, width)
    wout = exchange([w_out] * n_hid, "hid")
    cut = [jnp.stack([x[:, j * part : (j + 1) * part] for x in (w_gate, w_up, down_t)]) for j in range(n_dp)]
    cat, cut = together(cat, cut)
    cat = gather_end(gather_far(cat, "dp"), "dp")
    ff = [choose(cut, my_dp)]
    for r in range(1, n_dp):
        ff.append(lax.ppermute(choose(cut, my_dp ^ r), "dp", pairs(n_dp, r)))
    cat, gains = gathered_rows(cat[None], from_cores(cat), side)
    bias_own = lax.dynamic_slice_in_dim(b_beta, my_hid * own_heads, own_heads, 0).astype(F32)

    row_in, cat, ff, wout, grad_b, segs = together(row_in, cat, ff, wout, grad_b, segs)
    ff = lax.all_gather(jnp.stack(ff, axis=0), "hid", axis=0, tiled=False)
    gain_one, gain_two = gains[own_heads], gains[own_heads + 1]
    if ride:
        segs = jnp.concatenate(by_source(segs, "hid"), axis=0)
    else:
        segs = lax.all_gather(segment_ids, ("hid", "wid"), axis=0, tiled=False)
        segs = pick(segs, lax.axis_index("wid") // copies, 1).reshape(-1)
    act_one, query, key, value, raw, logits = projected(row_in, cat, gain_one[None], bias_own, own_heads, tok)
    raw, wout, grad_b = together(raw, wout, grad_b)
    wout = gather_near(jnp.stack(wout, axis=0), "dp")
    grad_all = gather_near(grad_b, "dp")
    local = attention_local(query, key, raw, logits, tok)
    local, wout, grad_all = together(local, wout, grad_all)
    wout = gather_far(wout, "dp")
    grad_all = gather_far(grad_all, "dp")
    att, saved = attention_cross(query, key, value, raw, logits, segs, local, tok)
    att = exchange([att[j * held : (j + 1) * held] for j in range(n_hid)], "hid")
    wout = gather_end(wout, "dp")
    wout_full, _ = gathered_rows(wout[None], from_cores(wout), 0)
    grad_all = gather_end(grad_all, "dp").reshape(-1, width)
    att, wout_full = together(att, wout_full)
    ff_own, ff_other = ff[:, None], jnp.moveaxis(from_cores(ff), 0, 1)
    att = from_row(jnp.concatenate(by_source(att, "hid"), axis=1), row_count)
    att = att.reshape(row_count * tok, width)

    layer_f = layer_in.astype(F32).reshape(row_count * tok, width)
    middle = layer_f + mm(att, wout_full)
    act_two = norm_in(middle, gain_two).astype(BF16)
    act_all = square_gather(act_two, "dp").reshape(-1, width)
    mlp, d_act, hidden, d_gate, d_up = feed_forward(act_all, grad_all, ff_own, ff_other)
    d_act = sum_near(sum_far(d_act.reshape(n_dp, -1, width), "dp"), "dp")
    hidden, d_gate, d_up, mine = together(hidden, d_gate, d_up, d_act[0])
    g_own, g_other = feed_forward_weights(act_all, grad_all, hidden, d_gate, d_up, ff_own, ff_other)
    near, g_own, g_other = together(d_act[1:], g_own, g_other)
    d_act = add(mine, *near)

    _, pull_two = jax.vjp(norm_in, middle, gain_two)
    d_mid_norm, _ = pull_two(d_act.astype(F32))
    d_middle = grad_b.astype(F32) + d_mid_norm
    d_branch = d_middle.astype(BF16)
    d_att = mm(d_branch, wout_full, NT).astype(BF16).reshape(row_count, tok, width)
    d_att = to_row(d_att)
    d_att, att = together(d_att, att)
    d_att = exchange([d_att[:, j * span : (j + 1) * span] for j in range(n_hid)], "hid")
    ff_grads = core_sum(jnp.moveaxis(g_own, 1, 0), jnp.moveaxis(g_other, 1, 0))[0]
    wout_rows = row_gradients(att, d_branch, n_dp, n_hid, n_wid)
    d_att, wout_rows, ff_grads, mlp = together(d_att, wout_rows, ff_grads, mlp)
    mlp = sum_far(mlp.reshape(n_dp, -1, width), "dp")
    ff_grads = lax.psum_scatter(ff_grads, "hid", scatter_dimension=0, tiled=False)
    d_att = jnp.concatenate(by_source(d_att, "hid"), axis=0)
    wout_grad = sum_far(core_sum(*wout_rows)[0], "dp")

    crossed = attention_backward_cross(saved, d_att, tok)
    crossed, wout_grad, mlp = together(crossed, wout_grad, mlp)
    wout_grad = sum_near(wout_grad, "dp")
    mlp = sum_near(mlp, "dp")
    dv, *crossed = crossed
    dq, dk, draw, dlogit = attention_backward_local(saved, crossed, tok)
    d_logit = dlogit.transpose(0, 2, 1).reshape(-1, own_heads).astype(BF16)
    d_cat = jnp.concatenate(
        [dq, dk, dv, draw, jnp.pad(d_logit, ((0, 0), (0, side - own_heads)))], axis=1)
    d_gain_two = jnp.sum(d_act.astype(F32) * norm_in(middle, 1.0), axis=0, keepdims=True)
    bias_grad = jnp.sum(d_logit.astype(F32), axis=0)
    once = lax.axis_index("wid") % copies == 0
    d_act_one, *cat_grad = input_gradients(act_one, d_cat, cat, d_gain_two, bias_grad, once, n_dp, n_hid, n_wid)
    d_act_one, cat_grad, wout_grad, mlp = together(d_act_one, cat_grad, wout_grad, mlp)
    d_parts = d_act_one.reshape(n_hid, held, width)
    first_half = exchange_rows(d_parts[:, : held // 2], "hid")
    last_half = exchange_rows(d_parts[:, held // 2 :], "hid")
    wout_grad = add(*wout_grad)
    wout_got = exchange([wout_grad[j] for j in range(n_hid)], "hid")
    layer_out = (middle + add(*mlp).astype(F32)).astype(BF16)
    cat_grad = sum_far(core_sum(*cat_grad)[0], "dp")
    ff_got = [ff_grads[0]]
    for r in range(1, n_dp):
        ff_got.append(lax.ppermute(ff_grads[r], "dp", pairs(n_dp, r)))
    cat_grad, wout_got, ff_got, first_half = together(cat_grad, wout_got, ff_got, first_half)
    cat_grad = sum_near(cat_grad, "dp")
    cat_grad, last_half = together(cat_grad, last_half)
    cat_grad = add(*cat_grad)
    cat_got = exchange([cat_grad[j] for j in range(n_hid)], "hid")
    d_sum = jnp.concatenate([add(*first_half), add(*last_half)], axis=0)
    d_sum = from_row(d_sum, row_count).reshape(row_count * tok, width).astype(F32)
    grad_gate, grad_up, grad_down = laid_ff(ff_got)
    *weight_grads, tails = laid_columns(cat_got, side)
    grad_wout = sum(x.astype(F32) for x in wout_got)
    grad_beta = tails[:, :, :own_heads].transpose(1, 0, 2).reshape(shard, heads)
    gain_grads = jnp.sum(tails[:, :, own_heads : own_heads + 2], axis=0)
    grad_bias = tails[:, :own_heads, own_heads + 2].reshape(heads)

    _, pull_one = jax.vjp(lambda t: norm_in(t, gain_one), layer_f)
    grad_in = (d_middle + pull_one(d_sum)[0]).astype(BF16)

    return (
        layer_out.reshape(layer_in.shape), grad_in.reshape(layer_in.shape), gain_grads[:, 0],
        *weight_grads, grad_beta, grad_bias,
        grad_wout, gain_grads[:, 1], grad_gate, grad_up, grad_down,
    )


def solution(mesh):
    in_specs = (
        P("dp", ("hid", "wid"), None),
        P("dp", ("hid", "wid")),
        P("dp", ("hid", "wid"), None),
        P(("dp", "hid", "wid")),
        P(("dp", "hid", "wid"), None),
        P(("dp", "hid", "wid"), None),
        P(("dp", "hid", "wid"), None),
        P(("dp", "hid", "wid"), None),
        P(("dp", "hid", "wid"), None),
        P(),
        P(("dp", "hid", "wid"), None),
        P(("dp", "hid", "wid")),
        P(("dp", "wid"), "hid"),
        P(("dp", "wid"), "hid"),
        P("hid", ("dp", "wid")),
    )
    out_specs = (
        P("dp", ("hid", "wid"), None),
        P("dp", ("hid", "wid"), None),
        P(("dp", "hid", "wid")),
        P(("dp", "hid", "wid"), None),
        P(("dp", "hid", "wid"), None),
        P(("dp", "hid", "wid"), None),
        P(("dp", "hid", "wid"), None),
        P(("dp", "hid", "wid"), None),
        P(),
        P(("dp", "hid", "wid"), None),
        P(("dp", "hid", "wid")),
        P(("dp", "wid"), "hid"),
        P(("dp", "wid"), "hid"),
        P("hid", ("dp", "wid")),
    )
    return jax.shard_map(
        per_device, mesh=mesh, in_specs=in_specs, out_specs=out_specs, check_vma=False
    )
```

```python
import functools
import math

import jax
import jax.numpy as jnp
from jax import lax
from jax.experimental import pallas as pl
from jax.experimental.pallas import tpu as pltpu
from jax.sharding import PartitionSpec as P

EPS = 1e-06
NEG = -1e30
F32 = jnp.float32
BF16 = jnp.bfloat16
NN = ((1,), (0,))
NT = ((1,), (1,))
TN = ((0,), (0,))
VMEM_BYTES = 56 * 1024 * 1024
SOME = 2


def mm(left, right, dims=NN):
    return lax.dot_general(left, right, (dims, ((), ())), preferred_element_type=F32)


def halves(x):
    if x.dtype == BF16:
        return (x,)
    top = x.astype(BF16)
    return (top, (x - top.astype(F32)).astype(BF16))


def dot(left, right, dims):
    picked = [(a, b) for a in range(len(left)) for b in range(len(right)) if a + b < 2]
    if len(picked) == 1:
        return mm(left[0], right[0], dims)
    x = jnp.concatenate([left[a] for a, _ in picked], axis=dims[0][0])
    y = jnp.concatenate([right[b] for _, b in picked], axis=dims[1][0])
    return mm(x, y, dims)


def iotas(size):
    rows = lax.broadcasted_iota(jnp.int32, (size, size), 0)
    cols = lax.broadcasted_iota(jnp.int32, (size, size), 1)
    return rows, cols


def unit_dirs(raw):
    inv = lax.rsqrt(jnp.sum(raw * raw, axis=-1, keepdims=True) + EPS)
    return raw * inv, inv


def local_forward(heads, size, q_ref, k_ref, raw_ref, logit_ref, qin_ref, kout_ref, ptop_ref, plow_ref,
                  intra_ref, t_ref, e_ref, cm_ref, s_ref):
    width = q_ref.shape[1] // heads
    rows, cols = iotas(size)
    strict, lower, diag = rows > cols, rows >= cols, rows == cols
    apart = rows ^ cols
    some = range(q_ref.shape[0] // size)
    at = [(slice(n * size, (n + 1) * size), slice(h * width, (h + 1) * width)) for n in some for h in range(heads)]
    wide = [(slice(n * width, (n + 1) * width), slice(h * width, (h + 1) * width)) for n in some for h in range(heads)]
    every = range(len(at))
    betas = [2.0 * jax.nn.sigmoid(logit_ref[n, h : h + 1, :]) for n in some for h in range(heads)]
    q, k = [q_ref[a] for a in at], [k_ref[a] for a in at]
    ws = [halves(unit_dirs(raw_ref[a])[0]) for a in at]
    gram = [jnp.where(strict, dot(w, w, NT), 0.0) for w in ws]
    beta = [jnp.where(diag, b, 0.0) for b in betas]
    beta_col = [jnp.sum(b, axis=1, keepdims=True) for b in beta]
    t = [beta[u] - jnp.where(apart == 1, beta_col[u] * gram[u] * betas[u], 0.0) for u in every]
    shift = 1
    while (1 << shift) < size:
        near = (apart >> shift) == 1
        part = [halves(jnp.where(near, g, 0.0)) for g in gram]
        ts = [halves(x) for x in t]
        once = [dot(ts[u], part[u], NN) for u in every]
        t = [t[u] - dot(halves(once[u]), ts[u], NN) for u in every]
        shift += 1
    ts = [halves(x) for x in t]
    bs = [halves(jnp.where(lower, dot((q[u],), ws[u], NT), 0.0)) for u in every]
    ms = [halves(jnp.where(strict, dot(ws[u], (k[u],), NT), 0.0)) for u in every]
    e = [dot(ts[u], ms[u], NN) for u in every]
    s = [dot(ts[u], ws[u], NN) for u in every]
    cm = [dot(bs[u], ts[u], NN) for u in every]
    es = [halves(x) for x in e]
    for u in every:
        t_ref[at[u]], e_ref[at[u]], cm_ref[at[u]], s_ref[at[u]] = t[u], e[u], cm[u], s[u]
        intra_ref[at[u]] = dot((q[u],), (k[u],), NT) - dot(bs[u], es[u], NN)
        qin_ref[at[u]] = (q[u].astype(F32) - dot(halves(cm[u]), ws[u], NN)).astype(BF16)
        kout_ref[at[u]] = (k[u].astype(F32) - dot(es[u], ws[u], TN)).astype(BF16)
        step = jnp.where(diag, 1.0, 0.0) - dot(ws[u], halves(s[u]), TN)
        ptop_ref[wide[u]], plow_ref[wide[u]] = halves(step)


def cross_forward(heads, group, scale, qin_ref, kout_ref, ptop_ref, plow_ref, intra_ref, v_ref,
                  segc_ref, segr_ref, out_ref, prob_ref, keep_ref, frame, score):
    size = qin_ref.shape[0]
    width = qin_ref.shape[1] // heads
    total = v_ref.shape[0]
    wide = group * size
    c = pl.program_id(0)
    parts = [slice(g * wide, (g + 1) * wide) for g in range(total // wide)]
    at = [slice(h * width, (h + 1) * width) for h in range(heads)]
    every = range(heads)

    @pl.when(c == 0)
    def _():
        frame[...] = jnp.zeros_like(frame)
        score[...] = jnp.full_like(score, NEG)

    rows, cols = iotas(size)
    own = pl.multiple_of(c * size, size)
    seg = segc_ref[...]
    for g, part in enumerate(parts):

        @pl.when(g * group < c)
        def _():
            raw = [mm(qin_ref[:, at[h]], frame[h, part, :], NT) for h in every]
            place = lax.broadcasted_iota(jnp.int32, (size, wide), 1) + g * wide
            permit = (place < own) & (seg == segr_ref[:, part])
            for h in every:
                score[h, :, part] = jnp.where(permit, scale * raw[h], NEG)

    permit = (rows >= cols) & (seg == segr_ref[:, pl.ds(own, size)])
    for h in every:
        score[h, :, pl.ds(own, size)] = jnp.where(permit, scale * intra_ref[:, at[h]], NEG)
    top = [jnp.max(score[h], axis=-1, keepdims=True) for h in every]
    e = [jnp.exp(score[h] - top[h]) for h in every]
    inv = [1.0 / jnp.sum(x, axis=-1, keepdims=True) for x in e]
    for h in every:
        prob_ref[0, h] = (e[h] * inv[h]).astype(BF16)
    for h in every:
        out_ref[:, at[h]] = mm(prob_ref[0, h], v_ref[:, at[h]]).astype(BF16)
        keep_ref[0, h] = frame[h]
    for g, part in enumerate(parts):

        @pl.when(g * group < c)
        def _():
            moved = [dot((frame[h, part, :],), (ptop_ref[:, at[h]], plow_ref[:, at[h]]), NT) for h in every]
            for h in every:
                frame[h, part, :] = moved[h].astype(BF16)

    for h in every:
        frame[h, pl.ds(own, size), :] = kout_ref[:, at[h]]


def cross_backward(heads, group, scale, grad_ref, v_ref, prob_ref, keep_ref, qin_ref, ptop_ref,
                   plow_ref, dqin_ref, dintra_ref, dkout_ref, dstep_ref, dv_ref, carry, dvals, ds_ref):
    size = grad_ref.shape[0]
    width = grad_ref.shape[1] // heads
    total = v_ref.shape[0]
    wide = group * size
    c = pl.num_programs(0) - 1 - pl.program_id(0)
    parts = [slice(g * wide, (g + 1) * wide) for g in range(total // wide)]
    at = [slice(h * width, (h + 1) * width) for h in range(heads)]
    every = range(heads)

    @pl.when(pl.program_id(0) == 0)
    def _():
        carry[...] = jnp.zeros_like(carry)
        dvals[...] = jnp.zeros_like(dvals)

    own = pl.multiple_of(c * size, size)
    dp = [mm(grad_ref[:, at[h]], v_ref[:, at[h]], NT) for h in every]
    pf = [prob_ref[0, h].astype(F32) for h in every]
    delta = [jnp.sum(pf[h] * dp[h], axis=-1, keepdims=True) for h in every]
    for h in every:
        ds_ref[h] = (pf[h] * (dp[h] - delta[h])).astype(BF16)
    low = [carry[h].astype(BF16) for h in every]
    dqin = [mm(ds_ref[h], keep_ref[0, h]) for h in every]
    dstep = [mm(low[h], keep_ref[0, h], TN) for h in every]
    for h in every:
        dqin_ref[:, at[h]] = scale * dqin[h]
        dstep_ref[:, at[h]] = dstep[h]
        dintra_ref[:, at[h]] = ds_ref[h, :, pl.ds(own, size)]
        dkout_ref[:, at[h]] = carry[h, pl.ds(own, size), :]
    for g, part in enumerate(parts):

        @pl.when(g * group <= c)
        def _():
            more = [mm(prob_ref[0, h, :, part], grad_ref[:, at[h]], TN) for h in every]
            for h in every:
                dvals[h, part, :] += more[h]

        @pl.when(g * group < c)
        def _():
            fresh = [mm(ds_ref[h, :, part], qin_ref[:, at[h]], TN) for h in every]
            moved = [dot((carry[h, part, :].astype(BF16),), (ptop_ref[:, at[h]], plow_ref[:, at[h]]), NN)
                     for h in every]
            for h in every:
                carry[h, part, :] = scale * fresh[h] + moved[h]

    @pl.when(c == 0)
    def _():
        for h in every:
            dv_ref[:, at[h]] = dvals[h].astype(BF16)


def local_backward(heads, size, scale, q_ref, k_ref, raw_ref, logit_ref, t_ref, e_ref, cm_ref, s_ref,
                   dqin_ref, dintra_ref, dkout_ref, dstep_ref, dv_ref, out_ref):
    width = q_ref.shape[1] // heads
    rows, cols = iotas(size)
    strict, lower, diag = rows > cols, rows >= cols, rows == cols
    some = range(q_ref.shape[0] // size)
    units = [(n, h) for n in some for h in range(heads)]
    at = [(slice(n * size, (n + 1) * size), slice(h * width, (h + 1) * width)) for n, h in units]
    wide = [(slice(n * width, (n + 1) * width), slice(h * width, (h + 1) * width)) for n, h in units]
    every = range(len(units))
    span = heads * width
    out = lambda u, part: (at[u][0], slice(part * span + units[u][1] * width, part * span + (units[u][1] + 1) * width))
    q, k = [(q_ref[a],) for a in at], [(k_ref[a],) for a in at]
    both = [unit_dirs(raw_ref[a]) for a in at]
    betas = [2.0 * jax.nn.sigmoid(logit_ref[n, h : h + 1, :]) for n, h in units]
    ws = [halves(w) for w, _ in both]
    ts, es, cms, ss = ([halves(ref[a]) for a in at] for ref in (t_ref, e_ref, cm_ref, s_ref))
    dintra = [(dintra_ref[a],) for a in at]
    dqs, dks = [halves(dqin_ref[a]) for a in at], [halves(dkout_ref[a]) for a in at]
    dps = [halves(dstep_ref[a]) for a in wide]
    b = [halves(jnp.where(lower, dot(q[u], ws[u], NT), 0.0)) for u in every]
    d_s = [halves(-dot(ws[u], dps[u], NN)) for u in every]
    d_e = [halves(-(dot(ws[u], dks[u], NT) + scale * dot(b[u], dintra[u], TN))) for u in every]
    d_cm = [halves(-dot(dqs[u], ws[u], NT)) for u in every]
    y_s = [dot(ts[u], d_s[u], TN) for u in every]
    y_e = [dot(ts[u], d_e[u], TN) for u in every]
    y_c = [dot(d_cm[u], ts[u], NT) for u in every]
    d_x = [-(dot(halves(y_s[u]), ss[u], NT) + dot(halves(y_e[u]), es[u], NT) + dot(cms[u], halves(y_c[u]), TN))
           for u in every]
    d_b = [halves(jnp.where(lower, y_c[u] - scale * dot(dintra[u], es[u], NT), 0.0)) for u in every]
    d_m = [halves(jnp.where(strict, y_e[u], 0.0)) for u in every]
    d_a = [halves(jnp.where(strict, d_x[u], 0.0)) for u in every]
    for u in every:
        a = at[u]
        out_ref[out(u, 0)] = (dqin_ref[a] + scale * dot(dintra[u], k[u], NN) + dot(d_b[u], ws[u], NN)).astype(BF16)
        out_ref[out(u, 1)] = (dkout_ref[a] + scale * dot(dintra[u], q[u], TN) + dot(d_m[u], ws[u], TN)).astype(BF16)
    d_w = [y_s[u] - dot(ss[u], dps[u], NT) - dot(es[u], dks[u], NN) - dot(cms[u], dqs[u], TN)
           + dot(d_b[u], q[u], TN) + dot(d_m[u], k[u], NN) + dot(d_a[u], ws[u], NN) + dot(d_a[u], ws[u], TN)
           for u in every]
    for u in every:
        raw, inv = raw_ref[at[u]], both[u][1]
        draw = inv * d_w[u] - raw * (inv * inv * inv) * jnp.sum(raw * d_w[u], axis=-1, keepdims=True)
        out_ref[out(u, 3)] = draw.astype(BF16)
    out_ref[:, 2 * span : 3 * span] = dv_ref[...]
    side = out_ref.shape[1] - 4 * span
    for n in some:
        lines = []
        for h in range(heads):
            u = n * heads + h
            at_diag = jnp.sum(jnp.where(diag, d_x[u], 0.0), axis=0, keepdims=True)
            lines.append(-at_diag * (1.0 - 0.5 * betas[u]) / betas[u])
        lines.append(jnp.zeros((side - heads, size), F32))
        out_ref[n * size : (n + 1) * size, 4 * span :] = jnp.transpose(jnp.concatenate(lines, axis=0)).astype(BF16)


def run(body, grid, inputs, in_specs, outputs, out_specs, scratch, flops):
    return pl.pallas_call(
        body, grid=(grid,), in_specs=in_specs, out_specs=out_specs, out_shape=outputs,
        scratch_shapes=scratch,
        compiler_params=pltpu.CompilerParams(
            dimension_semantics=("arbitrary",), vmem_limit_bytes=VMEM_BYTES),
        cost_estimate=pl.CostEstimate(
            flops=flops, transcendentals=0,
            bytes_accessed=sum(x.size * x.dtype.itemsize for x in (*inputs, *outputs))),
    )(*inputs)


def shape(dims, dtype):
    return jax.ShapeDtypeStruct(dims, dtype)


def group_of(blocks):
    return 4 if blocks % 4 == 0 else 1


def attention_local(q, k, raw, logits, size):
    tokens, width = q.shape
    blocks, heads, _ = logits.shape
    head = width // heads
    some = SOME if blocks % SOME == 0 else 1
    block = pl.BlockSpec((some * size, width), lambda c: (c, 0))
    square = pl.BlockSpec((some * head, width), lambda c: (c, 0))
    logit_block = pl.BlockSpec((some, heads, size), lambda c: (c, 0, 0))
    f, b = shape((tokens, width), F32), shape((tokens, width), BF16)
    stepped = shape((blocks * head, width), BF16)
    return run(
        functools.partial(local_forward, heads, size), blocks // some, (q, k, raw, logits),
        [block, block, block, logit_block], (b, b, stepped, stepped, f, f, f, f, f),
        [block, block, square, square, block, block, block, block, block], [],
        blocks * heads * 62 * 2 * size * size * head)


def attention_cross(q, k, v, raw, logits, segments, local, size):
    qin, kout, ptop, plow, intra, t, e, cm, s = local
    tokens, width = q.shape
    blocks, heads, _ = logits.shape
    head = width // heads
    block = pl.BlockSpec((size, width), lambda c: (c, 0))
    square = pl.BlockSpec((head, width), lambda c: (c, 0))
    b = shape((tokens, width), BF16)
    group = group_of(blocks)
    whole = pl.BlockSpec((tokens, width), lambda c: (0, 0))
    wide_prob = pl.BlockSpec((1, heads, size, tokens), lambda c: (c, 0, 0, 0))
    wide_keep = pl.BlockSpec((1, heads, tokens, head), lambda c: (c, 0, 0, 0))
    out, prob, keep = run(
        functools.partial(cross_forward, heads, group, 1.0 / math.sqrt(head)), blocks,
        (qin, kout, ptop, plow, intra, v, segments.reshape(tokens, 1), segments.reshape(1, tokens)),
        [block, block, square, square, block, whole,
         pl.BlockSpec((size, 1), lambda c: (c, 0)), pl.BlockSpec((1, tokens), lambda c: (0, 0))],
        (b, shape((blocks, heads, size, tokens), BF16), shape((blocks, heads, tokens, head), BF16)),
        [block, wide_prob, wide_keep],
        [pltpu.VMEM((heads, tokens, head), BF16), pltpu.VMEM((heads, size, tokens), F32)],
        blocks * heads * 4 * 2 * size * tokens * head)
    return out, (q, k, v, raw, logits, qin, ptop, plow, t, e, cm, s, prob, keep)


def attention_backward_cross(saved, grad, size):
    q, k, v, raw, logits, qin, ptop, plow, t, e, cm, s, prob, keep = saved
    tokens, width = q.shape
    blocks, heads, _ = logits.shape
    head = width // heads
    scale = 1.0 / math.sqrt(head)
    back = lambda c: (blocks - 1 - c, 0)
    block = pl.BlockSpec((size, width), back)
    square = pl.BlockSpec((head, width), back)
    whole = pl.BlockSpec((tokens, width), lambda c: (0, 0))
    wide_prob = pl.BlockSpec((1, heads, size, tokens), lambda c: (blocks - 1 - c, 0, 0, 0))
    wide_keep = pl.BlockSpec((1, heads, tokens, head), lambda c: (blocks - 1 - c, 0, 0, 0))
    f, b = shape((tokens, width), F32), shape((tokens, width), BF16)
    dqin, dintra, dkout, dstep, dv = run(
        functools.partial(cross_backward, heads, group_of(blocks), scale), blocks,
        (grad, v, prob, keep, qin, ptop, plow),
        [block, whole, wide_prob, wide_keep, block, square, square],
        (f, b, f, shape((blocks * head, width), F32), b),
        [block, block, block, square, whole],
        [pltpu.VMEM((heads, tokens, head), F32), pltpu.VMEM((heads, tokens, head), F32),
         pltpu.VMEM((heads, size, tokens), BF16)],
        blocks * heads * 7 * 2 * size * tokens * head)
    return dv, dqin, dintra, dkout, dstep


def attention_backward_local(saved, dv, crossed, size, side):
    q, k, v, raw, logits, qin, ptop, plow, t, e, cm, s, prob, keep = saved
    tokens, width = q.shape
    blocks, heads, _ = logits.shape
    head = width // heads
    scale = 1.0 / math.sqrt(head)
    some = SOME if blocks % SOME == 0 else 1
    block = pl.BlockSpec((some * size, width), lambda c: (c, 0))
    square = pl.BlockSpec((some * head, width), lambda c: (c, 0))
    logit_block = pl.BlockSpec((some, heads, size), lambda c: (c, 0, 0))
    return run(
        functools.partial(local_backward, heads, size, scale), blocks // some,
        (q, k, raw, logits, t, e, cm, s, *crossed, dv),
        [block, block, block, logit_block, block, block, block, block, block, block, block, square, block],
        (shape((tokens, 4 * width + side), BF16),), [pl.BlockSpec((some * size, 4 * width + side), lambda c: (c, 0))], [],
        blocks * heads * 60 * 2 * size * size * head)[0]


def ff_forward(me_ref, act_ref, grad_ref, own_ref, other_ref, mlp_ref, dact_ref, hid_ref, dgate_ref, dup_ref,
               gate_w, up_w, down_w, mlp, dact):
    tokens = act_ref.shape[0]
    cores, chips, rows = own_ref.shape[1] + other_ref.shape[1], own_ref.shape[2], own_ref.shape[4]
    tile = min(tokens, 256)

    for r in range(chips):
        for n in range(cores):
            held = own_ref.at[0, 0, r] if n == 0 else other_ref.at[0, n - 1, r]
            chip, core = me_ref[0] ^ r, me_ref[1] ^ n
            to = pl.ds(pl.multiple_of((chip * cores + core) * rows, rows), rows)
            gate_w[to, :] = held[0]
            up_w[to, :] = held[1]
            down_w[to, :] = held[2]

    @pl.when(pl.program_id(0) == 0)
    def _():
        mlp[...] = jnp.zeros_like(mlp)
        dact[...] = jnp.zeros_like(dact)

    @pl.loop(0, tokens // tile)
    def _(i):
        at = pl.ds(pl.multiple_of(i * tile, tile), tile)
        act, grad = act_ref[at, :], grad_ref[at, :]
        gate, up = mm(act, gate_w[...]), mm(act, up_w[...])
        sig = jax.nn.sigmoid(gate)
        silu = gate * sig
        hidden = (silu * up).astype(BF16)
        d_hidden = mm(grad, down_w[...])
        d_gate = (d_hidden * up * sig * (1.0 + gate * (1.0 - sig))).astype(BF16)
        d_up = (d_hidden * silu).astype(BF16)
        hid_ref[at, :] = hidden
        dgate_ref[at, :] = d_gate
        dup_ref[at, :] = d_up
        mlp[at, :] += mm(hidden, down_w[...], NT)
        dact[at, :] += mm(d_gate, gate_w[...], NT) + mm(d_up, up_w[...], NT)

    @pl.when(pl.program_id(0) == pl.num_programs(0) - 1)
    def _():
        mlp_ref[...] = mlp[...].astype(BF16)
        dact_ref[...] = dact[...].astype(BF16)


def ff_weights(me_ref, *refs):
    *ins, own_ref, other_ref = refs
    groups = [ins[5 * n : 5 * n + 5] for n in range(len(ins) // 5)]
    cores, chips, rows = own_ref.shape[1] + other_ref.shape[1], own_ref.shape[2], own_ref.shape[4]
    for d in range(chips):
        at = slice(d * cores * rows, (d + 1) * cores * rows)
        r = me_ref[0] ^ d
        gate = up = down = 0.0
        for act_ref, grad_ref, hid_ref, dgate_ref, dup_ref in groups:
            act, grad = act_ref[:, at], grad_ref[:, at]
            gate = gate + mm(act, dgate_ref[...], TN)
            up = up + mm(act, dup_ref[...], TN)
            down = down + mm(grad, hid_ref[...], TN)
        for i, part in enumerate((gate, up, down)):
            pieces = [part[w * rows : (w + 1) * rows, :].astype(BF16) for w in range(cores)]
            for n in range(cores):
                piece = pieces[0]
                for w in range(1, cores):
                    piece = jnp.where((me_ref[1] ^ n) == w, pieces[w], piece)
                if n == 0:
                    own_ref[0, 0, r, i] = piece
                else:
                    other_ref[0, n - 1, r, i] = piece


def place_self():
    return jnp.stack([lax.axis_index("dp"), lax.axis_index("wid")]).astype(jnp.int32)


SCALARS = pl.BlockSpec(memory_space=pltpu.SMEM)


def feed_forward(act, grad, own, other):
    tokens, width = act.shape
    groups, part = own.shape[0], own.shape[5]
    whole = pl.BlockSpec((tokens, width), lambda h: (0, 0))
    units = pl.BlockSpec((tokens, part), lambda h: (0, h))
    held = [pl.BlockSpec((1,) + x.shape[1:], lambda h: (h, 0, 0, 0, 0, 0)) for x in (own, other)]
    full, some = shape((tokens, width), BF16), shape((tokens, groups * part), BF16)
    flops = 6 * 2 * tokens * width * groups * part
    return run(ff_forward, groups, (place_self(), act, grad, own, other), [SCALARS, whole, whole, *held],
               (full, full, some, some, some), [whole, whole, units, units, units],
               [pltpu.VMEM((width, part), BF16)] * 3 + [pltpu.VMEM((tokens, width), F32)] * 2, flops)


def feed_forward_weights(acts, grads, saved, own, other):
    width = acts[0].shape[1]
    groups, part = own.shape[0], own.shape[5]
    values, specs = [], []
    for act, grad, some in zip(acts, grads, saved):
        values += [act, grad, *some]
        specs += [pl.BlockSpec(act.shape, lambda h: (0, 0))] * 2
        specs += [pl.BlockSpec((act.shape[0], part), lambda h: (0, h))] * 3
    held = [pl.BlockSpec((1,) + x.shape[1:], lambda h: (h, 0, 0, 0, 0, 0)) for x in (own, other)]
    return run(ff_weights, groups, (place_self(), *values), [SCALARS, *specs],
               (shape(own.shape, BF16), shape(other.shape, BF16)), held, [],
               3 * 2 * sum(x.shape[0] for x in acts) * width * groups * part)


def split_rows(me_ref, part, at, own_ref, other_ref):
    cores, shards, rows = own_ref.shape[0] + other_ref.shape[0], own_ref.shape[2], own_ref.shape[3]
    for h in range(shards):
        pieces = [part[(h * cores + w) * rows : (h * cores + w + 1) * rows, :] for w in range(cores)]
        for n in range(cores):
            piece = pieces[0]
            for w in range(1, cores):
                piece = jnp.where((me_ref[1] ^ n) == w, pieces[w], piece)
            if n == 0:
                own_ref[0, 0, h, :, at] = piece
            else:
                other_ref[n - 1, 0, h, :, at] = piece


def row_grads(me_ref, left_ref, right_ref, own_ref, other_ref):
    columns = right_ref.shape[1]
    for start in range(0, columns, 512):
        at = slice(start, min(start + 512, columns))
        split_rows(me_ref, mm(left_ref[...], right_ref[:, at], TN).astype(BF16), at, own_ref, other_ref)


def split_whole(full, chips, shards, cores, rows):
    full = full.astype(BF16).reshape(chips, shards, cores, rows, full.shape[1])
    full = jnp.take(full, lax.axis_index("wid") ^ jnp.arange(cores), axis=2).transpose(2, 0, 1, 3, 4)
    return full[:1], full[1:]


def row_gradients(left, right, chips, shards, cores):
    tokens, width = left.shape
    columns = right.shape[1]
    rows = width // (chips * shards * cores)
    if rows % 16:
        return split_whole(mm(left, right, TN), chips, shards, cores, rows)
    outs = [shape((n, chips, shards, rows, columns), BF16) for n in (1, cores - 1)]
    specs = [pl.BlockSpec((x.shape[0], 1, shards, rows, columns), lambda d: (0, d, 0, 0, 0)) for x in outs]
    return run(row_grads, chips, (place_self(), left, right),
               [SCALARS, pl.BlockSpec((tokens, width // chips), lambda d: (0, d)),
                pl.BlockSpec((tokens, columns), lambda d: (0, 0))],
               tuple(outs), specs, [], 2 * tokens * width * columns)


def input_grads(me_ref, bias_ref, left_ref, right_ref, w_ref, two_ref, din_ref, own_ref, other_ref):
    columns, side = right_ref.shape[1], 128
    heads, rows = bias_ref.shape[0], own_ref.shape[3]
    din_ref[...] = mm(right_ref[...], w_ref[...], NT).astype(BF16)
    spans = [(start, min(start + 512, columns - side)) for start in range(0, columns - side, 512)]
    gain_sum = jnp.zeros((left_ref.shape[1], 1), F32)
    for start, stop in spans + [(columns - side, columns)]:
        part = mm(left_ref[...], right_ref[:, start:stop], TN)
        weight = w_ref[:, start:stop].astype(F32)
        lane = lax.broadcasted_iota(jnp.int32, part.shape, 1)
        if stop == columns:
            gain_sum = gain_sum + jnp.sum(jnp.where(lane < heads, part * weight, 0.0), axis=1, keepdims=True)
            gain = jnp.sum(jnp.where(lane == heads, weight, 0.0), axis=1, keepdims=True)
            row = lax.rem(lax.broadcasted_iota(jnp.int32, part.shape, 0), rows)
            two = jnp.transpose(jnp.broadcast_to(two_ref[...], (side, part.shape[0])))
            part = jnp.where(lane < heads, part, 0.0) + jnp.where(lane == heads, gain_sum / gain, 0.0)
            for n in range(heads):
                part = part + jnp.where((lane == heads + 2) & (row == n), bias_ref[n], 0.0)
            part = jnp.where(me_ref[2] == 1, part, 0.0) + jnp.where(lane == heads + 1, two, 0.0)
        else:
            gain_sum = gain_sum + jnp.sum(part * weight, axis=1, keepdims=True)
            part = jnp.where(me_ref[2] == 1, part, 0.0)
        split_rows(me_ref, part.astype(BF16), slice(start, stop), own_ref, other_ref)


def input_gradients(left, right, weights, two, bias, once, chips, shards, cores):
    tokens, width = left.shape
    columns, heads = right.shape[1], bias.shape[0]
    rows = width // (chips * shards * cores)
    if rows % 16:
        full = mm(left, right, TN)
        lane = lax.broadcasted_iota(jnp.int32, (width, columns), 1) - (columns - 128)
        row = lax.broadcasted_iota(jnp.int32, (width, columns), 0) % rows
        wide = weights.astype(F32)
        gain = jnp.sum(jnp.where(lane < heads, full * wide, 0.0), axis=1, keepdims=True)
        gain = gain / wide[:, columns - 128 + heads][:, None]
        full = full + jnp.where(lane == heads, gain, 0.0)
        for n in range(heads):
            full = full + jnp.where((lane == heads + 2) & (row == n), bias[n], 0.0)
        full = jnp.where(once, full, 0.0) + jnp.where(lane == heads + 1, two.T, 0.0)
        return (mm(right, weights, NT).astype(BF16), *split_whole(full, chips, shards, cores, rows))
    outs = [shape((n, chips, shards, rows, columns), BF16) for n in (1, cores - 1)]
    specs = [pl.BlockSpec((x.shape[0], 1, shards, rows, columns), lambda d: (0, d, 0, 0, 0)) for x in outs]
    features = pl.BlockSpec((tokens, width // chips), lambda d: (0, d))
    me = jnp.concatenate([place_self(), once[None].astype(jnp.int32)])
    return run(input_grads, chips, (me, bias, left, right, weights, two),
               [SCALARS, SCALARS, features, pl.BlockSpec((tokens, columns), lambda d: (0, 0)),
                pl.BlockSpec((width // chips, columns), lambda d: (d, 0)), pl.BlockSpec((1, width // chips), lambda d: (0, d))],
               (shape((tokens, width), BF16), *outs), [features, *specs], [], 4 * tokens * width * columns)


def lay_columns(me_ref, *refs):
    *got, a_ref, b_ref, c_ref, d_ref, tail_ref = refs
    count, span = len(got), a_ref.shape[1] // len(got)
    for k, ref in enumerate(got):
        source = lax.rem(me_ref[0] - k + count, count)
        to = pl.ds(pl.multiple_of(source * span, 128), span)
        for i, out in enumerate((a_ref, b_ref, c_ref, d_ref)):
            out[:, to] = ref[:, i * span : (i + 1) * span].astype(F32)
        tail_ref[source] = ref[:, 4 * span :].astype(F32)


def laid_columns(got, side):
    count, (rows, columns) = len(got), got[0].shape
    span = (columns - side) // 4
    if rows % 16 or span % 128:
        got = by_source(got, "hid")
        whole = [jnp.concatenate([x[:, i * span : (i + 1) * span] for x in got], axis=1).astype(F32) for i in range(4)]
        return (*whole, jnp.stack([x[:, 4 * span :] for x in got]).astype(F32))
    one = pl.BlockSpec((rows, columns), lambda i: (0, 0))
    out = pl.BlockSpec((rows, count * span), lambda i: (0, 0))
    return run(lay_columns, 1, (lax.axis_index("hid")[None].astype(jnp.int32), *got), [SCALARS] + [one] * count,
               (shape((rows, count * span), F32),) * 4 + (shape((count, rows, side), F32),),
               [out] * 4 + [pl.BlockSpec((count, rows, side), lambda i: (0, 0, 0))], [], 0)


def lay_ff(me_ref, *refs):
    *got, gate_ref, up_ref, down_ref = refs
    part = got[0].shape[2]
    for r, ref in enumerate(got):
        to = pl.ds(pl.multiple_of((me_ref[0] ^ r) * part, 128), part)
        gate_ref[:, to] = ref[0].astype(F32)
        up_ref[:, to] = ref[1].astype(F32)
        down_ref[to, :] = jnp.transpose(ref[2].astype(F32))


def laid_ff(got):
    count, (_, rows, part) = len(got), got[0].shape
    outs = ((rows, count * part), (rows, count * part), (count * part, rows))
    return run(lay_ff, 1, (lax.axis_index("dp")[None].astype(jnp.int32), *got),
               [SCALARS] + [pl.BlockSpec((3, rows, part), lambda i: (0, 0, 0))] * count,
               tuple(shape(x, F32) for x in outs), [pl.BlockSpec(x, lambda i: (0, 0)) for x in outs], [], 0)


def lay_rows(me_ref, own_ref, other_ref, out_ref, *turned):
    cores, shards, rows = own_ref.shape[0] + other_ref.shape[0], own_ref.shape[2], own_ref.shape[3]
    for k in range(shards):
        h = lax.rem(me_ref[2] - k + shards, shards)
        for n in range(cores):
            to = pl.ds(pl.multiple_of((h * cores + (me_ref[1] ^ n)) * rows, rows), rows)
            out_ref[to, :] = own_ref[0, 0, k] if n == 0 else other_ref[n - 1, 0, k]
    for ref in turned:
        ref[...] = jnp.transpose(out_ref[:, -ref.shape[0] :].astype(F32))


def gathered_rows(own, other, side):
    _, chips, shards, rows, columns = own.shape
    cores = 1 + other.shape[0]
    if rows % 16:
        full = jnp.concatenate([own, other], axis=0)
        full = jnp.take(full, lax.axis_index("wid") ^ jnp.arange(cores), axis=0)
        full = jnp.take(full, (lax.axis_index("hid") - jnp.arange(shards)) % shards, axis=2)
        full = full.transpose(1, 2, 0, 3, 4).reshape(-1, columns)
        return full, (full[:, columns - side :].astype(F32).T if side else None)
    me = jnp.concatenate([place_self(), lax.axis_index("hid")[None].astype(jnp.int32)])
    specs = [pl.BlockSpec((x.shape[0], 1, shards, rows, columns), lambda d: (0, d, 0, 0, 0)) for x in (own, other)]
    size = cores * shards * rows
    outs, out_specs = [shape((chips * size, columns), BF16)], [pl.BlockSpec((size, columns), lambda d: (d, 0))]
    if side:
        outs.append(shape((side, chips * size), F32))
        out_specs.append(pl.BlockSpec((side, size), lambda d: (0, d)))
    out = run(lay_rows, chips, (me, own, other), [SCALARS, *specs], tuple(outs), out_specs, [], 0)
    return out[0], (out[1] if side else None)


def project(heads, tok, bias_ref, x_ref, w_ref, gain_ref, act_ref, q_ref, k_ref, v_ref, raw_ref, logit_ref):
    x = x_ref[...].astype(F32)
    unit = x * lax.rsqrt(jnp.mean(x * x, axis=-1, keepdims=True) + EPS)
    act_ref[...] = (unit * gain_ref[...]).astype(BF16)
    act, span = act_ref[...], q_ref.shape[1]
    for i, out in enumerate((q_ref, k_ref, v_ref, raw_ref)):
        out[...] = mm(act, w_ref[:, i * span : (i + 1) * span]).astype(out.dtype)
    beside = mm(act, w_ref[:, 4 * span :])
    for n in range(beside.shape[0] // tok):
        rows = jnp.transpose(beside[n * tok : (n + 1) * tok, :])
        for h in range(heads):
            logit_ref[n, h : h + 1, :] = rows[h : h + 1, :] + bias_ref[h]


def projected(x, weights, gain, bias, heads, tok):
    tokens, width = x.shape
    span = (weights.shape[1] - 128) // 4
    blocks = tokens // tok
    some = 2 if blocks % 2 == 0 else 1
    wide, narrow = (pl.BlockSpec((some * tok, n), lambda c: (c, 0)) for n in (width, span))
    whole = lambda c: (0, 0)
    return run(
        functools.partial(project, heads, tok), blocks // some, (bias, x, weights, gain),
        [SCALARS, wide, pl.BlockSpec(weights.shape, whole), pl.BlockSpec((1, width), whole)],
        (shape((tokens, width), BF16), shape((tokens, span), BF16),
         shape((tokens, span), BF16), shape((tokens, span), BF16), shape((tokens, span), F32),
         shape((blocks, heads, tok), F32)),
        [wide, narrow, narrow, narrow, narrow, pl.BlockSpec((some, heads, tok), lambda c: (c, 0, 0))], [],
        2 * tokens * width * weights.shape[1])


def norm_in(tensor, gain_vec):
    return tensor * lax.rsqrt(jnp.mean(tensor * tensor, axis=-1, keepdims=True) + EPS) * gain_vec


def pick(x, index, axis=0):
    return lax.dynamic_index_in_dim(x, index, axis, keepdims=False)


def place(buffer, piece, index, axis=0):
    return lax.dynamic_update_index_in_dim(buffer, piece, index, axis)


def add(left, *others):
    total = left.astype(F32)
    for other in others:
        total = total + other.astype(F32)
    return total.astype(left.dtype)


def to_row(x):
    cores, rows = lax.axis_size("wid"), x.shape[0]
    me = lax.axis_index("wid")
    if cores == rows == 2:
        got = lax.ppermute(pick(x, 1 - me), "wid", [(0, 1), (1, 0)])
        mine = pick(x, me)
        return jnp.concatenate([jnp.where(me == 0, mine, got), jnp.where(me == 0, got, mine)], axis=0)
    every = pick(lax.all_gather(x, "wid", axis=0, tiled=False), me // (cores // rows), 1)
    return every.reshape((-1,) + x.shape[2:])


def from_row(x, rows):
    cores = lax.axis_size("wid")
    me = lax.axis_index("wid")
    parts = x.reshape((cores, x.shape[0] // cores) + x.shape[1:])
    if cores == rows == 2:
        got = lax.ppermute(pick(parts, 1 - me), "wid", [(0, 1), (1, 0)])
        mine = pick(parts, me)
        return jnp.stack([jnp.where(me == 0, mine, got), jnp.where(me == 0, got, mine)], axis=0)
    return lax.all_to_all(parts, "wid", 0, 0, tiled=True)[:: cores // rows]


def choose(parts, index):
    return lax.select_n(index.astype(jnp.int32), *parts)


def exchange(blocks, axis):
    count, me = lax.axis_size(axis), lax.axis_index(axis)
    got = [choose(blocks, me)]
    for k in range(1, count):
        sent = choose(blocks, lax.rem(me + k, count))
        got.append(lax.ppermute(sent, axis, [(i, (i + k) % count) for i in range(count)]))
    return got


def exchange_rows(x, axis):
    count, me = lax.axis_size(axis), lax.axis_index(axis)
    sent = together(*[pick(x, lax.rem(me + k, count)) for k in range(1, count)])
    return [pick(x, me)] + [lax.ppermute(sent[k - 1], axis, [(i, (i + k) % count) for i in range(count)])
                            for k in range(1, count)]


def by_source(got, axis):
    count, me = lax.axis_size(axis), lax.axis_index(axis)
    return [choose(got, lax.rem(me - j + count, count)) for j in range(count)]


def pairs(count, flip):
    return [(i, i ^ flip) for i in range(count)]


def gather_near(x, axis):
    if lax.axis_size(axis) != 4:
        return (x,)
    return x, lax.ppermute(x, axis, pairs(4, 1)), lax.ppermute(x, axis, pairs(4, 2))


def gather_far(near, axis):
    if len(near) == 1:
        return near
    x, one, two = near
    half = x.shape[0] // 2
    return x, one, two, lax.ppermute(one[:half], axis, pairs(4, 2)), lax.ppermute(two[half:], axis, pairs(4, 1))


def gather_end(far, axis):
    if len(far) == 1:
        return lax.all_gather(far[0], axis, axis=0, tiled=False)
    x, one, two, top, low = far
    me = lax.axis_index(axis)
    out = jnp.zeros((4,) + x.shape, x.dtype)
    out = place(place(place(out, x, me), one, me ^ 1), two, me ^ 2)
    return place(out, jnp.concatenate([top, low], axis=0), me ^ 3)


def square_gather(x, axis):
    return gather_end(gather_far(gather_near(x, axis), axis), axis)


def by_distance(far):
    x, one, two, top, low = far
    return x, jnp.concatenate([one, two], axis=0), jnp.concatenate([top, low], axis=0)


def sum_far(far, axis):
    half = far.shape[0] // 2
    return lax.ppermute(far[:half], axis, pairs(4, 2)), lax.ppermute(far[half:], axis, pairs(4, 1))


def sum_near(one, two, came, axis):
    half = one.shape[0] // 2
    one = jnp.concatenate([add(one[:half], came[0]), one[half:]], axis=0)
    two = jnp.concatenate([two[:half], add(two[half:], came[1])], axis=0)
    one, two = together(one, two)
    return lax.ppermute(one, axis, pairs(4, 1)), lax.ppermute(two, axis, pairs(4, 2))


def from_cores(x):
    cores = lax.axis_size("wid")
    return jnp.stack([lax.ppermute(x, "wid", pairs(cores, n)) for n in range(1, cores)], axis=0)


def core_sum(own, other):
    cores = lax.axis_size("wid")
    return add(own, *[lax.ppermute(other[n - 1 : n], "wid", pairs(cores, n)) for n in range(1, cores)])


def together(*values):
    return lax.optimization_barrier(values)


def per_device(layer_in, segment_ids, out_grad, gain_attn, w_query, w_key, w_value, w_dir, w_beta,
               b_beta, w_out, gain_mlp, w_gate, w_up, w_down):
    n_dp, n_hid, n_wid = (lax.axis_size(axis) for axis in ("dp", "hid", "wid"))
    row_count, tok, width = layer_in.shape
    heads = b_beta.shape[0]
    own_heads = heads // n_hid
    span = width // n_hid
    shard = w_query.shape[0]
    held = n_wid * tok
    copies = n_wid // row_count
    my_hid, my_dp = lax.axis_index("hid"), lax.axis_index("dp")
    side = 128
    columns = 4 * span + side

    row_own = to_row(layer_in)
    row_own, w_query, w_key, w_value, w_dir, w_beta, w_out, w_gate, w_up, w_down, out_grad = together(
        row_own, w_query, w_key, w_value, w_dir, w_beta, w_out, w_gate, w_up, w_down, out_grad)
    row_in = lax.all_gather(row_own, "hid", axis=0, tiled=True)

    down_t = w_down.T
    ff_rows, ff_cols = down_t.shape
    part = ff_cols // n_dp

    spare = side // 2
    ride = n_wid == row_count == 2 and own_heads + 2 <= spare and shard * spare >= held
    seg_rows = to_row(segment_ids).astype(BF16) if ride else jnp.zeros((held,), BF16)
    seg_rows = jnp.pad(seg_rows[: shard * spare], (0, max(0, shard * spare - held))).reshape(shard, spare)
    blank = jnp.zeros((shard, spare - own_heads - 2), BF16)
    blocks = []
    for j in range(n_hid):
        at = slice(j * span, (j + 1) * span)
        blocks.append(jnp.concatenate(
            [w_query[:, at], w_key[:, at], w_value[:, at], w_dir[:, at], w_beta[:, j * own_heads : (j + 1) * own_heads],
             gain_attn[:, None], gain_mlp[:, None], blank, seg_rows], axis=1))
    cat = exchange(blocks, "hid")
    segs = [x[:, columns - spare :].reshape(-1)[:held].astype(jnp.int32) for x in cat]
    grad_b = out_grad.reshape(row_count * tok, width)
    cat, grads = together(cat, gather_near(grad_b, "dp"))
    cat = gather_near(jnp.stack(cat, axis=0), "dp")
    wout = exchange([w_out] * n_hid, "hid")
    cut = [jnp.stack([x[:, j * part : (j + 1) * part] for x in (w_gate, w_up, down_t)]) for j in range(n_dp)]
    cat, cut = together(cat, cut)
    cat = gather_end(gather_far(cat, "dp"), "dp")
    grads = by_distance(gather_far(grads, "dp"))
    ff = [choose(cut, my_dp)]
    for r in range(1, n_dp):
        ff.append(lax.ppermute(choose(cut, my_dp ^ r), "dp", pairs(n_dp, r)))
    cat, gains = gathered_rows(cat[None], from_cores(cat), side)
    bias_own = lax.dynamic_slice_in_dim(b_beta, my_hid * own_heads, own_heads, 0).astype(F32)

    row_in, cat, ff, wout, grads, segs = together(row_in, cat, ff, wout, grads, segs)
    wout = gather_near(jnp.stack(wout, axis=0), "dp")
    ff = lax.all_gather(jnp.stack(ff, axis=0), "hid", axis=0, tiled=False)
    gain_one, gain_two = gains[own_heads], gains[own_heads + 1]
    if ride:
        segs = jnp.concatenate(by_source(segs, "hid"), axis=0)
    else:
        segs = lax.all_gather(segment_ids, ("hid", "wid"), axis=0, tiled=False)
        segs = pick(segs, lax.axis_index("wid") // copies, 1).reshape(-1)
    act_one, query, key, value, raw, logits = projected(row_in, cat, gain_one[None], bias_own, own_heads, tok)
    raw, wout = together(raw, wout)
    wout = gather_far(wout, "dp")
    local = attention_local(query, key, raw, logits, tok)
    att, saved = attention_cross(query, key, value, raw, logits, segs, local, tok)
    att, wout = together(att, wout)
    att = exchange([att[j * held : (j + 1) * held] for j in range(n_hid)], "hid")
    wout = gather_end(wout, "dp")
    wout_full, _ = gathered_rows(wout[None], from_cores(wout), 0)
    att, wout_full = together(att, wout_full)
    att = from_row(jnp.concatenate(by_source(att, "hid"), axis=1), row_count)
    att = att.reshape(row_count * tok, width)

    layer_f = layer_in.astype(F32).reshape(row_count * tok, width)
    middle = layer_f + mm(att, wout_full)
    act_two = norm_in(middle, gain_two).astype(BF16)
    act_two, ff = together(act_two, ff)
    ff_own, ff_other = ff[:, None], jnp.moveaxis(from_cores(ff), 0, 1)
    near = gather_near(act_two, "dp")
    own = feed_forward(act_two, grads[0], ff_own, ff_other)
    own, near = together(own, near)
    far = gather_far(near, "dp")
    acts = by_distance(far)
    mid = feed_forward(acts[1], grads[1], ff_own, ff_other)
    mid, end = together(mid, acts[2])
    end = feed_forward(end, grads[2], ff_own, ff_other)
    tokens = row_count * tok
    came = sum_far(end[1], "dp")
    near = sum_near(mid[1][:tokens], mid[1][tokens:], came, "dp")
    own, mid, end, near_sent = together(own, mid, end, came)
    g_own, g_other = feed_forward_weights(
        (act_two, *acts[1:]), grads, [(x[2], x[3], x[4]) for x in (own, mid, end)], ff_own, ff_other)
    near, g_own, g_other = together(near, g_own, g_other)
    d_act = add(own[1], *near)

    _, pull_two = jax.vjp(norm_in, middle, gain_two)
    d_mid_norm, _ = pull_two(d_act.astype(F32))
    d_middle = grad_b.astype(F32) + d_mid_norm
    d_branch = d_middle.astype(BF16)
    d_att = mm(d_branch, wout_full, NT).astype(BF16).reshape(row_count, tok, width)
    d_att = to_row(d_att)
    d_att, att = together(d_att, att)
    d_att = exchange([d_att[:, j * span : (j + 1) * span] for j in range(n_hid)], "hid")
    ff_grads = core_sum(jnp.moveaxis(g_own, 1, 0), jnp.moveaxis(g_other, 1, 0))[0]
    wout_rows = row_gradients(att, d_branch, n_dp, n_hid, n_wid)
    d_att, wout_rows, ff_grads = together(d_att, wout_rows, ff_grads)
    ff_grads = lax.psum_scatter(ff_grads, "hid", scatter_dimension=0, tiled=False)
    d_att = jnp.concatenate(by_source(d_att, "hid"), axis=0)
    my = lambda x, r: pick(x, my_dp ^ r)
    wout_sum = core_sum(*wout_rows)[0]
    wout_came = sum_far(my(wout_sum, 3), "dp")

    crossed = attention_backward_cross(saved, d_att, tok)
    crossed, wout_came, mlp_far = together(crossed, wout_came, end[0])
    wout_grad = sum_near(my(wout_sum, 1), my(wout_sum, 2), wout_came, "dp")
    mlp_came = sum_far(mlp_far, "dp")
    dv, *crossed = crossed
    d_cat = attention_backward_local(saved, dv, crossed, tok, side)
    d_gain_two = jnp.sum(d_act.astype(F32) * norm_in(middle, 1.0), axis=0, keepdims=True)
    bias_grad = jnp.sum(d_cat[:, 4 * span : 4 * span + own_heads].astype(F32), axis=0)
    once = lax.axis_index("wid") % copies == 0
    d_act_one, *cat_grad = input_gradients(act_one, d_cat, cat, d_gain_two, bias_grad, once, n_dp, n_hid, n_wid)
    d_act_one, cat_grad, wout_grad, mlp_came = together(d_act_one, cat_grad, wout_grad, mlp_came)
    d_parts = d_act_one.reshape(n_hid, held, width)
    first_half = exchange_rows(d_parts[:, : held // 2], "hid")
    last_half = exchange_rows(d_parts[:, held // 2 :], "hid")
    wout_grad = add(my(wout_sum, 0), *wout_grad)
    grad_wout = lax.psum_scatter(wout_grad, "hid", scatter_dimension=0, tiled=False).astype(F32)
    cat_sum = core_sum(*cat_grad)[0]
    cat_came = sum_far(my(cat_sum, 3), "dp")
    ff_got = [ff_grads[0]]
    for r in range(1, n_dp):
        ff_got.append(lax.ppermute(ff_grads[r], "dp", pairs(n_dp, r)))
    cat_came, ff_got, first_half = together(cat_came, ff_got, first_half)
    cat_grad = sum_near(my(cat_sum, 1), my(cat_sum, 2), cat_came, "dp")
    cat_grad, last_half = together(cat_grad, last_half)
    cat_grad = add(my(cat_sum, 0), *cat_grad)
    mlp = sum_near(mid[0][:tokens], mid[0][tokens:], mlp_came, "dp")
    cat_got = exchange([cat_grad[j] for j in range(n_hid)], "hid")
    d_sum = jnp.concatenate([add(*first_half), add(*last_half)], axis=0)
    d_sum = from_row(d_sum, row_count).reshape(row_count * tok, width).astype(F32)
    grad_gate, grad_up, grad_down = laid_ff(ff_got)
    *weight_grads, tails = laid_columns(cat_got, side)
    grad_beta = tails[:, :, :own_heads].transpose(1, 0, 2).reshape(shard, heads)
    gain_grads = jnp.sum(tails[:, :, own_heads : own_heads + 2], axis=0)
    grad_bias = tails[:, :own_heads, own_heads + 2].reshape(heads)

    layer_out = (middle + add(own[0], *mlp).astype(F32)).astype(BF16)
    _, pull_one = jax.vjp(lambda t: norm_in(t, gain_one), layer_f)
    grad_in = (d_middle + pull_one(d_sum)[0]).astype(BF16)

    return (
        layer_out.reshape(layer_in.shape), grad_in.reshape(layer_in.shape), gain_grads[:, 0],
        *weight_grads, grad_beta, grad_bias,
        grad_wout, gain_grads[:, 1], grad_gate, grad_up, grad_down,
    )


def solution(mesh):
    in_specs = (
        P("dp", ("hid", "wid"), None),
        P("dp", ("hid", "wid")),
        P("dp", ("hid", "wid"), None),
        P(("dp", "hid", "wid")),
        P(("dp", "hid", "wid"), None),
        P(("dp", "hid", "wid"), None),
        P(("dp", "hid", "wid"), None),
        P(("dp", "hid", "wid"), None),
        P(("dp", "hid", "wid"), None),
        P(),
        P(("dp", "hid", "wid"), None),
        P(("dp", "hid", "wid")),
        P(("dp", "wid"), "hid"),
        P(("dp", "wid"), "hid"),
        P("hid", ("dp", "wid")),
    )
    out_specs = (
        P("dp", ("hid", "wid"), None),
        P("dp", ("hid", "wid"), None),
        P(("dp", "hid", "wid")),
        P(("dp", "hid", "wid"), None),
        P(("dp", "hid", "wid"), None),
        P(("dp", "hid", "wid"), None),
        P(("dp", "hid", "wid"), None),
        P(("dp", "hid", "wid"), None),
        P(),
        P(("dp", "hid", "wid"), None),
        P(("dp", "hid", "wid")),
        P(("dp", "wid"), "hid"),
        P(("dp", "wid"), "hid"),
        P("hid", ("dp", "wid")),
    )
    return jax.shard_map(
        per_device, mesh=mesh, in_specs=in_specs, out_specs=out_specs, check_vma=False
    )
```

```python
import functools
import math

import jax
import jax.numpy as jnp
from jax import lax
from jax.experimental import pallas as pl
from jax.experimental.pallas import tpu as pltpu
from jax.sharding import PartitionSpec as P

EPS = 1e-06
NEG = -1e30
F32 = jnp.float32
BF16 = jnp.bfloat16
NN = ((1,), (0,))
NT = ((1,), (1,))
TN = ((0,), (0,))
VMEM_BYTES = 56 * 1024 * 1024
SOME = 2


def mm(left, right, dims=NN):
    return lax.dot_general(left, right, (dims, ((), ())), preferred_element_type=F32)


def halves(x):
    if x.dtype == BF16:
        return (x,)
    top = x.astype(BF16)
    return (top, (x - top.astype(F32)).astype(BF16))


def dot(left, right, dims):
    picked = [(a, b) for a in range(len(left)) for b in range(len(right)) if a + b < 2]
    if len(picked) == 1:
        return mm(left[0], right[0], dims)
    x = jnp.concatenate([left[a] for a, _ in picked], axis=dims[0][0])
    y = jnp.concatenate([right[b] for _, b in picked], axis=dims[1][0])
    return mm(x, y, dims)


def iotas(size):
    rows = lax.broadcasted_iota(jnp.int32, (size, size), 0)
    cols = lax.broadcasted_iota(jnp.int32, (size, size), 1)
    return rows, cols


def unit_dirs(raw):
    inv = lax.rsqrt(jnp.sum(raw * raw, axis=-1, keepdims=True) + EPS)
    return raw * inv, inv


def local_forward(heads, size, q_ref, k_ref, raw_ref, logit_ref, qin_ref, kout_ref, ptop_ref, plow_ref,
                  intra_ref, t_ref, e_ref, cm_ref, s_ref):
    width = q_ref.shape[1] // heads
    rows, cols = iotas(size)
    strict, lower, diag = rows > cols, rows >= cols, rows == cols
    apart = rows ^ cols
    some = range(q_ref.shape[0] // size)
    at = [(slice(n * size, (n + 1) * size), slice(h * width, (h + 1) * width)) for n in some for h in range(heads)]
    wide = [(slice(n * width, (n + 1) * width), slice(h * width, (h + 1) * width)) for n in some for h in range(heads)]
    every = range(len(at))
    betas = [2.0 * jax.nn.sigmoid(logit_ref[n, h : h + 1, :]) for n in some for h in range(heads)]
    q, k = [q_ref[a] for a in at], [k_ref[a] for a in at]
    ws = [halves(unit_dirs(raw_ref[a])[0]) for a in at]
    gram = [jnp.where(strict, dot(w, w, NT), 0.0) for w in ws]
    beta = [jnp.where(diag, b, 0.0) for b in betas]
    beta_col = [jnp.sum(b, axis=1, keepdims=True) for b in beta]
    t = [beta[u] - jnp.where(apart == 1, beta_col[u] * gram[u] * betas[u], 0.0) for u in every]
    shift = 1
    while (1 << shift) < size:
        near = (apart >> shift) == 1
        part = [halves(jnp.where(near, g, 0.0)) for g in gram]
        ts = [halves(x) for x in t]
        once = [dot(ts[u], part[u], NN) for u in every]
        t = [t[u] - dot(halves(once[u]), ts[u], NN) for u in every]
        shift += 1
    ts = [halves(x) for x in t]
    bs = [halves(jnp.where(lower, dot((q[u],), ws[u], NT), 0.0)) for u in every]
    ms = [halves(jnp.where(strict, dot(ws[u], (k[u],), NT), 0.0)) for u in every]
    e = [dot(ts[u], ms[u], NN) for u in every]
    s = [dot(ts[u], ws[u], NN) for u in every]
    cm = [dot(bs[u], ts[u], NN) for u in every]
    es = [halves(x) for x in e]
    for u in every:
        t_ref[at[u]], e_ref[at[u]], cm_ref[at[u]], s_ref[at[u]] = t[u], e[u], cm[u], s[u]
        intra_ref[at[u]] = dot((q[u],), (k[u],), NT) - dot(bs[u], es[u], NN)
        qin_ref[at[u]] = (q[u].astype(F32) - dot(halves(cm[u]), ws[u], NN)).astype(BF16)
        kout_ref[at[u]] = (k[u].astype(F32) - dot(es[u], ws[u], TN)).astype(BF16)
        step = jnp.where(diag, 1.0, 0.0) - dot(ws[u], halves(s[u]), TN)
        ptop_ref[wide[u]], plow_ref[wide[u]] = halves(step)


def cross_forward(heads, group, scale, qin_ref, kout_ref, ptop_ref, plow_ref, intra_ref, v_ref,
                  segc_ref, segr_ref, out_ref, prob_ref, keep_ref, frame, score):
    size = qin_ref.shape[0]
    width = qin_ref.shape[1] // heads
    total = v_ref.shape[0]
    wide = group * size
    c = pl.program_id(0)
    parts = [slice(g * wide, (g + 1) * wide) for g in range(total // wide)]
    at = [slice(h * width, (h + 1) * width) for h in range(heads)]
    every = range(heads)

    @pl.when(c == 0)
    def _():
        frame[...] = jnp.zeros_like(frame)
        score[...] = jnp.full_like(score, NEG)

    rows, cols = iotas(size)
    own = pl.multiple_of(c * size, size)
    seg = segc_ref[...]
    for g, part in enumerate(parts):

        @pl.when(g * group < c)
        def _():
            raw = [mm(qin_ref[:, at[h]], frame[h, part, :], NT) for h in every]
            place = lax.broadcasted_iota(jnp.int32, (size, wide), 1) + g * wide
            permit = (place < own) & (seg == segr_ref[:, part])
            for h in every:
                score[h, :, part] = jnp.where(permit, scale * raw[h], NEG)

    permit = (rows >= cols) & (seg == segr_ref[:, pl.ds(own, size)])
    for h in every:
        score[h, :, pl.ds(own, size)] = jnp.where(permit, scale * intra_ref[:, at[h]], NEG)
    top = [jnp.max(score[h], axis=-1, keepdims=True) for h in every]
    e = [jnp.exp(score[h] - top[h]) for h in every]
    inv = [1.0 / jnp.sum(x, axis=-1, keepdims=True) for x in e]
    for h in every:
        prob_ref[0, h] = (e[h] * inv[h]).astype(BF16)
    for h in every:
        out_ref[:, at[h]] = mm(prob_ref[0, h], v_ref[:, at[h]]).astype(BF16)
        keep_ref[0, h] = frame[h]
    for g, part in enumerate(parts):

        @pl.when(g * group < c)
        def _():
            moved = [dot((frame[h, part, :],), (ptop_ref[:, at[h]], plow_ref[:, at[h]]), NT) for h in every]
            for h in every:
                frame[h, part, :] = moved[h].astype(BF16)

    for h in every:
        frame[h, pl.ds(own, size), :] = kout_ref[:, at[h]]


def cross_backward(heads, group, scale, grad_ref, v_ref, prob_ref, keep_ref, qin_ref, ptop_ref,
                   plow_ref, dqin_ref, dintra_ref, dkout_ref, dstep_ref, dv_ref, carry, dvals, ds_ref):
    size = grad_ref.shape[0]
    width = grad_ref.shape[1] // heads
    total = v_ref.shape[0]
    wide = group * size
    c = pl.num_programs(0) - 1 - pl.program_id(0)
    parts = [slice(g * wide, (g + 1) * wide) for g in range(total // wide)]
    at = [slice(h * width, (h + 1) * width) for h in range(heads)]
    every = range(heads)

    @pl.when(pl.program_id(0) == 0)
    def _():
        carry[...] = jnp.zeros_like(carry)
        dvals[...] = jnp.zeros_like(dvals)

    own = pl.multiple_of(c * size, size)
    dp = [mm(grad_ref[:, at[h]], v_ref[:, at[h]], NT) for h in every]
    pf = [prob_ref[0, h].astype(F32) for h in every]
    delta = [jnp.sum(pf[h] * dp[h], axis=-1, keepdims=True) for h in every]
    for h in every:
        ds_ref[h] = (pf[h] * (dp[h] - delta[h])).astype(BF16)
    low = [carry[h].astype(BF16) for h in every]
    dqin = [mm(ds_ref[h], keep_ref[0, h]) for h in every]
    dstep = [mm(low[h], keep_ref[0, h], TN) for h in every]
    for h in every:
        dqin_ref[:, at[h]] = scale * dqin[h]
        dstep_ref[:, at[h]] = dstep[h]
        dintra_ref[:, at[h]] = ds_ref[h, :, pl.ds(own, size)]
        dkout_ref[:, at[h]] = carry[h, pl.ds(own, size), :]
    for g, part in enumerate(parts):

        @pl.when(g * group <= c)
        def _():
            more = [mm(prob_ref[0, h, :, part], grad_ref[:, at[h]], TN) for h in every]
            for h in every:
                dvals[h, part, :] += more[h]

        @pl.when(g * group < c)
        def _():
            fresh = [mm(ds_ref[h, :, part], qin_ref[:, at[h]], TN) for h in every]
            moved = [dot((carry[h, part, :].astype(BF16),), (ptop_ref[:, at[h]], plow_ref[:, at[h]]), NN)
                     for h in every]
            for h in every:
                carry[h, part, :] = scale * fresh[h] + moved[h]

    @pl.when(c == 0)
    def _():
        for h in every:
            dv_ref[:, at[h]] = dvals[h].astype(BF16)


def local_backward(heads, size, scale, q_ref, k_ref, raw_ref, logit_ref, t_ref, e_ref, cm_ref, s_ref,
                   dqin_ref, dintra_ref, dkout_ref, dstep_ref, dv_ref, out_ref):
    width = q_ref.shape[1] // heads
    rows, cols = iotas(size)
    strict, lower, diag = rows > cols, rows >= cols, rows == cols
    some = range(q_ref.shape[0] // size)
    units = [(n, h) for n in some for h in range(heads)]
    at = [(slice(n * size, (n + 1) * size), slice(h * width, (h + 1) * width)) for n, h in units]
    wide = [(slice(n * width, (n + 1) * width), slice(h * width, (h + 1) * width)) for n, h in units]
    every = range(len(units))
    span = heads * width
    out = lambda u, part: (at[u][0], slice(part * span + units[u][1] * width, part * span + (units[u][1] + 1) * width))
    q, k = [(q_ref[a],) for a in at], [(k_ref[a],) for a in at]
    both = [unit_dirs(raw_ref[a]) for a in at]
    betas = [2.0 * jax.nn.sigmoid(logit_ref[n, h : h + 1, :]) for n, h in units]
    ws = [halves(w) for w, _ in both]
    ts, es, cms, ss = ([halves(ref[a]) for a in at] for ref in (t_ref, e_ref, cm_ref, s_ref))
    dintra = [(dintra_ref[a],) for a in at]
    dqs, dks = [halves(dqin_ref[a]) for a in at], [halves(dkout_ref[a]) for a in at]
    dps = [halves(dstep_ref[a]) for a in wide]
    b = [halves(jnp.where(lower, dot(q[u], ws[u], NT), 0.0)) for u in every]
    d_s = [halves(-dot(ws[u], dps[u], NN)) for u in every]
    d_e = [halves(-(dot(ws[u], dks[u], NT) + scale * dot(b[u], dintra[u], TN))) for u in every]
    d_cm = [halves(-dot(dqs[u], ws[u], NT)) for u in every]
    y_s = [dot(ts[u], d_s[u], TN) for u in every]
    y_e = [dot(ts[u], d_e[u], TN) for u in every]
    y_c = [dot(d_cm[u], ts[u], NT) for u in every]
    d_x = [-(dot(halves(y_s[u]), ss[u], NT) + dot(halves(y_e[u]), es[u], NT) + dot(cms[u], halves(y_c[u]), TN))
           for u in every]
    d_b = [halves(jnp.where(lower, y_c[u] - scale * dot(dintra[u], es[u], NT), 0.0)) for u in every]
    d_m = [halves(jnp.where(strict, y_e[u], 0.0)) for u in every]
    d_a = [halves(jnp.where(strict, d_x[u], 0.0)) for u in every]
    for u in every:
        a = at[u]
        out_ref[out(u, 0)] = (dqin_ref[a] + scale * dot(dintra[u], k[u], NN) + dot(d_b[u], ws[u], NN)).astype(BF16)
        out_ref[out(u, 1)] = (dkout_ref[a] + scale * dot(dintra[u], q[u], TN) + dot(d_m[u], ws[u], TN)).astype(BF16)
    d_w = [y_s[u] - dot(ss[u], dps[u], NT) - dot(es[u], dks[u], NN) - dot(cms[u], dqs[u], TN)
           + dot(d_b[u], q[u], TN) + dot(d_m[u], k[u], NN) + dot(d_a[u], ws[u], NN) + dot(d_a[u], ws[u], TN)
           for u in every]
    for u in every:
        raw, inv = raw_ref[at[u]], both[u][1]
        draw = inv * d_w[u] - raw * (inv * inv * inv) * jnp.sum(raw * d_w[u], axis=-1, keepdims=True)
        out_ref[out(u, 3)] = draw.astype(BF16)
    out_ref[:, 2 * span : 3 * span] = dv_ref[...]
    side = out_ref.shape[1] - 4 * span
    for n in some:
        lines = []
        for h in range(heads):
            u = n * heads + h
            at_diag = jnp.sum(jnp.where(diag, d_x[u], 0.0), axis=0, keepdims=True)
            lines.append(-at_diag * (1.0 - 0.5 * betas[u]) / betas[u])
        lines.append(jnp.zeros((side - heads, size), F32))
        out_ref[n * size : (n + 1) * size, 4 * span :] = jnp.transpose(jnp.concatenate(lines, axis=0)).astype(BF16)


def run(body, grid, inputs, in_specs, outputs, out_specs, scratch, flops):
    return pl.pallas_call(
        body, grid=(grid,), in_specs=in_specs, out_specs=out_specs, out_shape=outputs,
        scratch_shapes=scratch,
        compiler_params=pltpu.CompilerParams(
            dimension_semantics=("arbitrary",), vmem_limit_bytes=VMEM_BYTES),
        cost_estimate=pl.CostEstimate(
            flops=flops, transcendentals=0,
            bytes_accessed=sum(x.size * x.dtype.itemsize for x in (*inputs, *outputs))),
    )(*inputs)


def shape(dims, dtype):
    return jax.ShapeDtypeStruct(dims, dtype)


def group_of(blocks):
    return 4 if blocks % 4 == 0 else 1


def attention_local(q, k, raw, logits, size):
    tokens, width = q.shape
    blocks, heads, _ = logits.shape
    head = width // heads
    some = SOME if blocks % SOME == 0 else 1
    block = pl.BlockSpec((some * size, width), lambda c: (c, 0))
    square = pl.BlockSpec((some * head, width), lambda c: (c, 0))
    logit_block = pl.BlockSpec((some, heads, size), lambda c: (c, 0, 0))
    f, b = shape((tokens, width), F32), shape((tokens, width), BF16)
    stepped = shape((blocks * head, width), BF16)
    return run(
        functools.partial(local_forward, heads, size), blocks // some, (q, k, raw, logits),
        [block, block, block, logit_block], (b, b, stepped, stepped, f, f, f, f, f),
        [block, block, square, square, block, block, block, block, block], [],
        blocks * heads * 62 * 2 * size * size * head)


def attention_cross(q, k, v, raw, logits, segments, local, size):
    qin, kout, ptop, plow, intra, t, e, cm, s = local
    tokens, width = q.shape
    blocks, heads, _ = logits.shape
    head = width // heads
    block = pl.BlockSpec((size, width), lambda c: (c, 0))
    square = pl.BlockSpec((head, width), lambda c: (c, 0))
    b = shape((tokens, width), BF16)
    group = group_of(blocks)
    whole = pl.BlockSpec((tokens, width), lambda c: (0, 0))
    wide_prob = pl.BlockSpec((1, heads, size, tokens), lambda c: (c, 0, 0, 0))
    wide_keep = pl.BlockSpec((1, heads, tokens, head), lambda c: (c, 0, 0, 0))
    out, prob, keep = run(
        functools.partial(cross_forward, heads, group, 1.0 / math.sqrt(head)), blocks,
        (qin, kout, ptop, plow, intra, v, segments.reshape(tokens, 1), segments.reshape(1, tokens)),
        [block, block, square, square, block, whole,
         pl.BlockSpec((size, 1), lambda c: (c, 0)), pl.BlockSpec((1, tokens), lambda c: (0, 0))],
        (b, shape((blocks, heads, size, tokens), BF16), shape((blocks, heads, tokens, head), BF16)),
        [block, wide_prob, wide_keep],
        [pltpu.VMEM((heads, tokens, head), BF16), pltpu.VMEM((heads, size, tokens), F32)],
        blocks * heads * 4 * 2 * size * tokens * head)
    return out, (q, k, v, raw, logits, qin, ptop, plow, t, e, cm, s, prob, keep)


def attention_backward_cross(saved, grad, size):
    q, k, v, raw, logits, qin, ptop, plow, t, e, cm, s, prob, keep = saved
    tokens, width = q.shape
    blocks, heads, _ = logits.shape
    head = width // heads
    scale = 1.0 / math.sqrt(head)
    back = lambda c: (blocks - 1 - c, 0)
    block = pl.BlockSpec((size, width), back)
    square = pl.BlockSpec((head, width), back)
    whole = pl.BlockSpec((tokens, width), lambda c: (0, 0))
    wide_prob = pl.BlockSpec((1, heads, size, tokens), lambda c: (blocks - 1 - c, 0, 0, 0))
    wide_keep = pl.BlockSpec((1, heads, tokens, head), lambda c: (blocks - 1 - c, 0, 0, 0))
    f, b = shape((tokens, width), F32), shape((tokens, width), BF16)
    dqin, dintra, dkout, dstep, dv = run(
        functools.partial(cross_backward, heads, group_of(blocks), scale), blocks,
        (grad, v, prob, keep, qin, ptop, plow),
        [block, whole, wide_prob, wide_keep, block, square, square],
        (f, b, f, shape((blocks * head, width), F32), b),
        [block, block, block, square, whole],
        [pltpu.VMEM((heads, tokens, head), F32), pltpu.VMEM((heads, tokens, head), F32),
         pltpu.VMEM((heads, size, tokens), BF16)],
        blocks * heads * 7 * 2 * size * tokens * head)
    return dv, dqin, dintra, dkout, dstep


def attention_backward_local(saved, dv, crossed, size, side):
    q, k, v, raw, logits, qin, ptop, plow, t, e, cm, s, prob, keep = saved
    tokens, width = q.shape
    blocks, heads, _ = logits.shape
    head = width // heads
    scale = 1.0 / math.sqrt(head)
    some = SOME if blocks % SOME == 0 else 1
    block = pl.BlockSpec((some * size, width), lambda c: (c, 0))
    square = pl.BlockSpec((some * head, width), lambda c: (c, 0))
    logit_block = pl.BlockSpec((some, heads, size), lambda c: (c, 0, 0))
    return run(
        functools.partial(local_backward, heads, size, scale), blocks // some,
        (q, k, raw, logits, t, e, cm, s, *crossed, dv),
        [block, block, block, logit_block, block, block, block, block, block, block, block, square, block],
        (shape((tokens, 4 * width + side), BF16),), [pl.BlockSpec((some * size, 4 * width + side), lambda c: (c, 0))], [],
        blocks * heads * 60 * 2 * size * size * head)[0]


def ff_forward(me_ref, act_ref, grad_ref, own_ref, other_ref, mlp_ref, dact_ref, hid_ref, dgate_ref, dup_ref,
               gate_w, up_w, down_w, mlp, dact):
    tokens = act_ref.shape[0]
    cores, chips, rows = own_ref.shape[1] + other_ref.shape[1], own_ref.shape[2], own_ref.shape[4]
    tile = min(tokens, 256)

    for r in range(chips):
        for n in range(cores):
            held = own_ref.at[0, 0, r] if n == 0 else other_ref.at[0, n - 1, r]
            chip, core = me_ref[0] ^ r, me_ref[1] ^ n
            to = pl.ds(pl.multiple_of((chip * cores + core) * rows, rows), rows)
            gate_w[to, :] = held[0]
            up_w[to, :] = held[1]
            down_w[to, :] = held[2]

    @pl.when(pl.program_id(0) == 0)
    def _():
        mlp[...] = jnp.zeros_like(mlp)
        dact[...] = jnp.zeros_like(dact)

    @pl.loop(0, tokens // tile)
    def _(i):
        at = pl.ds(pl.multiple_of(i * tile, tile), tile)
        act, grad = act_ref[at, :], grad_ref[at, :]
        gate, up = mm(act, gate_w[...]), mm(act, up_w[...])
        sig = jax.nn.sigmoid(gate)
        silu = gate * sig
        hidden = (silu * up).astype(BF16)
        d_hidden = mm(grad, down_w[...])
        d_gate = (d_hidden * up * sig * (1.0 + gate * (1.0 - sig))).astype(BF16)
        d_up = (d_hidden * silu).astype(BF16)
        hid_ref[at, :] = hidden
        dgate_ref[at, :] = d_gate
        dup_ref[at, :] = d_up
        mlp[at, :] += mm(hidden, down_w[...], NT)
        dact[at, :] += mm(d_gate, gate_w[...], NT) + mm(d_up, up_w[...], NT)

    @pl.when(pl.program_id(0) == pl.num_programs(0) - 1)
    def _():
        mlp_ref[...] = mlp[...].astype(BF16)
        dact_ref[...] = dact[...].astype(BF16)


def ff_weights(me_ref, *refs):
    *ins, own_ref, other_ref = refs
    groups = [ins[5 * n : 5 * n + 5] for n in range(len(ins) // 5)]
    cores, chips, rows = own_ref.shape[1] + other_ref.shape[1], own_ref.shape[2], own_ref.shape[4]
    for d in range(chips):
        at = slice(d * cores * rows, (d + 1) * cores * rows)
        r = me_ref[0] ^ d
        gate = up = down = 0.0
        for act_ref, grad_ref, hid_ref, dgate_ref, dup_ref in groups:
            act, grad = act_ref[:, at], grad_ref[:, at]
            gate = gate + mm(act, dgate_ref[...], TN)
            up = up + mm(act, dup_ref[...], TN)
            down = down + mm(grad, hid_ref[...], TN)
        for i, part in enumerate((gate, up, down)):
            pieces = [part[w * rows : (w + 1) * rows, :].astype(BF16) for w in range(cores)]
            for n in range(cores):
                piece = pieces[0]
                for w in range(1, cores):
                    piece = jnp.where((me_ref[1] ^ n) == w, pieces[w], piece)
                if n == 0:
                    own_ref[0, 0, r, i] = piece
                else:
                    other_ref[0, n - 1, r, i] = piece


def place_self():
    return jnp.stack([lax.axis_index("dp"), lax.axis_index("wid")]).astype(jnp.int32)


SCALARS = pl.BlockSpec(memory_space=pltpu.SMEM)


def feed_forward(act, grad, own, other):
    tokens, width = act.shape
    groups, part = own.shape[0], own.shape[5]
    whole = pl.BlockSpec((tokens, width), lambda h: (0, 0))
    units = pl.BlockSpec((tokens, part), lambda h: (0, h))
    held = [pl.BlockSpec((1,) + x.shape[1:], lambda h: (h, 0, 0, 0, 0, 0)) for x in (own, other)]
    full, some = shape((tokens, width), BF16), shape((tokens, groups * part), BF16)
    flops = 6 * 2 * tokens * width * groups * part
    return run(ff_forward, groups, (place_self(), act, grad, own, other), [SCALARS, whole, whole, *held],
               (full, full, some, some, some), [whole, whole, units, units, units],
               [pltpu.VMEM((width, part), BF16)] * 3 + [pltpu.VMEM((tokens, width), F32)] * 2, flops)


def feed_forward_weights(acts, grads, saved, own, other):
    width = acts[0].shape[1]
    groups, part = own.shape[0], own.shape[5]
    values, specs = [], []
    for act, grad, some in zip(acts, grads, saved):
        values += [act, grad, *some]
        specs += [pl.BlockSpec(act.shape, lambda h: (0, 0))] * 2
        specs += [pl.BlockSpec((act.shape[0], part), lambda h: (0, h))] * 3
    held = [pl.BlockSpec((1,) + x.shape[1:], lambda h: (h, 0, 0, 0, 0, 0)) for x in (own, other)]
    return run(ff_weights, groups, (place_self(), *values), [SCALARS, *specs],
               (shape(own.shape, BF16), shape(other.shape, BF16)), held, [],
               3 * 2 * sum(x.shape[0] for x in acts) * width * groups * part)


def split_rows(me_ref, part, at, own_ref, other_ref):
    cores, shards, rows = own_ref.shape[0] + other_ref.shape[0], own_ref.shape[2], own_ref.shape[3]
    for h in range(shards):
        pieces = [part[(h * cores + w) * rows : (h * cores + w + 1) * rows, :] for w in range(cores)]
        for n in range(cores):
            piece = pieces[0]
            for w in range(1, cores):
                piece = jnp.where((me_ref[1] ^ n) == w, pieces[w], piece)
            if n == 0:
                own_ref[0, 0, h, :, at] = piece
            else:
                other_ref[n - 1, 0, h, :, at] = piece


def row_grads(me_ref, left_ref, right_ref, own_ref, other_ref):
    columns = right_ref.shape[1]
    for start in range(0, columns, 512):
        at = slice(start, min(start + 512, columns))
        split_rows(me_ref, mm(left_ref[...], right_ref[:, at], TN).astype(BF16), at, own_ref, other_ref)


def split_whole(full, chips, shards, cores, rows):
    full = full.astype(BF16).reshape(chips, shards, cores, rows, full.shape[1])
    full = jnp.take(full, lax.axis_index("wid") ^ jnp.arange(cores), axis=2).transpose(2, 0, 1, 3, 4)
    return full[:1], full[1:]


def row_gradients(left, right, chips, shards, cores):
    tokens, width = left.shape
    columns = right.shape[1]
    rows = width // (chips * shards * cores)
    if rows % 16:
        return split_whole(mm(left, right, TN), chips, shards, cores, rows)
    outs = [shape((n, chips, shards, rows, columns), BF16) for n in (1, cores - 1)]
    specs = [pl.BlockSpec((x.shape[0], 1, shards, rows, columns), lambda d: (0, d, 0, 0, 0)) for x in outs]
    return run(row_grads, chips, (place_self(), left, right),
               [SCALARS, pl.BlockSpec((tokens, width // chips), lambda d: (0, d)),
                pl.BlockSpec((tokens, columns), lambda d: (0, 0))],
               tuple(outs), specs, [], 2 * tokens * width * columns)


def input_grads(me_ref, bias_ref, left_ref, right_ref, w_ref, two_ref, din_ref, own_ref, other_ref):
    columns, side = right_ref.shape[1], 128
    heads, rows = bias_ref.shape[0], own_ref.shape[3]
    din_ref[...] = mm(right_ref[...], w_ref[...], NT).astype(BF16)
    spans = [(start, min(start + 512, columns - side)) for start in range(0, columns - side, 512)]
    gain_sum = jnp.zeros((left_ref.shape[1], 1), F32)
    for start, stop in spans + [(columns - side, columns)]:
        part = mm(left_ref[...], right_ref[:, start:stop], TN)
        weight = w_ref[:, start:stop].astype(F32)
        lane = lax.broadcasted_iota(jnp.int32, part.shape, 1)
        if stop == columns:
            gain_sum = gain_sum + jnp.sum(jnp.where(lane < heads, part * weight, 0.0), axis=1, keepdims=True)
            gain = jnp.sum(jnp.where(lane == heads, weight, 0.0), axis=1, keepdims=True)
            row = lax.rem(lax.broadcasted_iota(jnp.int32, part.shape, 0), rows)
            two = jnp.transpose(jnp.broadcast_to(two_ref[...], (side, part.shape[0])))
            part = jnp.where(lane < heads, part, 0.0) + jnp.where(lane == heads, gain_sum / gain, 0.0)
            for n in range(heads):
                part = part + jnp.where((lane == heads + 2) & (row == n), bias_ref[n], 0.0)
            part = jnp.where(me_ref[2] == 1, part, 0.0) + jnp.where(lane == heads + 1, two, 0.0)
        else:
            gain_sum = gain_sum + jnp.sum(part * weight, axis=1, keepdims=True)
            part = jnp.where(me_ref[2] == 1, part, 0.0)
        split_rows(me_ref, part.astype(BF16), slice(start, stop), own_ref, other_ref)


def input_gradients(left, right, weights, two, bias, once, chips, shards, cores):
    tokens, width = left.shape
    columns, heads = right.shape[1], bias.shape[0]
    rows = width // (chips * shards * cores)
    if rows % 16:
        full = mm(left, right, TN)
        lane = lax.broadcasted_iota(jnp.int32, (width, columns), 1) - (columns - 128)
        row = lax.broadcasted_iota(jnp.int32, (width, columns), 0) % rows
        wide = weights.astype(F32)
        gain = jnp.sum(jnp.where(lane < heads, full * wide, 0.0), axis=1, keepdims=True)
        gain = gain / wide[:, columns - 128 + heads][:, None]
        full = full + jnp.where(lane == heads, gain, 0.0)
        for n in range(heads):
            full = full + jnp.where((lane == heads + 2) & (row == n), bias[n], 0.0)
        full = jnp.where(once, full, 0.0) + jnp.where(lane == heads + 1, two.T, 0.0)
        return (mm(right, weights, NT).astype(BF16), *split_whole(full, chips, shards, cores, rows))
    outs = [shape((n, chips, shards, rows, columns), BF16) for n in (1, cores - 1)]
    specs = [pl.BlockSpec((x.shape[0], 1, shards, rows, columns), lambda d: (0, d, 0, 0, 0)) for x in outs]
    features = pl.BlockSpec((tokens, width // chips), lambda d: (0, d))
    me = jnp.concatenate([place_self(), once[None].astype(jnp.int32)])
    return run(input_grads, chips, (me, bias, left, right, weights, two),
               [SCALARS, SCALARS, features, pl.BlockSpec((tokens, columns), lambda d: (0, 0)),
                pl.BlockSpec((width // chips, columns), lambda d: (d, 0)), pl.BlockSpec((1, width // chips), lambda d: (0, d))],
               (shape((tokens, width), BF16), *outs), [features, *specs], [], 4 * tokens * width * columns)


def lay_columns(me_ref, *refs):
    *got, a_ref, b_ref, c_ref, d_ref, tail_ref = refs
    count, span = len(got), a_ref.shape[1] // len(got)
    for k, ref in enumerate(got):
        source = lax.rem(me_ref[0] - k + count, count)
        to = pl.ds(pl.multiple_of(source * span, 128), span)
        for i, out in enumerate((a_ref, b_ref, c_ref, d_ref)):
            out[:, to] = ref[:, i * span : (i + 1) * span].astype(F32)
        tail_ref[source] = ref[:, 4 * span :].astype(F32)


def laid_columns(got, side):
    count, (rows, columns) = len(got), got[0].shape
    span = (columns - side) // 4
    if rows % 16 or span % 128:
        got = by_source(got, "hid")
        whole = [jnp.concatenate([x[:, i * span : (i + 1) * span] for x in got], axis=1).astype(F32) for i in range(4)]
        return (*whole, jnp.stack([x[:, 4 * span :] for x in got]).astype(F32))
    one = pl.BlockSpec((rows, columns), lambda i: (0, 0))
    out = pl.BlockSpec((rows, count * span), lambda i: (0, 0))
    return run(lay_columns, 1, (lax.axis_index("hid")[None].astype(jnp.int32), *got), [SCALARS] + [one] * count,
               (shape((rows, count * span), F32),) * 4 + (shape((count, rows, side), F32),),
               [out] * 4 + [pl.BlockSpec((count, rows, side), lambda i: (0, 0, 0))], [], 0)


def lay_ff(me_ref, *refs):
    *got, gate_ref, up_ref, down_ref = refs
    part = got[0].shape[2]
    for r, ref in enumerate(got):
        to = pl.ds(pl.multiple_of((me_ref[0] ^ r) * part, 128), part)
        gate_ref[:, to] = ref[0].astype(F32)
        up_ref[:, to] = ref[1].astype(F32)
        down_ref[to, :] = jnp.transpose(ref[2].astype(F32))


def laid_ff(got):
    count, (_, rows, part) = len(got), got[0].shape
    outs = ((rows, count * part), (rows, count * part), (count * part, rows))
    return run(lay_ff, 1, (lax.axis_index("dp")[None].astype(jnp.int32), *got),
               [SCALARS] + [pl.BlockSpec((3, rows, part), lambda i: (0, 0, 0))] * count,
               tuple(shape(x, F32) for x in outs), [pl.BlockSpec(x, lambda i: (0, 0)) for x in outs], [], 0)


def lay_rows(me_ref, own_ref, other_ref, out_ref, *turned):
    cores, shards, rows = own_ref.shape[0] + other_ref.shape[0], own_ref.shape[2], own_ref.shape[3]
    for k in range(shards):
        h = lax.rem(me_ref[2] - k + shards, shards)
        for n in range(cores):
            to = pl.ds(pl.multiple_of((h * cores + (me_ref[1] ^ n)) * rows, rows), rows)
            out_ref[to, :] = own_ref[0, 0, k] if n == 0 else other_ref[n - 1, 0, k]
    for ref in turned:
        ref[...] = jnp.transpose(out_ref[:, -ref.shape[0] :].astype(F32))


def gathered_rows(own, other, side):
    _, chips, shards, rows, columns = own.shape
    cores = 1 + other.shape[0]
    if rows % 16:
        full = jnp.concatenate([own, other], axis=0)
        full = jnp.take(full, lax.axis_index("wid") ^ jnp.arange(cores), axis=0)
        full = jnp.take(full, (lax.axis_index("hid") - jnp.arange(shards)) % shards, axis=2)
        full = full.transpose(1, 2, 0, 3, 4).reshape(-1, columns)
        return full, (full[:, columns - side :].astype(F32).T if side else None)
    me = jnp.concatenate([place_self(), lax.axis_index("hid")[None].astype(jnp.int32)])
    specs = [pl.BlockSpec((x.shape[0], 1, shards, rows, columns), lambda d: (0, d, 0, 0, 0)) for x in (own, other)]
    size = cores * shards * rows
    outs, out_specs = [shape((chips * size, columns), BF16)], [pl.BlockSpec((size, columns), lambda d: (d, 0))]
    if side:
        outs.append(shape((side, chips * size), F32))
        out_specs.append(pl.BlockSpec((side, size), lambda d: (0, d)))
    out = run(lay_rows, chips, (me, own, other), [SCALARS, *specs], tuple(outs), out_specs, [], 0)
    return out[0], (out[1] if side else None)


def project(heads, tok, bias_ref, x_ref, w_ref, gain_ref, act_ref, q_ref, k_ref, v_ref, raw_ref, logit_ref):
    x = x_ref[...].astype(F32)
    unit = x * lax.rsqrt(jnp.mean(x * x, axis=-1, keepdims=True) + EPS)
    act_ref[...] = (unit * gain_ref[...]).astype(BF16)
    act, span = act_ref[...], q_ref.shape[1]
    for i, out in enumerate((q_ref, k_ref, v_ref, raw_ref)):
        out[...] = mm(act, w_ref[:, i * span : (i + 1) * span]).astype(out.dtype)
    beside = mm(act, w_ref[:, 4 * span :])
    for n in range(beside.shape[0] // tok):
        rows = jnp.transpose(beside[n * tok : (n + 1) * tok, :])
        for h in range(heads):
            logit_ref[n, h : h + 1, :] = rows[h : h + 1, :] + bias_ref[h]


def projected(x, weights, gain, bias, heads, tok):
    tokens, width = x.shape
    span = (weights.shape[1] - 128) // 4
    blocks = tokens // tok
    some = 2 if blocks % 2 == 0 else 1
    wide, narrow = (pl.BlockSpec((some * tok, n), lambda c: (c, 0)) for n in (width, span))
    whole = lambda c: (0, 0)
    return run(
        functools.partial(project, heads, tok), blocks // some, (bias, x, weights, gain),
        [SCALARS, wide, pl.BlockSpec(weights.shape, whole), pl.BlockSpec((1, width), whole)],
        (shape((tokens, width), BF16), shape((tokens, span), BF16),
         shape((tokens, span), BF16), shape((tokens, span), BF16), shape((tokens, span), F32),
         shape((blocks, heads, tok), F32)),
        [wide, narrow, narrow, narrow, narrow, pl.BlockSpec((some, heads, tok), lambda c: (c, 0, 0))], [],
        2 * tokens * width * weights.shape[1])


def norm_in(tensor, gain_vec):
    return tensor * lax.rsqrt(jnp.mean(tensor * tensor, axis=-1, keepdims=True) + EPS) * gain_vec


def pick(x, index, axis=0):
    return lax.dynamic_index_in_dim(x, index, axis, keepdims=False)


def place(buffer, piece, index, axis=0):
    return lax.dynamic_update_index_in_dim(buffer, piece, index, axis)


def add(left, *others):
    total = left.astype(F32)
    for other in others:
        total = total + other.astype(F32)
    return total.astype(left.dtype)


def to_row(x):
    cores, rows = lax.axis_size("wid"), x.shape[0]
    me = lax.axis_index("wid")
    if cores == rows == 2:
        got = lax.ppermute(pick(x, 1 - me), "wid", [(0, 1), (1, 0)])
        mine = pick(x, me)
        return jnp.concatenate([jnp.where(me == 0, mine, got), jnp.where(me == 0, got, mine)], axis=0)
    every = pick(lax.all_gather(x, "wid", axis=0, tiled=False), me // (cores // rows), 1)
    return every.reshape((-1,) + x.shape[2:])


def from_row(x, rows):
    cores = lax.axis_size("wid")
    me = lax.axis_index("wid")
    parts = x.reshape((cores, x.shape[0] // cores) + x.shape[1:])
    if cores == rows == 2:
        got = lax.ppermute(pick(parts, 1 - me), "wid", [(0, 1), (1, 0)])
        mine = pick(parts, me)
        return jnp.stack([jnp.where(me == 0, mine, got), jnp.where(me == 0, got, mine)], axis=0)
    return lax.all_to_all(parts, "wid", 0, 0, tiled=True)[:: cores // rows]


def choose(parts, index):
    return lax.select_n(index.astype(jnp.int32), *parts)


def exchange(blocks, axis):
    count, me = lax.axis_size(axis), lax.axis_index(axis)
    got = [choose(blocks, me)]
    for k in range(1, count):
        sent = choose(blocks, lax.rem(me + k, count))
        got.append(lax.ppermute(sent, axis, [(i, (i + k) % count) for i in range(count)]))
    return got


def exchange_rows(x, axis):
    count, me = lax.axis_size(axis), lax.axis_index(axis)
    sent = together(*[pick(x, lax.rem(me + k, count)) for k in range(1, count)])
    return [pick(x, me)] + [lax.ppermute(sent[k - 1], axis, [(i, (i + k) % count) for i in range(count)])
                            for k in range(1, count)]


def by_source(got, axis):
    count, me = lax.axis_size(axis), lax.axis_index(axis)
    return [choose(got, lax.rem(me - j + count, count)) for j in range(count)]


def pairs(count, flip):
    return [(i, i ^ flip) for i in range(count)]


def gather_near(x, axis):
    if lax.axis_size(axis) != 4:
        return (x,)
    return x, lax.ppermute(x, axis, pairs(4, 1)), lax.ppermute(x, axis, pairs(4, 2))


def gather_far(near, axis):
    if len(near) == 1:
        return near
    x, one, two = near
    half = x.shape[0] // 2
    return x, one, two, lax.ppermute(one[:half], axis, pairs(4, 2)), lax.ppermute(two[half:], axis, pairs(4, 1))


def gather_end(far, axis):
    if len(far) == 1:
        return lax.all_gather(far[0], axis, axis=0, tiled=False)
    x, one, two, top, low = far
    me = lax.axis_index(axis)
    out = jnp.zeros((4,) + x.shape, x.dtype)
    out = place(place(place(out, x, me), one, me ^ 1), two, me ^ 2)
    return place(out, jnp.concatenate([top, low], axis=0), me ^ 3)


def square_gather(x, axis):
    return gather_end(gather_far(gather_near(x, axis), axis), axis)


def by_distance(far):
    x, one, two, top, low = far
    return x, jnp.concatenate([one, two], axis=0), jnp.concatenate([top, low], axis=0)


def sum_far(far, axis):
    half = far.shape[0] // 2
    return lax.ppermute(far[:half], axis, pairs(4, 2)), lax.ppermute(far[half:], axis, pairs(4, 1))


def sum_near(one, two, came, axis):
    half = one.shape[0] // 2
    one = jnp.concatenate([add(one[:half], came[0]), one[half:]], axis=0)
    two = jnp.concatenate([two[:half], add(two[half:], came[1])], axis=0)
    one, two = together(one, two)
    return lax.ppermute(one, axis, pairs(4, 1)), lax.ppermute(two, axis, pairs(4, 2))


def from_cores(x):
    cores = lax.axis_size("wid")
    return jnp.stack([lax.ppermute(x, "wid", pairs(cores, n)) for n in range(1, cores)], axis=0)


def core_sum(own, other):
    cores = lax.axis_size("wid")
    return add(own, *[lax.ppermute(other[n - 1 : n], "wid", pairs(cores, n)) for n in range(1, cores)])


def together(*values):
    return lax.optimization_barrier(values)


def per_device(layer_in, segment_ids, out_grad, gain_attn, w_query, w_key, w_value, w_dir, w_beta,
               b_beta, w_out, gain_mlp, w_gate, w_up, w_down):
    n_dp, n_hid, n_wid = (lax.axis_size(axis) for axis in ("dp", "hid", "wid"))
    row_count, tok, width = layer_in.shape
    heads = b_beta.shape[0]
    own_heads = heads // n_hid
    span = width // n_hid
    shard = w_query.shape[0]
    held = n_wid * tok
    copies = n_wid // row_count
    my_hid, my_dp = lax.axis_index("hid"), lax.axis_index("dp")
    side = 128
    columns = 4 * span + side

    row_own = to_row(layer_in)
    row_own, w_query, w_key, w_value, w_dir, w_beta, w_out, w_gate, w_up, w_down, out_grad = together(
        row_own, w_query, w_key, w_value, w_dir, w_beta, w_out, w_gate, w_up, w_down, out_grad)
    row_in = lax.all_gather(row_own, "hid", axis=0, tiled=True)

    down_t = w_down.T
    ff_rows, ff_cols = down_t.shape
    part = ff_cols // n_dp

    spare = side // 2
    ride = n_wid == row_count == 2 and own_heads + 2 <= spare and shard * spare >= held
    seg_rows = to_row(segment_ids).astype(BF16) if ride else jnp.zeros((held,), BF16)
    seg_rows = jnp.pad(seg_rows[: shard * spare], (0, max(0, shard * spare - held))).reshape(shard, spare)
    blank = jnp.zeros((shard, spare - own_heads - 2), BF16)
    blocks = []
    for j in range(n_hid):
        at = slice(j * span, (j + 1) * span)
        blocks.append(jnp.concatenate(
            [w_query[:, at], w_key[:, at], w_value[:, at], w_dir[:, at], w_beta[:, j * own_heads : (j + 1) * own_heads],
             gain_attn[:, None], gain_mlp[:, None], blank, seg_rows], axis=1))
    cat = exchange(blocks, "hid")
    segs = [x[:, columns - spare :].reshape(-1)[:held].astype(jnp.int32) for x in cat]
    grad_b = out_grad.reshape(row_count * tok, width)
    cat, grads = together(cat, gather_near(grad_b, "dp"))
    cat = gather_near(jnp.stack(cat, axis=0), "dp")
    wout = exchange([w_out] * n_hid, "hid")
    cut = [jnp.stack([x[:, j * part : (j + 1) * part] for x in (w_gate, w_up, down_t)]) for j in range(n_dp)]
    cat, cut = together(cat, cut)
    cat = gather_end(gather_far(cat, "dp"), "dp")
    grads = by_distance(gather_far(grads, "dp"))
    ff = [choose(cut, my_dp)]
    for r in range(1, n_dp):
        ff.append(lax.ppermute(choose(cut, my_dp ^ r), "dp", pairs(n_dp, r)))
    cat, gains = gathered_rows(cat[None], from_cores(cat), side)
    bias_own = lax.dynamic_slice_in_dim(b_beta, my_hid * own_heads, own_heads, 0).astype(F32)

    row_in, cat, ff, wout, grads, segs = together(row_in, cat, ff, wout, grads, segs)
    wout = gather_near(jnp.stack(wout, axis=0), "dp")
    ff = lax.all_gather(jnp.stack(ff, axis=0), "hid", axis=0, tiled=False)
    gain_one, gain_two = gains[own_heads], gains[own_heads + 1]
    if ride:
        segs = jnp.concatenate(by_source(segs, "hid"), axis=0)
    else:
        segs = lax.all_gather(segment_ids, ("hid", "wid"), axis=0, tiled=False)
        segs = pick(segs, lax.axis_index("wid") // copies, 1).reshape(-1)
    act_one, query, key, value, raw, logits = projected(row_in, cat, gain_one[None], bias_own, own_heads, tok)
    raw, wout = together(raw, wout)
    wout = gather_far(wout, "dp")
    local = attention_local(query, key, raw, logits, tok)
    att, saved = attention_cross(query, key, value, raw, logits, segs, local, tok)
    att, wout = together(att, wout)
    att = exchange([att[j * held : (j + 1) * held] for j in range(n_hid)], "hid")
    wout = gather_end(wout, "dp")
    wout_full, _ = gathered_rows(wout[None], from_cores(wout), 0)
    att, wout_full = together(att, wout_full)
    att = from_row(jnp.concatenate(by_source(att, "hid"), axis=1), row_count)
    att = att.reshape(row_count * tok, width)

    layer_f = layer_in.astype(F32).reshape(row_count * tok, width)
    middle = layer_f + mm(att, wout_full)
    act_two = norm_in(middle, gain_two).astype(BF16)
    act_two, ff = together(act_two, ff)
    ff_own, ff_other = ff[:, None], jnp.moveaxis(from_cores(ff), 0, 1)
    near = gather_near(act_two, "dp")
    own = feed_forward(act_two, grads[0], ff_own, ff_other)
    own, near = together(own, near)
    far = gather_far(near, "dp")
    acts = by_distance(far)
    mid = feed_forward(acts[1], grads[1], ff_own, ff_other)
    mid, end = together(mid, acts[2])
    end = feed_forward(end, grads[2], ff_own, ff_other)
    tokens = row_count * tok
    came = sum_far(end[1], "dp")
    near = sum_near(mid[1][:tokens], mid[1][tokens:], came, "dp")
    own, mid, end, near_sent = together(own, mid, end, came)
    g_own, g_other = feed_forward_weights(
        (act_two, *acts[1:]), grads, [(x[2], x[3], x[4]) for x in (own, mid, end)], ff_own, ff_other)
    near, g_own, g_other = together(near, g_own, g_other)
    d_act = add(own[1], *near)

    _, pull_two = jax.vjp(norm_in, middle, gain_two)
    d_mid_norm, _ = pull_two(d_act.astype(F32))
    d_middle = grad_b.astype(F32) + d_mid_norm
    d_branch = d_middle.astype(BF16)
    d_att = mm(d_branch, wout_full, NT).astype(BF16).reshape(row_count, tok, width)
    d_att = to_row(d_att)
    d_att, att = together(d_att, att)
    d_att = exchange([d_att[:, j * span : (j + 1) * span] for j in range(n_hid)], "hid")
    ff_grads = core_sum(jnp.moveaxis(g_own, 1, 0), jnp.moveaxis(g_other, 1, 0))[0]
    wout_rows = row_gradients(att, d_branch, n_dp, n_hid, n_wid)
    d_att, wout_rows, ff_grads = together(d_att, wout_rows, ff_grads)
    ff_grads = lax.psum_scatter(ff_grads, "hid", scatter_dimension=0, tiled=False)
    d_att = jnp.concatenate(by_source(d_att, "hid"), axis=0)
    my = lambda x, r: pick(x, my_dp ^ r)
    wout_sum = core_sum(*wout_rows)[0]
    wout_came = sum_far(my(wout_sum, 3), "dp")

    crossed = attention_backward_cross(saved, d_att, tok)
    crossed, wout_came, mlp_far = together(crossed, wout_came, end[0])
    wout_grad = sum_near(my(wout_sum, 1), my(wout_sum, 2), wout_came, "dp")
    mlp_came = sum_far(mlp_far, "dp")
    dv, *crossed = crossed
    d_cat = attention_backward_local(saved, dv, crossed, tok, side)
    d_gain_two = jnp.sum(d_act.astype(F32) * norm_in(middle, 1.0), axis=0, keepdims=True)
    bias_grad = jnp.sum(d_cat[:, 4 * span : 4 * span + own_heads].astype(F32), axis=0)
    once = lax.axis_index("wid") % copies == 0
    d_act_one, *cat_grad = input_gradients(act_one, d_cat, cat, d_gain_two, bias_grad, once, n_dp, n_hid, n_wid)
    d_act_one, cat_grad, wout_grad, mlp_came = together(d_act_one, cat_grad, wout_grad, mlp_came)
    d_parts = d_act_one.reshape(n_hid, held, width)
    first_half = exchange_rows(d_parts[:, : held // 2], "hid")
    last_half = exchange_rows(d_parts[:, held // 2 :], "hid")
    wout_grad = add(my(wout_sum, 0), *wout_grad)
    grad_wout = lax.psum_scatter(wout_grad, "hid", scatter_dimension=0, tiled=False).astype(F32)
    cat_sum = core_sum(*cat_grad)[0]
    cat_came = sum_far(my(cat_sum, 3), "dp")
    ff_got = [ff_grads[0]]
    for r in range(1, n_dp):
        ff_got.append(lax.ppermute(ff_grads[r], "dp", pairs(n_dp, r)))
    cat_came, ff_got, first_half = together(cat_came, ff_got, first_half)
    cat_grad = sum_near(my(cat_sum, 1), my(cat_sum, 2), cat_came, "dp")
    cat_grad, last_half = together(cat_grad, last_half)
    cat_grad = add(my(cat_sum, 0), *cat_grad)
    mlp = sum_near(mid[0][:tokens], mid[0][tokens:], mlp_came, "dp")
    cat_got = exchange([cat_grad[j] for j in range(n_hid)], "hid")
    d_sum = jnp.concatenate([add(*first_half), add(*last_half)], axis=0)
    d_sum = from_row(d_sum, row_count).reshape(row_count * tok, width).astype(F32)
    grad_gate, grad_up, grad_down = laid_ff(ff_got)
    layer_out = (middle + add(own[0], *mlp).astype(F32)).astype(BF16)
    _, pull_one = jax.vjp(lambda t: norm_in(t, gain_one), layer_f)
    grad_in = (d_middle + pull_one(d_sum)[0]).astype(BF16)
    cat_got, grad_in, layer_out = together(cat_got, grad_in, layer_out)
    *weight_grads, tails = laid_columns(cat_got, side)
    grad_beta = tails[:, :, :own_heads].transpose(1, 0, 2).reshape(shard, heads)
    gain_grads = jnp.sum(tails[:, :, own_heads : own_heads + 2], axis=0)
    grad_bias = tails[:, :own_heads, own_heads + 2].reshape(heads)

    return (
        layer_out.reshape(layer_in.shape), grad_in.reshape(layer_in.shape), gain_grads[:, 0],
        *weight_grads, grad_beta, grad_bias,
        grad_wout, gain_grads[:, 1], grad_gate, grad_up, grad_down,
    )


def solution(mesh):
    in_specs = (
        P("dp", ("hid", "wid"), None),
        P("dp", ("hid", "wid")),
        P("dp", ("hid", "wid"), None),
        P(("dp", "hid", "wid")),
        P(("dp", "hid", "wid"), None),
        P(("dp", "hid", "wid"), None),
        P(("dp", "hid", "wid"), None),
        P(("dp", "hid", "wid"), None),
        P(("dp", "hid", "wid"), None),
        P(),
        P(("dp", "hid", "wid"), None),
        P(("dp", "hid", "wid")),
        P(("dp", "wid"), "hid"),
        P(("dp", "wid"), "hid"),
        P("hid", ("dp", "wid")),
    )
    out_specs = (
        P("dp", ("hid", "wid"), None),
        P("dp", ("hid", "wid"), None),
        P(("dp", "hid", "wid")),
        P(("dp", "hid", "wid"), None),
        P(("dp", "hid", "wid"), None),
        P(("dp", "hid", "wid"), None),
        P(("dp", "hid", "wid"), None),
        P(("dp", "hid", "wid"), None),
        P(),
        P(("dp", "hid", "wid"), None),
        P(("dp", "hid", "wid")),
        P(("dp", "wid"), "hid"),
        P(("dp", "wid"), "hid"),
        P("hid", ("dp", "wid")),
    )
    return jax.shard_map(
        per_device, mesh=mesh, in_specs=in_specs, out_specs=out_specs, check_vma=False
    )
```

```python
import functools
import math

import jax
import jax.numpy as jnp
from jax import lax
from jax.experimental import pallas as pl
from jax.experimental.pallas import tpu as pltpu
from jax.sharding import PartitionSpec as P

EPS = 1e-06
NEG = -1e30
F32 = jnp.float32
BF16 = jnp.bfloat16
NN = ((1,), (0,))
NT = ((1,), (1,))
TN = ((0,), (0,))
VMEM_BYTES = 56 * 1024 * 1024
SOME = 2


def mm(left, right, dims=NN):
    return lax.dot_general(left, right, (dims, ((), ())), preferred_element_type=F32)


def halves(x):
    if x.dtype == BF16:
        return (x,)
    top = x.astype(BF16)
    return (top, (x - top.astype(F32)).astype(BF16))


def dot(left, right, dims):
    picked = [(a, b) for a in range(len(left)) for b in range(len(right)) if a + b < 2]
    if len(picked) == 1:
        return mm(left[0], right[0], dims)
    x = jnp.concatenate([left[a] for a, _ in picked], axis=dims[0][0])
    y = jnp.concatenate([right[b] for _, b in picked], axis=dims[1][0])
    return mm(x, y, dims)


def iotas(size):
    rows = lax.broadcasted_iota(jnp.int32, (size, size), 0)
    cols = lax.broadcasted_iota(jnp.int32, (size, size), 1)
    return rows, cols


def unit_dirs(raw):
    inv = lax.rsqrt(jnp.sum(raw * raw, axis=-1, keepdims=True) + EPS)
    return raw * inv, inv


def local_forward(heads, size, q_ref, k_ref, raw_ref, logit_ref, qin_ref, kout_ref, ptop_ref, plow_ref,
                  intra_ref, t_ref, e_ref, cm_ref, s_ref):
    width = q_ref.shape[1] // heads
    rows, cols = iotas(size)
    strict, lower, diag = rows > cols, rows >= cols, rows == cols
    apart = rows ^ cols
    some = range(q_ref.shape[0] // size)
    at = [(slice(n * size, (n + 1) * size), slice(h * width, (h + 1) * width)) for n in some for h in range(heads)]
    wide = [(slice(n * width, (n + 1) * width), slice(h * width, (h + 1) * width)) for n in some for h in range(heads)]
    every = range(len(at))
    betas = [2.0 * jax.nn.sigmoid(logit_ref[n, h : h + 1, :]) for n in some for h in range(heads)]
    q, k = [q_ref[a] for a in at], [k_ref[a] for a in at]
    ws = [halves(unit_dirs(raw_ref[a])[0]) for a in at]
    gram = [jnp.where(strict, dot(w, w, NT), 0.0) for w in ws]
    beta = [jnp.where(diag, b, 0.0) for b in betas]
    beta_col = [jnp.sum(b, axis=1, keepdims=True) for b in beta]
    t = [beta[u] - jnp.where(apart == 1, beta_col[u] * gram[u] * betas[u], 0.0) for u in every]
    shift = 1
    while (1 << shift) < size:
        near = (apart >> shift) == 1
        part = [halves(jnp.where(near, g, 0.0)) for g in gram]
        ts = [halves(x) for x in t]
        once = [dot(ts[u], part[u], NN) for u in every]
        t = [t[u] - dot(halves(once[u]), ts[u], NN) for u in every]
        shift += 1
    ts = [halves(x) for x in t]
    bs = [halves(jnp.where(lower, dot((q[u],), ws[u], NT), 0.0)) for u in every]
    ms = [halves(jnp.where(strict, dot(ws[u], (k[u],), NT), 0.0)) for u in every]
    e = [dot(ts[u], ms[u], NN) for u in every]
    s = [dot(ts[u], ws[u], NN) for u in every]
    cm = [dot(bs[u], ts[u], NN) for u in every]
    es = [halves(x) for x in e]
    for u in every:
        t_ref[at[u]], e_ref[at[u]], cm_ref[at[u]], s_ref[at[u]] = t[u], e[u], cm[u], s[u]
        intra_ref[at[u]] = dot((q[u],), (k[u],), NT) - dot(bs[u], es[u], NN)
        qin_ref[at[u]] = (q[u].astype(F32) - dot(halves(cm[u]), ws[u], NN)).astype(BF16)
        kout_ref[at[u]] = (k[u].astype(F32) - dot(es[u], ws[u], TN)).astype(BF16)
        step = jnp.where(diag, 1.0, 0.0) - dot(ws[u], halves(s[u]), TN)
        ptop_ref[wide[u]], plow_ref[wide[u]] = halves(step)


def cross_forward(heads, group, scale, qin_ref, kout_ref, ptop_ref, plow_ref, intra_ref, v_ref,
                  segc_ref, segr_ref, out_ref, prob_ref, keep_ref, frame, score):
    size = qin_ref.shape[0]
    width = qin_ref.shape[1] // heads
    total = v_ref.shape[0]
    wide = group * size
    c = pl.program_id(0)
    parts = [slice(g * wide, (g + 1) * wide) for g in range(total // wide)]
    at = [slice(h * width, (h + 1) * width) for h in range(heads)]
    every = range(heads)

    @pl.when(c == 0)
    def _():
        frame[...] = jnp.zeros_like(frame)
        score[...] = jnp.full_like(score, NEG)

    rows, cols = iotas(size)
    own = pl.multiple_of(c * size, size)
    seg = segc_ref[...]
    for g, part in enumerate(parts):

        @pl.when(g * group < c)
        def _():
            raw = [mm(qin_ref[:, at[h]], frame[h, part, :], NT) for h in every]
            place = lax.broadcasted_iota(jnp.int32, (size, wide), 1) + g * wide
            permit = (place < own) & (seg == segr_ref[:, part])
            for h in every:
                score[h, :, part] = jnp.where(permit, scale * raw[h], NEG)

    permit = (rows >= cols) & (seg == segr_ref[:, pl.ds(own, size)])
    for h in every:
        score[h, :, pl.ds(own, size)] = jnp.where(permit, scale * intra_ref[:, at[h]], NEG)
    top = [jnp.max(score[h], axis=-1, keepdims=True) for h in every]
    e = [jnp.exp(score[h] - top[h]) for h in every]
    inv = [1.0 / jnp.sum(x, axis=-1, keepdims=True) for x in e]
    for h in every:
        prob_ref[0, h] = (e[h] * inv[h]).astype(BF16)
    for h in every:
        out_ref[:, at[h]] = mm(prob_ref[0, h], v_ref[:, at[h]]).astype(BF16)
        keep_ref[0, h] = frame[h]
    for g, part in enumerate(parts):

        @pl.when(g * group < c)
        def _():
            moved = [dot((frame[h, part, :],), (ptop_ref[:, at[h]], plow_ref[:, at[h]]), NT) for h in every]
            for h in every:
                frame[h, part, :] = moved[h].astype(BF16)

    for h in every:
        frame[h, pl.ds(own, size), :] = kout_ref[:, at[h]]


def cross_backward(heads, group, scale, grad_ref, v_ref, prob_ref, keep_ref, qin_ref, ptop_ref,
                   plow_ref, dqin_ref, dintra_ref, dkout_ref, dstep_ref, dv_ref, carry, dvals, ds_ref):
    size = grad_ref.shape[0]
    width = grad_ref.shape[1] // heads
    total = v_ref.shape[0]
    wide = group * size
    c = pl.num_programs(0) - 1 - pl.program_id(0)
    parts = [slice(g * wide, (g + 1) * wide) for g in range(total // wide)]
    at = [slice(h * width, (h + 1) * width) for h in range(heads)]
    every = range(heads)

    @pl.when(pl.program_id(0) == 0)
    def _():
        carry[...] = jnp.zeros_like(carry)
        dvals[...] = jnp.zeros_like(dvals)

    own = pl.multiple_of(c * size, size)
    dp = [mm(grad_ref[:, at[h]], v_ref[:, at[h]], NT) for h in every]
    pf = [prob_ref[0, h].astype(F32) for h in every]
    delta = [jnp.sum(pf[h] * dp[h], axis=-1, keepdims=True) for h in every]
    for h in every:
        ds_ref[h] = (pf[h] * (dp[h] - delta[h])).astype(BF16)
    low = [carry[h].astype(BF16) for h in every]
    dqin = [mm(ds_ref[h], keep_ref[0, h]) for h in every]
    dstep = [mm(low[h], keep_ref[0, h], TN) for h in every]
    for h in every:
        dqin_ref[:, at[h]] = scale * dqin[h]
        dstep_ref[:, at[h]] = dstep[h]
        dintra_ref[:, at[h]] = ds_ref[h, :, pl.ds(own, size)]
        dkout_ref[:, at[h]] = carry[h, pl.ds(own, size), :]
    for g, part in enumerate(parts):

        @pl.when(g * group <= c)
        def _():
            more = [mm(prob_ref[0, h, :, part], grad_ref[:, at[h]], TN) for h in every]
            for h in every:
                dvals[h, part, :] += more[h]

        @pl.when(g * group < c)
        def _():
            fresh = [mm(ds_ref[h, :, part], qin_ref[:, at[h]], TN) for h in every]
            moved = [dot((carry[h, part, :].astype(BF16),), (ptop_ref[:, at[h]], plow_ref[:, at[h]]), NN)
                     for h in every]
            for h in every:
                carry[h, part, :] = scale * fresh[h] + moved[h]

    @pl.when(c == 0)
    def _():
        for h in every:
            dv_ref[:, at[h]] = dvals[h].astype(BF16)


def local_backward(heads, size, scale, q_ref, k_ref, raw_ref, logit_ref, t_ref, e_ref, cm_ref, s_ref,
                   dqin_ref, dintra_ref, dkout_ref, dstep_ref, dv_ref, out_ref):
    width = q_ref.shape[1] // heads
    rows, cols = iotas(size)
    strict, lower, diag = rows > cols, rows >= cols, rows == cols
    some = range(q_ref.shape[0] // size)
    units = [(n, h) for n in some for h in range(heads)]
    at = [(slice(n * size, (n + 1) * size), slice(h * width, (h + 1) * width)) for n, h in units]
    wide = [(slice(n * width, (n + 1) * width), slice(h * width, (h + 1) * width)) for n, h in units]
    every = range(len(units))
    span = heads * width
    out = lambda u, part: (at[u][0], slice(part * span + units[u][1] * width, part * span + (units[u][1] + 1) * width))
    q, k = [(q_ref[a],) for a in at], [(k_ref[a],) for a in at]
    both = [unit_dirs(raw_ref[a]) for a in at]
    betas = [2.0 * jax.nn.sigmoid(logit_ref[n, h : h + 1, :]) for n, h in units]
    ws = [halves(w) for w, _ in both]
    ts, es, cms, ss = ([halves(ref[a]) for a in at] for ref in (t_ref, e_ref, cm_ref, s_ref))
    dintra = [(dintra_ref[a],) for a in at]
    dqs, dks = [halves(dqin_ref[a]) for a in at], [halves(dkout_ref[a]) for a in at]
    dps = [halves(dstep_ref[a]) for a in wide]
    b = [halves(jnp.where(lower, dot(q[u], ws[u], NT), 0.0)) for u in every]
    d_s = [halves(-dot(ws[u], dps[u], NN)) for u in every]
    d_e = [halves(-(dot(ws[u], dks[u], NT) + scale * dot(b[u], dintra[u], TN))) for u in every]
    d_cm = [halves(-dot(dqs[u], ws[u], NT)) for u in every]
    y_s = [dot(ts[u], d_s[u], TN) for u in every]
    y_e = [dot(ts[u], d_e[u], TN) for u in every]
    y_c = [dot(d_cm[u], ts[u], NT) for u in every]
    d_x = [-(dot(halves(y_s[u]), ss[u], NT) + dot(halves(y_e[u]), es[u], NT) + dot(cms[u], halves(y_c[u]), TN))
           for u in every]
    d_b = [halves(jnp.where(lower, y_c[u] - scale * dot(dintra[u], es[u], NT), 0.0)) for u in every]
    d_m = [halves(jnp.where(strict, y_e[u], 0.0)) for u in every]
    d_a = [halves(jnp.where(strict, d_x[u], 0.0)) for u in every]
    for u in every:
        a = at[u]
        out_ref[out(u, 0)] = (dqin_ref[a] + scale * dot(dintra[u], k[u], NN) + dot(d_b[u], ws[u], NN)).astype(BF16)
        out_ref[out(u, 1)] = (dkout_ref[a] + scale * dot(dintra[u], q[u], TN) + dot(d_m[u], ws[u], TN)).astype(BF16)
    d_w = [y_s[u] - dot(ss[u], dps[u], NT) - dot(es[u], dks[u], NN) - dot(cms[u], dqs[u], TN)
           + dot(d_b[u], q[u], TN) + dot(d_m[u], k[u], NN) + dot(d_a[u], ws[u], NN) + dot(d_a[u], ws[u], TN)
           for u in every]
    for u in every:
        raw, inv = raw_ref[at[u]], both[u][1]
        draw = inv * d_w[u] - raw * (inv * inv * inv) * jnp.sum(raw * d_w[u], axis=-1, keepdims=True)
        out_ref[out(u, 3)] = draw.astype(BF16)
    out_ref[:, 2 * span : 3 * span] = dv_ref[...]
    side = out_ref.shape[1] - 4 * span
    for n in some:
        lines = []
        for h in range(heads):
            u = n * heads + h
            at_diag = jnp.sum(jnp.where(diag, d_x[u], 0.0), axis=0, keepdims=True)
            lines.append(-at_diag * (1.0 - 0.5 * betas[u]) / betas[u])
        lines.append(jnp.zeros((side - heads, size), F32))
        out_ref[n * size : (n + 1) * size, 4 * span :] = jnp.transpose(jnp.concatenate(lines, axis=0)).astype(BF16)


def run(body, grid, inputs, in_specs, outputs, out_specs, scratch, flops):
    return pl.pallas_call(
        body, grid=(grid,), in_specs=in_specs, out_specs=out_specs, out_shape=outputs,
        scratch_shapes=scratch,
        compiler_params=pltpu.CompilerParams(
            dimension_semantics=("arbitrary",), vmem_limit_bytes=VMEM_BYTES),
        cost_estimate=pl.CostEstimate(
            flops=flops, transcendentals=0,
            bytes_accessed=sum(x.size * x.dtype.itemsize for x in (*inputs, *outputs))),
    )(*inputs)


def shape(dims, dtype):
    return jax.ShapeDtypeStruct(dims, dtype)


def group_of(blocks):
    return 4 if blocks % 4 == 0 else 1


def attention_local(q, k, raw, logits, size):
    tokens, width = q.shape
    blocks, heads, _ = logits.shape
    head = width // heads
    some = SOME if blocks % SOME == 0 else 1
    block = pl.BlockSpec((some * size, width), lambda c: (c, 0))
    square = pl.BlockSpec((some * head, width), lambda c: (c, 0))
    logit_block = pl.BlockSpec((some, heads, size), lambda c: (c, 0, 0))
    f, b = shape((tokens, width), F32), shape((tokens, width), BF16)
    stepped = shape((blocks * head, width), BF16)
    return run(
        functools.partial(local_forward, heads, size), blocks // some, (q, k, raw, logits),
        [block, block, block, logit_block], (b, b, stepped, stepped, f, f, f, f, f),
        [block, block, square, square, block, block, block, block, block], [],
        blocks * heads * 62 * 2 * size * size * head)


def attention_cross(q, k, v, raw, logits, segments, local, size):
    qin, kout, ptop, plow, intra, t, e, cm, s = local
    tokens, width = q.shape
    blocks, heads, _ = logits.shape
    head = width // heads
    block = pl.BlockSpec((size, width), lambda c: (c, 0))
    square = pl.BlockSpec((head, width), lambda c: (c, 0))
    b = shape((tokens, width), BF16)
    group = group_of(blocks)
    whole = pl.BlockSpec((tokens, width), lambda c: (0, 0))
    wide_prob = pl.BlockSpec((1, heads, size, tokens), lambda c: (c, 0, 0, 0))
    wide_keep = pl.BlockSpec((1, heads, tokens, head), lambda c: (c, 0, 0, 0))
    out, prob, keep = run(
        functools.partial(cross_forward, heads, group, 1.0 / math.sqrt(head)), blocks,
        (qin, kout, ptop, plow, intra, v, segments.reshape(tokens, 1), segments.reshape(1, tokens)),
        [block, block, square, square, block, whole,
         pl.BlockSpec((size, 1), lambda c: (c, 0)), pl.BlockSpec((1, tokens), lambda c: (0, 0))],
        (b, shape((blocks, heads, size, tokens), BF16), shape((blocks, heads, tokens, head), BF16)),
        [block, wide_prob, wide_keep],
        [pltpu.VMEM((heads, tokens, head), BF16), pltpu.VMEM((heads, size, tokens), F32)],
        blocks * heads * 4 * 2 * size * tokens * head)
    return out, (q, k, v, raw, logits, qin, ptop, plow, t, e, cm, s, prob, keep)


def attention_backward_cross(saved, grad, size):
    q, k, v, raw, logits, qin, ptop, plow, t, e, cm, s, prob, keep = saved
    tokens, width = q.shape
    blocks, heads, _ = logits.shape
    head = width // heads
    scale = 1.0 / math.sqrt(head)
    back = lambda c: (blocks - 1 - c, 0)
    block = pl.BlockSpec((size, width), back)
    square = pl.BlockSpec((head, width), back)
    whole = pl.BlockSpec((tokens, width), lambda c: (0, 0))
    wide_prob = pl.BlockSpec((1, heads, size, tokens), lambda c: (blocks - 1 - c, 0, 0, 0))
    wide_keep = pl.BlockSpec((1, heads, tokens, head), lambda c: (blocks - 1 - c, 0, 0, 0))
    f, b = shape((tokens, width), F32), shape((tokens, width), BF16)
    dqin, dintra, dkout, dstep, dv = run(
        functools.partial(cross_backward, heads, group_of(blocks), scale), blocks,
        (grad, v, prob, keep, qin, ptop, plow),
        [block, whole, wide_prob, wide_keep, block, square, square],
        (f, b, f, shape((blocks * head, width), F32), b),
        [block, block, block, square, whole],
        [pltpu.VMEM((heads, tokens, head), F32), pltpu.VMEM((heads, tokens, head), F32),
         pltpu.VMEM((heads, size, tokens), BF16)],
        blocks * heads * 7 * 2 * size * tokens * head)
    return dv, dqin, dintra, dkout, dstep


def attention_backward_local(saved, dv, crossed, size, side):
    q, k, v, raw, logits, qin, ptop, plow, t, e, cm, s, prob, keep = saved
    tokens, width = q.shape
    blocks, heads, _ = logits.shape
    head = width // heads
    scale = 1.0 / math.sqrt(head)
    some = SOME if blocks % SOME == 0 else 1
    block = pl.BlockSpec((some * size, width), lambda c: (c, 0))
    square = pl.BlockSpec((some * head, width), lambda c: (c, 0))
    logit_block = pl.BlockSpec((some, heads, size), lambda c: (c, 0, 0))
    return run(
        functools.partial(local_backward, heads, size, scale), blocks // some,
        (q, k, raw, logits, t, e, cm, s, *crossed, dv),
        [block, block, block, logit_block, block, block, block, block, block, block, block, square, block],
        (shape((tokens, 4 * width + side), BF16),), [pl.BlockSpec((some * size, 4 * width + side), lambda c: (c, 0))], [],
        blocks * heads * 60 * 2 * size * size * head)[0]


def ff_forward(me_ref, act_ref, grad_ref, own_ref, other_ref, mlp_ref, dact_ref, hid_ref, dgate_ref, dup_ref,
               gate_w, up_w, down_w, mlp, dact):
    tokens = act_ref.shape[0]
    cores, chips, rows = own_ref.shape[1] + other_ref.shape[1], own_ref.shape[2], own_ref.shape[4]
    tile = min(tokens, 512)

    for r in range(chips):
        for n in range(cores):
            held = own_ref.at[0, 0, r] if n == 0 else other_ref.at[0, n - 1, r]
            chip, core = me_ref[0] ^ r, me_ref[1] ^ n
            to = pl.ds(pl.multiple_of((chip * cores + core) * rows, rows), rows)
            gate_w[to, :] = held[0]
            up_w[to, :] = held[1]
            down_w[to, :] = held[2]

    @pl.when(pl.program_id(0) == 0)
    def _():
        mlp[...] = jnp.zeros_like(mlp)
        dact[...] = jnp.zeros_like(dact)

    @pl.loop(0, tokens // tile)
    def _(i):
        at = pl.ds(pl.multiple_of(i * tile, tile), tile)
        act, grad = act_ref[at, :], grad_ref[at, :]
        gate, up = mm(act, gate_w[...]), mm(act, up_w[...])
        sig = jax.nn.sigmoid(gate)
        silu = gate * sig
        hidden = (silu * up).astype(BF16)
        d_hidden = mm(grad, down_w[...])
        d_gate = (d_hidden * up * sig * (1.0 + gate * (1.0 - sig))).astype(BF16)
        d_up = (d_hidden * silu).astype(BF16)
        hid_ref[at, :] = hidden
        dgate_ref[at, :] = d_gate
        dup_ref[at, :] = d_up
        mlp[at, :] += mm(hidden, down_w[...], NT)
        dact[at, :] += mm(d_gate, gate_w[...], NT) + mm(d_up, up_w[...], NT)

    @pl.when(pl.program_id(0) == pl.num_programs(0) - 1)
    def _():
        mlp_ref[...] = mlp[...].astype(BF16)
        dact_ref[...] = dact[...].astype(BF16)


def ff_weights(me_ref, *refs):
    *ins, own_ref, other_ref = refs
    groups = [ins[5 * n : 5 * n + 5] for n in range(len(ins) // 5)]
    cores, chips, rows = own_ref.shape[1] + other_ref.shape[1], own_ref.shape[2], own_ref.shape[4]
    for d in range(chips):
        at = slice(d * cores * rows, (d + 1) * cores * rows)
        r = me_ref[0] ^ d
        gate = up = down = 0.0
        for act_ref, grad_ref, hid_ref, dgate_ref, dup_ref in groups:
            act, grad = act_ref[:, at], grad_ref[:, at]
            gate = gate + mm(act, dgate_ref[...], TN)
            up = up + mm(act, dup_ref[...], TN)
            down = down + mm(grad, hid_ref[...], TN)
        for i, part in enumerate((gate, up, down)):
            pieces = [part[w * rows : (w + 1) * rows, :].astype(BF16) for w in range(cores)]
            for n in range(cores):
                piece = pieces[0]
                for w in range(1, cores):
                    piece = jnp.where((me_ref[1] ^ n) == w, pieces[w], piece)
                if n == 0:
                    own_ref[0, 0, r, i] = piece
                else:
                    other_ref[0, n - 1, r, i] = piece


def place_self():
    return jnp.stack([lax.axis_index("dp"), lax.axis_index("wid")]).astype(jnp.int32)


SCALARS = pl.BlockSpec(memory_space=pltpu.SMEM)


def feed_forward(act, grad, own, other):
    tokens, width = act.shape
    groups, part = own.shape[0], own.shape[5]
    whole = pl.BlockSpec((tokens, width), lambda h: (0, 0))
    units = pl.BlockSpec((tokens, part), lambda h: (0, h))
    held = [pl.BlockSpec((1,) + x.shape[1:], lambda h: (h, 0, 0, 0, 0, 0)) for x in (own, other)]
    full, some = shape((tokens, width), BF16), shape((tokens, groups * part), BF16)
    flops = 6 * 2 * tokens * width * groups * part
    return run(ff_forward, groups, (place_self(), act, grad, own, other), [SCALARS, whole, whole, *held],
               (full, full, some, some, some), [whole, whole, units, units, units],
               [pltpu.VMEM((width, part), BF16)] * 3 + [pltpu.VMEM((tokens, width), F32)] * 2, flops)


def feed_forward_weights(acts, grads, saved, own, other):
    width = acts[0].shape[1]
    groups, part = own.shape[0], own.shape[5]
    values, specs = [], []
    for act, grad, some in zip(acts, grads, saved):
        values += [act, grad, *some]
        specs += [pl.BlockSpec(act.shape, lambda h: (0, 0))] * 2
        specs += [pl.BlockSpec((act.shape[0], part), lambda h: (0, h))] * 3
    held = [pl.BlockSpec((1,) + x.shape[1:], lambda h: (h, 0, 0, 0, 0, 0)) for x in (own, other)]
    return run(ff_weights, groups, (place_self(), *values), [SCALARS, *specs],
               (shape(own.shape, BF16), shape(other.shape, BF16)), held, [],
               3 * 2 * sum(x.shape[0] for x in acts) * width * groups * part)


def split_rows(me_ref, part, at, own_ref, other_ref):
    cores, shards, rows = own_ref.shape[0] + other_ref.shape[0], own_ref.shape[2], own_ref.shape[3]
    for h in range(shards):
        pieces = [part[(h * cores + w) * rows : (h * cores + w + 1) * rows, :] for w in range(cores)]
        for n in range(cores):
            piece = pieces[0]
            for w in range(1, cores):
                piece = jnp.where((me_ref[1] ^ n) == w, pieces[w], piece)
            if n == 0:
                own_ref[0, 0, h, :, at] = piece
            else:
                other_ref[n - 1, 0, h, :, at] = piece


def row_grads(me_ref, left_ref, right_ref, own_ref, other_ref):
    columns = right_ref.shape[1]
    for start in range(0, columns, 512):
        at = slice(start, min(start + 512, columns))
        split_rows(me_ref, mm(left_ref[...], right_ref[:, at], TN).astype(BF16), at, own_ref, other_ref)


def split_whole(full, chips, shards, cores, rows):
    full = full.astype(BF16).reshape(chips, shards, cores, rows, full.shape[1])
    full = jnp.take(full, lax.axis_index("wid") ^ jnp.arange(cores), axis=2).transpose(2, 0, 1, 3, 4)
    return full[:1], full[1:]


def row_gradients(left, right, chips, shards, cores):
    tokens, width = left.shape
    columns = right.shape[1]
    rows = width // (chips * shards * cores)
    if rows % 16:
        return split_whole(mm(left, right, TN), chips, shards, cores, rows)
    outs = [shape((n, chips, shards, rows, columns), BF16) for n in (1, cores - 1)]
    specs = [pl.BlockSpec((x.shape[0], 1, shards, rows, columns), lambda d: (0, d, 0, 0, 0)) for x in outs]
    return run(row_grads, chips, (place_self(), left, right),
               [SCALARS, pl.BlockSpec((tokens, width // chips), lambda d: (0, d)),
                pl.BlockSpec((tokens, columns), lambda d: (0, 0))],
               tuple(outs), specs, [], 2 * tokens * width * columns)


def input_grads(me_ref, bias_ref, left_ref, right_ref, w_ref, two_ref, din_ref, own_ref, other_ref):
    columns, side = right_ref.shape[1], 128
    heads, rows = bias_ref.shape[0], own_ref.shape[3]
    din_ref[...] = mm(right_ref[...], w_ref[...], NT).astype(BF16)
    spans = [(start, min(start + 512, columns - side)) for start in range(0, columns - side, 512)]
    gain_sum = jnp.zeros((left_ref.shape[1], 1), F32)
    for start, stop in spans + [(columns - side, columns)]:
        part = mm(left_ref[...], right_ref[:, start:stop], TN)
        weight = w_ref[:, start:stop].astype(F32)
        lane = lax.broadcasted_iota(jnp.int32, part.shape, 1)
        if stop == columns:
            gain_sum = gain_sum + jnp.sum(jnp.where(lane < heads, part * weight, 0.0), axis=1, keepdims=True)
            gain = jnp.sum(jnp.where(lane == heads, weight, 0.0), axis=1, keepdims=True)
            row = lax.rem(lax.broadcasted_iota(jnp.int32, part.shape, 0), rows)
            two = jnp.transpose(jnp.broadcast_to(two_ref[...], (side, part.shape[0])))
            part = jnp.where(lane < heads, part, 0.0) + jnp.where(lane == heads, gain_sum / gain, 0.0)
            for n in range(heads):
                part = part + jnp.where((lane == heads + 2) & (row == n), bias_ref[n], 0.0)
            part = jnp.where(me_ref[2] == 1, part, 0.0) + jnp.where(lane == heads + 1, two, 0.0)
        else:
            gain_sum = gain_sum + jnp.sum(part * weight, axis=1, keepdims=True)
            part = jnp.where(me_ref[2] == 1, part, 0.0)
        split_rows(me_ref, part.astype(BF16), slice(start, stop), own_ref, other_ref)


def input_gradients(left, right, weights, two, bias, once, chips, shards, cores):
    tokens, width = left.shape
    columns, heads = right.shape[1], bias.shape[0]
    rows = width // (chips * shards * cores)
    if rows % 16:
        full = mm(left, right, TN)
        lane = lax.broadcasted_iota(jnp.int32, (width, columns), 1) - (columns - 128)
        row = lax.broadcasted_iota(jnp.int32, (width, columns), 0) % rows
        wide = weights.astype(F32)
        gain = jnp.sum(jnp.where(lane < heads, full * wide, 0.0), axis=1, keepdims=True)
        gain = gain / wide[:, columns - 128 + heads][:, None]
        full = full + jnp.where(lane == heads, gain, 0.0)
        for n in range(heads):
            full = full + jnp.where((lane == heads + 2) & (row == n), bias[n], 0.0)
        full = jnp.where(once, full, 0.0) + jnp.where(lane == heads + 1, two.T, 0.0)
        return (mm(right, weights, NT).astype(BF16), *split_whole(full, chips, shards, cores, rows))
    outs = [shape((n, chips, shards, rows, columns), BF16) for n in (1, cores - 1)]
    specs = [pl.BlockSpec((x.shape[0], 1, shards, rows, columns), lambda d: (0, d, 0, 0, 0)) for x in outs]
    features = pl.BlockSpec((tokens, width // chips), lambda d: (0, d))
    me = jnp.concatenate([place_self(), once[None].astype(jnp.int32)])
    return run(input_grads, chips, (me, bias, left, right, weights, two),
               [SCALARS, SCALARS, features, pl.BlockSpec((tokens, columns), lambda d: (0, 0)),
                pl.BlockSpec((width // chips, columns), lambda d: (d, 0)), pl.BlockSpec((1, width // chips), lambda d: (0, d))],
               (shape((tokens, width), BF16), *outs), [features, *specs], [], 4 * tokens * width * columns)


def lay_columns(me_ref, *refs):
    *got, a_ref, b_ref, c_ref, d_ref, tail_ref = refs
    count, span = len(got), a_ref.shape[1] // len(got)
    for k, ref in enumerate(got):
        source = lax.rem(me_ref[0] - k + count, count)
        to = pl.ds(pl.multiple_of(source * span, 128), span)
        for i, out in enumerate((a_ref, b_ref, c_ref, d_ref)):
            out[:, to] = ref[:, i * span : (i + 1) * span].astype(F32)
        tail_ref[source] = ref[:, 4 * span :].astype(F32)


def laid_columns(got, side):
    count, (rows, columns) = len(got), got[0].shape
    span = (columns - side) // 4
    if rows % 16 or span % 128:
        got = by_source(got, "hid")
        whole = [jnp.concatenate([x[:, i * span : (i + 1) * span] for x in got], axis=1).astype(F32) for i in range(4)]
        return (*whole, jnp.stack([x[:, 4 * span :] for x in got]).astype(F32))
    one = pl.BlockSpec((rows, columns), lambda i: (0, 0))
    out = pl.BlockSpec((rows, count * span), lambda i: (0, 0))
    return run(lay_columns, 1, (lax.axis_index("hid")[None].astype(jnp.int32), *got), [SCALARS] + [one] * count,
               (shape((rows, count * span), F32),) * 4 + (shape((count, rows, side), F32),),
               [out] * 4 + [pl.BlockSpec((count, rows, side), lambda i: (0, 0, 0))], [], 0)


def lay_ff(me_ref, *refs):
    *got, gate_ref, up_ref, down_ref = refs
    part = got[0].shape[2]
    for r, ref in enumerate(got):
        to = pl.ds(pl.multiple_of((me_ref[0] ^ r) * part, 128), part)
        gate_ref[:, to] = ref[0].astype(F32)
        up_ref[:, to] = ref[1].astype(F32)
        down_ref[to, :] = jnp.transpose(ref[2].astype(F32))


def laid_ff(got):
    count, (_, rows, part) = len(got), got[0].shape
    outs = ((rows, count * part), (rows, count * part), (count * part, rows))
    return run(lay_ff, 1, (lax.axis_index("dp")[None].astype(jnp.int32), *got),
               [SCALARS] + [pl.BlockSpec((3, rows, part), lambda i: (0, 0, 0))] * count,
               tuple(shape(x, F32) for x in outs), [pl.BlockSpec(x, lambda i: (0, 0)) for x in outs], [], 0)


def lay_rows(me_ref, own_ref, other_ref, out_ref, *turned):
    cores, shards, rows = own_ref.shape[0] + other_ref.shape[0], own_ref.shape[2], own_ref.shape[3]
    for k in range(shards):
        h = lax.rem(me_ref[2] - k + shards, shards)
        for n in range(cores):
            to = pl.ds(pl.multiple_of((h * cores + (me_ref[1] ^ n)) * rows, rows), rows)
            out_ref[to, :] = own_ref[0, 0, k] if n == 0 else other_ref[n - 1, 0, k]
    for ref in turned:
        ref[...] = jnp.transpose(out_ref[:, -ref.shape[0] :].astype(F32))


def gathered_rows(own, other, side):
    _, chips, shards, rows, columns = own.shape
    cores = 1 + other.shape[0]
    if rows % 16:
        full = jnp.concatenate([own, other], axis=0)
        full = jnp.take(full, lax.axis_index("wid") ^ jnp.arange(cores), axis=0)
        full = jnp.take(full, (lax.axis_index("hid") - jnp.arange(shards)) % shards, axis=2)
        full = full.transpose(1, 2, 0, 3, 4).reshape(-1, columns)
        return full, (full[:, columns - side :].astype(F32).T if side else None)
    me = jnp.concatenate([place_self(), lax.axis_index("hid")[None].astype(jnp.int32)])
    specs = [pl.BlockSpec((x.shape[0], 1, shards, rows, columns), lambda d: (0, d, 0, 0, 0)) for x in (own, other)]
    size = cores * shards * rows
    outs, out_specs = [shape((chips * size, columns), BF16)], [pl.BlockSpec((size, columns), lambda d: (d, 0))]
    if side:
        outs.append(shape((side, chips * size), F32))
        out_specs.append(pl.BlockSpec((side, size), lambda d: (0, d)))
    out = run(lay_rows, chips, (me, own, other), [SCALARS, *specs], tuple(outs), out_specs, [], 0)
    return out[0], (out[1] if side else None)


def project(heads, tok, bias_ref, x_ref, w_ref, gain_ref, act_ref, q_ref, k_ref, v_ref, raw_ref, logit_ref):
    x = x_ref[...].astype(F32)
    unit = x * lax.rsqrt(jnp.mean(x * x, axis=-1, keepdims=True) + EPS)
    act_ref[...] = (unit * gain_ref[...]).astype(BF16)
    act, span = act_ref[...], q_ref.shape[1]
    for i, out in enumerate((q_ref, k_ref, v_ref, raw_ref)):
        out[...] = mm(act, w_ref[:, i * span : (i + 1) * span]).astype(out.dtype)
    beside = mm(act, w_ref[:, 4 * span :])
    for n in range(beside.shape[0] // tok):
        rows = jnp.transpose(beside[n * tok : (n + 1) * tok, :])
        for h in range(heads):
            logit_ref[n, h : h + 1, :] = rows[h : h + 1, :] + bias_ref[h]


def projected(x, weights, gain, bias, heads, tok):
    tokens, width = x.shape
    span = (weights.shape[1] - 128) // 4
    blocks = tokens // tok
    some = 2 if blocks % 2 == 0 else 1
    wide, narrow = (pl.BlockSpec((some * tok, n), lambda c: (c, 0)) for n in (width, span))
    whole = lambda c: (0, 0)
    return run(
        functools.partial(project, heads, tok), blocks // some, (bias, x, weights, gain),
        [SCALARS, wide, pl.BlockSpec(weights.shape, whole), pl.BlockSpec((1, width), whole)],
        (shape((tokens, width), BF16), shape((tokens, span), BF16),
         shape((tokens, span), BF16), shape((tokens, span), BF16), shape((tokens, span), F32),
         shape((blocks, heads, tok), F32)),
        [wide, narrow, narrow, narrow, narrow, pl.BlockSpec((some, heads, tok), lambda c: (c, 0, 0))], [],
        2 * tokens * width * weights.shape[1])


def norm_in(tensor, gain_vec):
    return tensor * lax.rsqrt(jnp.mean(tensor * tensor, axis=-1, keepdims=True) + EPS) * gain_vec


def pick(x, index, axis=0):
    return lax.dynamic_index_in_dim(x, index, axis, keepdims=False)


def place(buffer, piece, index, axis=0):
    return lax.dynamic_update_index_in_dim(buffer, piece, index, axis)


def add(left, *others):
    total = left.astype(F32)
    for other in others:
        total = total + other.astype(F32)
    return total.astype(left.dtype)


def to_row(x):
    cores, rows = lax.axis_size("wid"), x.shape[0]
    me = lax.axis_index("wid")
    if cores == rows == 2:
        got = lax.ppermute(pick(x, 1 - me), "wid", [(0, 1), (1, 0)])
        mine = pick(x, me)
        return jnp.concatenate([jnp.where(me == 0, mine, got), jnp.where(me == 0, got, mine)], axis=0)
    every = pick(lax.all_gather(x, "wid", axis=0, tiled=False), me // (cores // rows), 1)
    return every.reshape((-1,) + x.shape[2:])


def from_row(x, rows):
    cores = lax.axis_size("wid")
    me = lax.axis_index("wid")
    parts = x.reshape((cores, x.shape[0] // cores) + x.shape[1:])
    if cores == rows == 2:
        got = lax.ppermute(pick(parts, 1 - me), "wid", [(0, 1), (1, 0)])
        mine = pick(parts, me)
        return jnp.stack([jnp.where(me == 0, mine, got), jnp.where(me == 0, got, mine)], axis=0)
    return lax.all_to_all(parts, "wid", 0, 0, tiled=True)[:: cores // rows]


def choose(parts, index):
    return lax.select_n(index.astype(jnp.int32), *parts)


def exchange(blocks, axis):
    count, me = lax.axis_size(axis), lax.axis_index(axis)
    got = [choose(blocks, me)]
    for k in range(1, count):
        sent = choose(blocks, lax.rem(me + k, count))
        got.append(lax.ppermute(sent, axis, [(i, (i + k) % count) for i in range(count)]))
    return got


def exchange_rows(x, axis):
    count, me = lax.axis_size(axis), lax.axis_index(axis)
    sent = together(*[pick(x, lax.rem(me + k, count)) for k in range(1, count)])
    return [pick(x, me)] + [lax.ppermute(sent[k - 1], axis, [(i, (i + k) % count) for i in range(count)])
                            for k in range(1, count)]


def by_source(got, axis):
    count, me = lax.axis_size(axis), lax.axis_index(axis)
    return [choose(got, lax.rem(me - j + count, count)) for j in range(count)]


def pairs(count, flip):
    return [(i, i ^ flip) for i in range(count)]


def gather_near(x, axis):
    if lax.axis_size(axis) != 4:
        return (x,)
    return x, lax.ppermute(x, axis, pairs(4, 1)), lax.ppermute(x, axis, pairs(4, 2))


def gather_far(near, axis):
    if len(near) == 1:
        return near
    x, one, two = near
    half = x.shape[0] // 2
    return x, one, two, lax.ppermute(one[:half], axis, pairs(4, 2)), lax.ppermute(two[half:], axis, pairs(4, 1))


def gather_end(far, axis):
    if len(far) == 1:
        return lax.all_gather(far[0], axis, axis=0, tiled=False)
    x, one, two, top, low = far
    me = lax.axis_index(axis)
    out = jnp.zeros((4,) + x.shape, x.dtype)
    out = place(place(place(out, x, me), one, me ^ 1), two, me ^ 2)
    return place(out, jnp.concatenate([top, low], axis=0), me ^ 3)


def square_gather(x, axis):
    return gather_end(gather_far(gather_near(x, axis), axis), axis)


def by_distance(far):
    x, one, two, top, low = far
    return x, jnp.concatenate([one, two], axis=0), jnp.concatenate([top, low], axis=0)


def sum_far(far, axis):
    half = far.shape[0] // 2
    return lax.ppermute(far[:half], axis, pairs(4, 2)), lax.ppermute(far[half:], axis, pairs(4, 1))


def sum_near(one, two, came, axis):
    half = one.shape[0] // 2
    one = jnp.concatenate([add(one[:half], came[0]), one[half:]], axis=0)
    two = jnp.concatenate([two[:half], add(two[half:], came[1])], axis=0)
    one, two = together(one, two)
    return lax.ppermute(one, axis, pairs(4, 1)), lax.ppermute(two, axis, pairs(4, 2))


def from_cores(x):
    cores = lax.axis_size("wid")
    return jnp.stack([lax.ppermute(x, "wid", pairs(cores, n)) for n in range(1, cores)], axis=0)


def core_sum(own, other):
    cores = lax.axis_size("wid")
    return add(own, *[lax.ppermute(other[n - 1 : n], "wid", pairs(cores, n)) for n in range(1, cores)])


def together(*values):
    return lax.optimization_barrier(values)


def per_device(layer_in, segment_ids, out_grad, gain_attn, w_query, w_key, w_value, w_dir, w_beta,
               b_beta, w_out, gain_mlp, w_gate, w_up, w_down):
    n_dp, n_hid, n_wid = (lax.axis_size(axis) for axis in ("dp", "hid", "wid"))
    row_count, tok, width = layer_in.shape
    heads = b_beta.shape[0]
    own_heads = heads // n_hid
    span = width // n_hid
    shard = w_query.shape[0]
    held = n_wid * tok
    copies = n_wid // row_count
    my_hid, my_dp = lax.axis_index("hid"), lax.axis_index("dp")
    side = 128
    columns = 4 * span + side

    row_own = to_row(layer_in)
    row_own, w_query, w_key, w_value, w_dir, w_beta, w_out, w_gate, w_up, w_down, out_grad = together(
        row_own, w_query, w_key, w_value, w_dir, w_beta, w_out, w_gate, w_up, w_down, out_grad)
    row_in = lax.all_gather(row_own, "hid", axis=0, tiled=True)

    down_t = w_down.T
    ff_rows, ff_cols = down_t.shape
    part = ff_cols // n_dp

    spare = side // 2
    ride = n_wid == row_count == 2 and own_heads + 2 <= spare and shard * spare >= held
    seg_rows = to_row(segment_ids).astype(BF16) if ride else jnp.zeros((held,), BF16)
    seg_rows = jnp.pad(seg_rows[: shard * spare], (0, max(0, shard * spare - held))).reshape(shard, spare)
    blank = jnp.zeros((shard, spare - own_heads - 2), BF16)
    blocks = []
    for j in range(n_hid):
        at = slice(j * span, (j + 1) * span)
        blocks.append(jnp.concatenate(
            [w_query[:, at], w_key[:, at], w_value[:, at], w_dir[:, at], w_beta[:, j * own_heads : (j + 1) * own_heads],
             gain_attn[:, None], gain_mlp[:, None], blank, seg_rows], axis=1))
    cat = exchange(blocks, "hid")
    segs = [x[:, columns - spare :].reshape(-1)[:held].astype(jnp.int32) for x in cat]
    grad_b = out_grad.reshape(row_count * tok, width)
    cat, grads = together(cat, gather_near(grad_b, "dp"))
    cat = gather_near(jnp.stack(cat, axis=0), "dp")
    wout = exchange([w_out] * n_hid, "hid")
    cut = [jnp.stack([x[:, j * part : (j + 1) * part] for x in (w_gate, w_up, down_t)]) for j in range(n_dp)]
    cat, cut = together(cat, cut)
    cat = gather_end(gather_far(cat, "dp"), "dp")
    grads = by_distance(gather_far(grads, "dp"))
    ff = [choose(cut, my_dp)]
    for r in range(1, n_dp):
        ff.append(lax.ppermute(choose(cut, my_dp ^ r), "dp", pairs(n_dp, r)))
    cat, gains = gathered_rows(cat[None], from_cores(cat), side)
    bias_own = lax.dynamic_slice_in_dim(b_beta, my_hid * own_heads, own_heads, 0).astype(F32)

    row_in, cat, ff, wout, grads, segs = together(row_in, cat, ff, wout, grads, segs)
    wout = gather_near(jnp.stack(wout, axis=0), "dp")
    ff = lax.all_gather(jnp.stack(ff, axis=0), "hid", axis=0, tiled=False)
    gain_one, gain_two = gains[own_heads], gains[own_heads + 1]
    if ride:
        segs = jnp.concatenate(by_source(segs, "hid"), axis=0)
    else:
        segs = lax.all_gather(segment_ids, ("hid", "wid"), axis=0, tiled=False)
        segs = pick(segs, lax.axis_index("wid") // copies, 1).reshape(-1)
    act_one, query, key, value, raw, logits = projected(row_in, cat, gain_one[None], bias_own, own_heads, tok)
    raw, wout = together(raw, wout)
    wout = gather_far(wout, "dp")
    local = attention_local(query, key, raw, logits, tok)
    att, saved = attention_cross(query, key, value, raw, logits, segs, local, tok)
    att, wout = together(att, wout)
    att = exchange([att[j * held : (j + 1) * held] for j in range(n_hid)], "hid")
    wout = gather_end(wout, "dp")
    wout_full, _ = gathered_rows(wout[None], from_cores(wout), 0)
    att, wout_full = together(att, wout_full)
    att = from_row(jnp.concatenate(by_source(att, "hid"), axis=1), row_count)
    att = att.reshape(row_count * tok, width)

    layer_f = layer_in.astype(F32).reshape(row_count * tok, width)
    middle = layer_f + mm(att, wout_full)
    act_two = norm_in(middle, gain_two).astype(BF16)
    act_two, ff = together(act_two, ff)
    ff_own, ff_other = ff[:, None], jnp.moveaxis(from_cores(ff), 0, 1)
    near = gather_near(act_two, "dp")
    own = feed_forward(act_two, grads[0], ff_own, ff_other)
    own, near = together(own, near)
    far = gather_far(near, "dp")
    acts = by_distance(far)
    mid = feed_forward(acts[1], grads[1], ff_own, ff_other)
    mid, end = together(mid, acts[2])
    end = feed_forward(end, grads[2], ff_own, ff_other)
    tokens = row_count * tok
    came = sum_far(end[1], "dp")
    near = sum_near(mid[1][:tokens], mid[1][tokens:], came, "dp")
    own, mid, end, near_sent = together(own, mid, end, came)
    g_own, g_other = feed_forward_weights(
        (act_two, *acts[1:]), grads, [(x[2], x[3], x[4]) for x in (own, mid, end)], ff_own, ff_other)
    near, g_own, g_other = together(near, g_own, g_other)
    d_act = add(own[1], *near)

    _, pull_two = jax.vjp(norm_in, middle, gain_two)
    d_mid_norm, _ = pull_two(d_act.astype(F32))
    d_middle = grad_b.astype(F32) + d_mid_norm
    d_branch = d_middle.astype(BF16)
    d_att = mm(d_branch, wout_full, NT).astype(BF16).reshape(row_count, tok, width)
    d_att = to_row(d_att)
    d_att, att = together(d_att, att)
    d_att = exchange([d_att[:, j * span : (j + 1) * span] for j in range(n_hid)], "hid")
    ff_grads = core_sum(jnp.moveaxis(g_own, 1, 0), jnp.moveaxis(g_other, 1, 0))[0]
    wout_rows = row_gradients(att, d_branch, n_dp, n_hid, n_wid)
    d_att, wout_rows, ff_grads = together(d_att, wout_rows, ff_grads)
    ff_grads = lax.psum_scatter(ff_grads, "hid", scatter_dimension=0, tiled=False)
    d_att = jnp.concatenate(by_source(d_att, "hid"), axis=0)
    my = lambda x, r: pick(x, my_dp ^ r)
    wout_sum = core_sum(*wout_rows)[0]
    wout_came = sum_far(my(wout_sum, 3), "dp")

    crossed = attention_backward_cross(saved, d_att, tok)
    crossed, wout_came, mlp_far = together(crossed, wout_came, end[0])
    wout_grad = sum_near(my(wout_sum, 1), my(wout_sum, 2), wout_came, "dp")
    mlp_came = sum_far(mlp_far, "dp")
    dv, *crossed = crossed
    d_cat = attention_backward_local(saved, dv, crossed, tok, side)
    d_gain_two = jnp.sum(d_act.astype(F32) * norm_in(middle, 1.0), axis=0, keepdims=True)
    bias_grad = jnp.sum(d_cat[:, 4 * span : 4 * span + own_heads].astype(F32), axis=0)
    once = lax.axis_index("wid") % copies == 0
    d_act_one, *cat_grad = input_gradients(act_one, d_cat, cat, d_gain_two, bias_grad, once, n_dp, n_hid, n_wid)
    d_act_one, cat_grad, wout_grad, mlp_came = together(d_act_one, cat_grad, wout_grad, mlp_came)
    d_parts = d_act_one.reshape(n_hid, held, width)
    first_half = exchange_rows(d_parts[:, : held // 2], "hid")
    last_half = exchange_rows(d_parts[:, held // 2 :], "hid")
    wout_grad = add(my(wout_sum, 0), *wout_grad)
    grad_wout = lax.psum_scatter(wout_grad, "hid", scatter_dimension=0, tiled=False).astype(F32)
    cat_sum = core_sum(*cat_grad)[0]
    cat_came = sum_far(my(cat_sum, 3), "dp")
    ff_got = [ff_grads[0]]
    for r in range(1, n_dp):
        ff_got.append(lax.ppermute(ff_grads[r], "dp", pairs(n_dp, r)))
    cat_came, ff_got, first_half = together(cat_came, ff_got, first_half)
    cat_grad = sum_near(my(cat_sum, 1), my(cat_sum, 2), cat_came, "dp")
    cat_grad, last_half = together(cat_grad, last_half)
    cat_grad = add(my(cat_sum, 0), *cat_grad)
    mlp = sum_near(mid[0][:tokens], mid[0][tokens:], mlp_came, "dp")
    cat_got = exchange([cat_grad[j] for j in range(n_hid)], "hid")
    d_sum = jnp.concatenate([add(*first_half), add(*last_half)], axis=0)
    d_sum = from_row(d_sum, row_count).reshape(row_count * tok, width).astype(F32)
    grad_gate, grad_up, grad_down = laid_ff(ff_got)
    layer_out = (middle + add(own[0], *mlp).astype(F32)).astype(BF16)
    _, pull_one = jax.vjp(lambda t: norm_in(t, gain_one), layer_f)
    grad_in = (d_middle + pull_one(d_sum)[0]).astype(BF16)
    cat_got, grad_in, layer_out = together(cat_got, grad_in, layer_out)
    *weight_grads, tails = laid_columns(cat_got, side)
    grad_beta = tails[:, :, :own_heads].transpose(1, 0, 2).reshape(shard, heads)
    gain_grads = jnp.sum(tails[:, :, own_heads : own_heads + 2], axis=0)
    grad_bias = tails[:, :own_heads, own_heads + 2].reshape(heads)

    return (
        layer_out.reshape(layer_in.shape), grad_in.reshape(layer_in.shape), gain_grads[:, 0],
        *weight_grads, grad_beta, grad_bias,
        grad_wout, gain_grads[:, 1], grad_gate, grad_up, grad_down,
    )


def solution(mesh):
    in_specs = (
        P("dp", ("hid", "wid"), None),
        P("dp", ("hid", "wid")),
        P("dp", ("hid", "wid"), None),
        P(("dp", "hid", "wid")),
        P(("dp", "hid", "wid"), None),
        P(("dp", "hid", "wid"), None),
        P(("dp", "hid", "wid"), None),
        P(("dp", "hid", "wid"), None),
        P(("dp", "hid", "wid"), None),
        P(),
        P(("dp", "hid", "wid"), None),
        P(("dp", "hid", "wid")),
        P(("dp", "wid"), "hid"),
        P(("dp", "wid"), "hid"),
        P("hid", ("dp", "wid")),
    )
    out_specs = (
        P("dp", ("hid", "wid"), None),
        P("dp", ("hid", "wid"), None),
        P(("dp", "hid", "wid")),
        P(("dp", "hid", "wid"), None),
        P(("dp", "hid", "wid"), None),
        P(("dp", "hid", "wid"), None),
        P(("dp", "hid", "wid"), None),
        P(("dp", "hid", "wid"), None),
        P(),
        P(("dp", "hid", "wid"), None),
        P(("dp", "hid", "wid")),
        P(("dp", "wid"), "hid"),
        P(("dp", "wid"), "hid"),
        P("hid", ("dp", "wid")),
    )
    return jax.shard_map(
        per_device, mesh=mesh, in_specs=in_specs, out_specs=out_specs, check_vma=False
    )
```
